32 devices in a mesh: gx: 8 (over z, x), gy: 2 (over core), gz: 2 (over y).
Axes of the slice: x: 2, y: 2, z: 4, core: 2. Of those that a mesh axis runs over, the one named last changes fastest.
Arguments:
- flow_field: bfloat16 [256, 128, 1024], P('gx', 'gy', 'gz'), may hold values from -96 to 96
- left_x: bfloat16 [256, 128], P('gx'), may hold values from -0.046875 to 0.046875
- last_x: bfloat16 [256, 128], P('gx'), may hold values from -0.375 to 0.375
- last_y: bfloat16 [128, 128], P('gy'), may hold values from -0.0078125 to 0.0078125
- right_y: bfloat16 [128, 256], P('gy'), may hold values from -0.5 to 0.5
- right_m: bfloat16 [1024, 256], P('gz'), may hold values from -0.1875 to 0.1875
- last_m: bfloat16 [1024, 256], P('gz'), may hold values from -0.1875 to 0.1875
Outputs:
- core_first: float32 [256, 128], P('gx')
- core_middle: float32 [128, 128, 128], P(('gx', 'gz'), 'gy')
- core_last: float32 [128, 1024], P(None, 'gz')
The draws below stay inside these ranges and needn't reach their ends.
All inputs are finite; a program needn't handle non-finite values.
Results may differ from the reference program's by a relative error of at most 0.0053.
Values sent between devices are 32-bit elements; how exact they have to be, the bound alone decides.
No kernel may reach another device: no remote copies, remote signals or barrier semaphores. Data moves between devices by JAX's collectives and lax.ppermute only.
A program may use at most 64 MiB of HBM per device.

```python
import jax
import jax.numpy as jnp
from jax import lax

R = 128
L = 256
NX = 256
NY = 128
M = 1024


def shard_levels(own_key, shape, cuts, smallest, high):
    factor_of = 1.0
    for axis_at, parts in cuts:
        draws = jax.random.uniform(jax.random.fold_in(jax.random.fold_in(own_key, 6), axis_at), (parts,), jnp.float32, smallest / len(cuts), high / len(cuts))
        factor_of = factor_of * jnp.repeat(jnp.exp(draws), shape[axis_at] // parts).reshape((-1,) + (1,) * (len(shape) - 1 - axis_at))
    return factor_of


def centred(key, extent, width, bound, cuts=(), held_as=jnp.bfloat16):
    factor_of = shard_levels(key, extent, cuts, -0.22, 0.18) if cuts else 1.0
    array = jax.random.normal(key, extent, jnp.float32) * width * factor_of
    return jnp.minimum(jnp.maximum(array, -bound), bound).astype(held_as)


def setup_inputs(seed: int = 0) -> dict:
    arg_keys = jax.random.split(jax.random.key(seed), 8)
    flow_field = centred(arg_keys[0], (NX, NY, M), 16.0, 96.0, ((0, 8), (1, 2), (2, 2)))
    left_x = centred(arg_keys[1], (NX, R), (NX * NX // 4) ** -0.5, 0.046875, ((0, 8),))
    last_x = centred(arg_keys[2], (NX, R), NX ** -0.5, 0.375, ((0, 8),))
    last_y = centred(arg_keys[3], (NY, R), (NY * 4096) ** -0.5, 0.0078125, ((0, 2),))
    right_y = centred(arg_keys[4], (NY, L), NY ** -0.5, 0.5, ((0, 2),))
    right_m = centred(arg_keys[5], (M, L), M ** -0.5, 0.1875, ((0, 2),))
    last_m = centred(arg_keys[6], (M, L), M ** -0.5, 0.1875, ((0, 2),))
    return {"flow_field": flow_field, "left_x": left_x, "last_x": last_x, "last_y": last_y, "right_y": right_y, "right_m": right_m, "last_m": last_m}


def reference(flow_field, left_x, last_x, last_y, right_y, right_m, last_m):
    highest = lax.Precision.HIGHEST
    blocks = 8
    x_size = NX // blocks
    field_blocks = flow_field.reshape(blocks, x_size, NY, M)
    left_blocks = left_x.reshape(blocks, x_size, R)
    last_blocks = last_x.reshape(blocks, x_size, R)
    y_factor = right_y.astype(jnp.float32)
    y_left = last_y.astype(jnp.float32)

    def block_step(totals, pieces):
        x_block, left_piece, last_piece = pieces
        flat_field = x_block.reshape(x_size * NY, M)
        first_terms = jnp.dot(flat_field.astype(jnp.float32), right_m.astype(jnp.float32), preferred_element_type=jnp.float32).reshape(x_size, NY, L)
        first_rows = jnp.sum(first_terms * y_factor[None], axis=1)
        last_terms = jnp.dot(flat_field.astype(jnp.float32), last_m.astype(jnp.float32), preferred_element_type=jnp.float32).reshape(x_size, NY * L)
        middle_part = jnp.dot(left_piece.astype(jnp.float32).T, last_terms, precision=highest)
        khatri = (last_piece.astype(jnp.float32)[:, None, :] * y_left[None]).astype(jnp.bfloat16)
        khatri = khatri.reshape(x_size * NY, R)
        last_part = jnp.dot(khatri.T.astype(jnp.float32), flat_field.astype(jnp.float32), preferred_element_type=jnp.float32)
        return ((totals[0] + middle_part, totals[1] + last_part), first_rows)
    start = (jnp.zeros((R, NY * L), jnp.float32), jnp.zeros((R, M), jnp.float32))
    (middle_sum, core_last), first_rows = lax.scan(block_step, start, (field_blocks, left_blocks, last_blocks))
    first_rows = first_rows.reshape(NX, L)
    first_gram = jnp.dot(left_x.astype(jnp.float32).T, first_rows, precision=highest)
    gram_first = jnp.dot(first_gram, first_gram.T, precision=highest)
    core_first = jnp.linalg.solve(gram_first, jnp.dot(first_gram, first_rows.T, precision=highest)).T
    last_gram = jnp.dot(core_last, last_m.astype(jnp.float32), precision=highest)
    gram_last = jnp.dot(last_gram, last_gram.T, precision=highest)
    pinv_last = jnp.linalg.solve(gram_last, last_gram).T
    core_middle = jnp.dot(middle_sum.reshape(R * NY, L), pinv_last, precision=highest).reshape(R, NY, R)
    return (core_first, core_middle, core_last)
```

```python
import jax
import jax.numpy as jnp
from jax import lax
from jax.sharding import PartitionSpec as P

ALL = ("gx", "gy", "gz")


def spread(array, axes):
    count = lax.axis_size(axes)
    copies = jnp.broadcast_to(array[None], (count, *array.shape))
    return lax.all_to_all(copies, axes, 0, 0, tiled=True)


def all_sum(array, axes):
    count = lax.axis_size(axes)
    rows = array.reshape(count, array.shape[0] // count, *array.shape[1:])
    share = jnp.sum(lax.all_to_all(rows, axes, 0, 0, tiled=True), axis=0)
    return spread(share, axes).reshape(array.shape)


def normal_solve(system):
    gram_matrix = jnp.dot(system, system.T, precision=lax.Precision.HIGHEST)
    factor = jnp.linalg.cholesky(gram_matrix)
    return jax.scipy.linalg.cho_solve((factor, True), system).T


def split_dot(left, right):
    high = right.astype(jnp.bfloat16)
    low = (right - high.astype(jnp.float32)).astype(jnp.bfloat16)
    both = jnp.dot(left, jnp.concatenate([high, low], axis=1), preferred_element_type=jnp.float32)
    return both[:, : right.shape[1]] + both[:, right.shape[1] :]


def per_device(flow_field, left_x, last_x, last_y, right_y, right_m, last_m):
    highest = lax.Precision.HIGHEST
    x_cells, y_cells, m_cells = flow_field.shape
    rank_cols = left_x.shape[1]
    sketch_cols = right_m.shape[1]
    flat_field = flow_field.reshape(x_cells * y_cells, m_cells)
    left_wide = left_x.astype(jnp.float32)
    left_all = spread(left_wide, "gx").reshape(-1, rank_cols)

    khatri = (last_x.astype(jnp.float32)[:, None, :] * last_y.astype(jnp.float32)[None]).astype(
        jnp.bfloat16
    )
    khatri = khatri.reshape(x_cells * y_cells, rank_cols)
    last_part = jnp.dot(khatri.T, flat_field, preferred_element_type=jnp.float32)
    first_terms = jnp.dot(flat_field, right_m, preferred_element_type=jnp.float32).reshape(
        x_cells, y_cells, sketch_cols
    )
    first_part = jnp.sum(first_terms * right_y.astype(jnp.float32)[None], axis=1)

    grams = jnp.concatenate(
        [
            jnp.dot(last_part, last_m.astype(jnp.float32), precision=highest),
            jnp.dot(left_wide.T, first_part, precision=highest),
        ],
        axis=0,
    )
    grams = all_sum(grams, ALL)
    pinv_last = normal_solve(grams[:rank_cols])
    pinv_first = normal_solve(grams[rank_cols:])

    projector = jnp.dot(last_m.astype(jnp.float32), pinv_last, precision=highest)
    projected = split_dot(flat_field, projector).reshape(x_cells, y_cells, rank_cols)

    group = ("gx", "gz")
    devices = lax.axis_size(group)
    y_share = y_cells // devices
    pieces = projected.reshape(x_cells, devices, y_share, rank_cols).transpose(1, 0, 2, 3)
    pieces = lax.all_to_all(pieces, group, 0, 0, tiled=True)
    pieces = pieces.reshape(lax.axis_size("gx"), lax.axis_size("gz"), x_cells, y_share * rank_cols)
    column = jnp.sum(pieces, axis=1).reshape(-1, y_share * rank_cols)
    sketched = jnp.dot(left_all.T, column, precision=highest)
    sketched = sketched.reshape(devices, rank_cols // devices, y_share, rank_cols)
    middle = lax.all_to_all(sketched, group, 0, 0, tiled=True)
    core_middle = middle.transpose(1, 0, 2, 3).reshape(rank_cols // devices, y_cells, rank_cols)

    core_last = all_sum(last_part, ("gx", "gy"))
    core_first = all_sum(jnp.dot(first_part, pinv_first, precision=highest), ("gy", "gz"))
    return (core_first, core_middle, core_last)


def solution(mesh):
    return jax.shard_map(
        per_device,
        mesh=mesh,
        in_specs=(
            P("gx", "gy", "gz"),
            P("gx", None),
            P("gx", None),
            P("gy", None),
            P("gy", None),
            P("gz", None),
            P("gz", None),
        ),
        out_specs=(P("gx", None), P(("gx", "gz"), "gy", None), P(None, "gz")),
        check_vma=False,
    )
```

```python
import functools

import jax
import jax.numpy as jnp
from jax import lax
from jax.experimental import pallas as pl
from jax.experimental.pallas import tpu as pltpu
from jax.sharding import PartitionSpec as P

ALL = ("gx", "gy", "gz")
HIGHEST = lax.Precision.HIGHEST
VMEM_BYTES = 48 * 1024 * 1024
ROWS = 8


def spread(array, axes):
    count = lax.axis_size(axes)
    copies = jnp.broadcast_to(array[None], (count, *array.shape))
    return lax.all_to_all(copies, axes, 0, 0, tiled=True)


def all_sum(array, axes):
    count = lax.axis_size(axes)
    rows = array.reshape(count, array.shape[0] // count, *array.shape[1:])
    share = jnp.sum(lax.all_to_all(rows, axes, 0, 0, tiled=True), axis=0)
    return spread(share, axes).reshape(array.shape)


def pair_sum(array, axis):
    if lax.axis_size(axis) != 2:
        return lax.psum(array, axis)
    return array + lax.ppermute(array, axis, [(0, 1), (1, 0)])


def split_terms(array):
    high = lax.reduce_precision(array, 8, 7)
    return high.astype(jnp.bfloat16), (array - high).astype(jnp.bfloat16)


def invert(matrices):
    size = matrices[0].shape[0]
    lanes = lax.broadcasted_iota(jnp.int32, (ROWS, size), 1)
    subs = lax.broadcasted_iota(jnp.int32, (ROWS, size), 0)
    blocks = [[m[r : r + ROWS] for r in range(0, size, ROWS)] for m in matrices]

    def column(block, at):
        return jnp.broadcast_to(block[:, at : at + 1], (ROWS, size))

    for panel in range(size // ROWS):
        first = panel * ROWS
        inside = (lanes >= first) & (lanes < first + ROWS)
        unit = (lanes - first == subs).astype(jnp.float32)
        for rows in blocks:
            pivots = [column(rows[panel], first + c) for c in range(ROWS)]
            solved = jnp.where(inside, unit, rows[panel])
            for k in range(ROWS):
                scale = 1.0 / pivots[k][k : k + 1]
                here = subs == k
                top = solved[k : k + 1] * scale
                solved = jnp.where(here, top, solved - pivots[k] * top)
                for c in range(k + 1, ROWS):
                    top = pivots[c][k : k + 1] * scale
                    pivots[c] = jnp.where(here, top, pivots[c] - pivots[k] * top)
            for r in range(len(rows)):
                if r == panel:
                    continue
                old = rows[r]
                new = jnp.where(inside, 0.0, old)
                for c in range(ROWS):
                    new = new - column(old, first + c) * solved[c : c + 1]
                rows[r] = new
            rows[panel] = solved
    return [jnp.concatenate(rows, axis=0) for rows in blocks]


def solve_kernel(grams, terms, first_rows, projected, core_first, flat):
    rank = grams.shape[0] // 2
    systems = [grams[:rank], grams[rank:]]
    contract = (((1,), (1,)), ((), ()))
    squares = [
        lax.dot_general(s, s, contract, precision=HIGHEST, preferred_element_type=jnp.float32)
        for s in systems
    ]
    inverses = invert(squares)
    pinvs = [
        jnp.dot(i, s, precision=HIGHEST, preferred_element_type=jnp.float32)
        for i, s in zip(inverses, systems)
    ]
    core_first[...] = lax.dot_general(
        first_rows[...], pinvs[1], contract, precision=HIGHEST, preferred_element_type=jnp.float32
    )
    flat[...] = lax.dot_general(
        terms[...], pinvs[0], contract, precision=HIGHEST, preferred_element_type=jnp.float32
    )
    y_cells, x_cells, _ = projected.shape
    for j in range(y_cells):
        projected[j] = flat[pl.ds(j, x_cells, stride=y_cells), :]


def solve(grams, terms, first_rows):
    x_cells, y_cells, sketch_cols = terms.shape
    rank = grams.shape[0] // 2
    return pl.pallas_call(
        solve_kernel,
        out_shape=(
            jax.ShapeDtypeStruct((y_cells, x_cells, rank), jnp.float32),
            jax.ShapeDtypeStruct((first_rows.shape[0], rank), jnp.float32),
        ),
        scratch_shapes=[pltpu.VMEM((x_cells * y_cells, rank), jnp.float32)],
        compiler_params=pltpu.CompilerParams(vmem_limit_bytes=VMEM_BYTES),
        name="solve",
    )(grams, terms.reshape(x_cells * y_cells, sketch_cols), first_rows)


def sketch_kernel(pieces, left, out):
    blocks, y_cells = pieces.shape[:2]
    weights = left[...].astype(jnp.bfloat16)
    for j in range(y_cells):
        column = jnp.concatenate([pieces[b, j] for b in range(blocks)], axis=0)
        high = column.astype(jnp.bfloat16)
        low = (column - high.astype(jnp.float32)).astype(jnp.bfloat16)
        both = lax.dot_general(
            weights,
            jnp.concatenate([high, low], axis=1),
            (((0,), (0,)), ((), ())),
            preferred_element_type=jnp.float32,
        )
        out[j] = both[:, : column.shape[1]] + both[:, column.shape[1] :]


def sketch(pieces, left):
    y_cells, cols = pieces.shape[1], pieces.shape[3]
    return pl.pallas_call(
        sketch_kernel,
        out_shape=jax.ShapeDtypeStruct((y_cells, left.shape[1], cols), jnp.float32),
        compiler_params=pltpu.CompilerParams(vmem_limit_bytes=VMEM_BYTES),
        name="sketch",
    )(pieces, left)


def per_device(flow_field, left_x, last_x, last_y, right_y, right_m, last_m):
    x_cells, y_cells, m_cells = flow_field.shape
    rank_cols = left_x.shape[1]
    sketch_cols = right_m.shape[1]
    flat_field = flow_field.reshape(x_cells * y_cells, m_cells)
    left_all = spread(left_x.astype(jnp.float32), "gx").reshape(-1, rank_cols)

    khatri = (last_x.astype(jnp.float32)[:, None, :] * last_y.astype(jnp.float32)[None]).astype(
        jnp.bfloat16
    )
    khatri = khatri.reshape(x_cells * y_cells, rank_cols)
    last_part = jnp.dot(khatri.T, flat_field, preferred_element_type=jnp.float32)
    first_terms = jnp.dot(flat_field, right_m, preferred_element_type=jnp.float32).reshape(
        x_cells, y_cells, sketch_cols
    )
    first_part = jnp.sum(first_terms * right_y.astype(jnp.float32)[None], axis=1)

    last_both = jnp.dot(
        jnp.concatenate(split_terms(last_part), axis=0), last_m, preferred_element_type=jnp.float32
    )
    first_both = jnp.dot(
        left_x.T,
        jnp.concatenate(split_terms(first_part), axis=1),
        preferred_element_type=jnp.float32,
    )
    grams = jnp.concatenate(
        [
            last_both[:rank_cols] + last_both[rank_cols:],
            first_both[:, :sketch_cols] + first_both[:, sketch_cols:],
        ],
        axis=0,
    )
    grams = all_sum(grams, ALL)

    shares = lax.axis_size("gz")
    y_share = y_cells // shares
    if shares == 2:
        here = lax.axis_index("gz")
        parts = flow_field.reshape(x_cells, 2, y_share, m_cells)
        kept, sent = (
            jnp.dot(
                lax.dynamic_index_in_dim(parts, at, 1, False).reshape(-1, m_cells),
                last_m,
                preferred_element_type=jnp.float32,
            ).reshape(x_cells, y_share, sketch_cols)
            for at in (here, 1 - here)
        )
        terms = kept + lax.ppermute(sent, "gz", [(0, 1), (1, 0)])
    else:
        terms = jnp.dot(flat_field, last_m, preferred_element_type=jnp.float32)
        terms = terms.reshape(x_cells, shares, y_share, sketch_cols).transpose(1, 0, 2, 3)
        terms = jnp.sum(lax.all_to_all(terms, "gz", 0, 0, tiled=True), axis=0)

    first_rows = pair_sum(pair_sum(first_part, "gy"), "gz")
    projected, core_first = solve(grams, terms, first_rows)

    blocks = lax.axis_size("gx")
    y_own = y_share // blocks
    pieces = projected.reshape(blocks, y_own, x_cells, rank_cols)
    pieces = lax.all_to_all(pieces, "gx", 0, 0, tiled=True)
    sketched = sketch(pieces, left_all)
    group = ("gx", "gz")
    devices = lax.axis_size(group)
    rank_own = rank_cols // devices
    sketched = sketched.reshape(y_own, devices, rank_own, rank_cols).transpose(1, 0, 2, 3)
    middle = lax.all_to_all(sketched, group, 0, 0, tiled=True)
    middle = middle.reshape(blocks, shares, y_own, rank_own, rank_cols)
    core_middle = middle.transpose(3, 1, 0, 2, 4).reshape(rank_own, y_cells, rank_cols)

    core_last = all_sum(last_part, ("gx", "gy"))
    return (core_first, core_middle, core_last)


def solution(mesh):
    return jax.shard_map(
        per_device,
        mesh=mesh,
        in_specs=(
            P("gx", "gy", "gz"),
            P("gx", None),
            P("gx", None),
            P("gy", None),
            P("gy", None),
            P("gz", None),
            P("gz", None),
        ),
        out_specs=(P("gx", None), P(("gx", "gz"), "gy", None), P(None, "gz")),
        check_vma=False,
    )
```

```python
import functools

import jax
import jax.numpy as jnp
from jax import lax
from jax.experimental import pallas as pl
from jax.experimental.pallas import tpu as pltpu
from jax.sharding import PartitionSpec as P

ALL = ("gx", "gy", "gz")
HIGHEST = lax.Precision.HIGHEST
VMEM_BYTES = 48 * 1024 * 1024
ROWS = 8
ROW_ROW = (((1,), (1,)), ((), ()))


def spread(array, axes):
    count = lax.axis_size(axes)
    copies = jnp.broadcast_to(array[None], (count, *array.shape))
    return lax.all_to_all(copies, axes, 0, 0, tiled=True)


def pair_sum(array, axis):
    if lax.axis_size(axis) != 2:
        return lax.psum(array, axis)
    return array + lax.ppermute(array, axis, [(0, 1), (1, 0)])


def split_terms(array):
    high = lax.reduce_precision(array, 8, 7)
    return high.astype(jnp.bfloat16), (array - high).astype(jnp.bfloat16)


def invert(matrices):
    size = matrices[0].shape[0]
    lanes = lax.broadcasted_iota(jnp.int32, (ROWS, size), 1)
    subs = lax.broadcasted_iota(jnp.int32, (ROWS, size), 0)
    blocks = [[m[r : r + ROWS] for r in range(0, size, ROWS)] for m in matrices]

    def column(block, at):
        return jnp.broadcast_to(block[:, at : at + 1], (ROWS, size))

    for panel in range(size // ROWS):
        first = panel * ROWS
        inside = (lanes >= first) & (lanes < first + ROWS)
        unit = (lanes - first == subs).astype(jnp.float32)
        for rows in blocks:
            pivots = [column(rows[panel], first + c) for c in range(ROWS)]
            solved = jnp.where(inside, unit, rows[panel])
            for k in range(ROWS):
                scale = 1.0 / pivots[k][k : k + 1]
                here = subs == k
                top = solved[k : k + 1] * scale
                solved = jnp.where(here, top, solved - pivots[k] * top)
                for c in range(k + 1, ROWS):
                    top = pivots[c][k : k + 1] * scale
                    pivots[c] = jnp.where(here, top, pivots[c] - pivots[k] * top)
            for r in range(len(rows)):
                if r == panel:
                    continue
                old = rows[r]
                new = jnp.where(inside, 0.0, old)
                for c in range(ROWS):
                    new = new - column(old, first + c) * solved[c : c + 1]
                rows[r] = new
            rows[panel] = solved
    return [jnp.concatenate(rows, axis=0) for rows in blocks]


def spd_inverse(system):
    square = lax.dot_general(
        system, system, ROW_ROW, precision=HIGHEST, preferred_element_type=jnp.float32
    )
    return invert([square])[0]


def last_kernel(shares, kept, received, projected, flat):
    system = shares[:, 0]
    for k in range(1, shares.shape[1]):
        system = system + shares[:, k]
    system = system.reshape(-1, system.shape[-1])
    pinv = jnp.dot(
        spd_inverse(system), system, precision=HIGHEST, preferred_element_type=jnp.float32
    )
    flat[...] = lax.dot_general(
        kept[...] + received[...],
        pinv,
        ROW_ROW,
        precision=HIGHEST,
        preferred_element_type=jnp.float32,
    )
    y_cells, x_cells, _ = projected.shape
    for j in range(y_cells):
        projected[j] = flat[pl.ds(j, x_cells, stride=y_cells), :]


def solve_last(shares, kept, received):
    x_cells, y_cells, sketch_cols = kept.shape
    rank = shares.shape[0] * shares.shape[2]
    return pl.pallas_call(
        last_kernel,
        out_shape=jax.ShapeDtypeStruct((y_cells, x_cells, rank), jnp.float32),
        scratch_shapes=[pltpu.VMEM((x_cells * y_cells, rank), jnp.float32)],
        compiler_params=pltpu.CompilerParams(vmem_limit_bytes=VMEM_BYTES),
        name="solve_last",
    )(
        shares,
        kept.reshape(x_cells * y_cells, sketch_cols),
        received.reshape(x_cells * y_cells, sketch_cols),
    )


def first_kernel(rows, all_rows, left, core_first):
    system = lax.dot_general(
        left[...],
        all_rows[...],
        (((0,), (0,)), ((), ())),
        precision=HIGHEST,
        preferred_element_type=jnp.float32,
    )
    inverse = spd_inverse(system)
    scores = lax.dot_general(
        rows[...], system, ROW_ROW, precision=HIGHEST, preferred_element_type=jnp.float32
    )
    core_first[...] = jnp.dot(
        scores, inverse, precision=HIGHEST, preferred_element_type=jnp.float32
    )


def solve_first(rows, all_rows, left):
    return pl.pallas_call(
        first_kernel,
        out_shape=jax.ShapeDtypeStruct((rows.shape[0], left.shape[1]), jnp.float32),
        compiler_params=pltpu.CompilerParams(vmem_limit_bytes=VMEM_BYTES),
        name="solve_first",
    )(rows, all_rows, left)


def sketch_kernel(pieces, left, out):
    blocks, y_cells = pieces.shape[:2]
    weights = left[...].astype(jnp.bfloat16)
    for j in range(y_cells):
        column = jnp.concatenate([pieces[b, j] for b in range(blocks)], axis=0)
        high = column.astype(jnp.bfloat16)
        low = (column - high.astype(jnp.float32)).astype(jnp.bfloat16)
        both = lax.dot_general(
            weights,
            jnp.concatenate([high, low], axis=1),
            (((0,), (0,)), ((), ())),
            preferred_element_type=jnp.float32,
        )
        out[j] = both[:, : column.shape[1]] + both[:, column.shape[1] :]


def sketch(pieces, left):
    y_cells, cols = pieces.shape[1], pieces.shape[3]
    return pl.pallas_call(
        sketch_kernel,
        out_shape=jax.ShapeDtypeStruct((y_cells, left.shape[1], cols), jnp.float32),
        compiler_params=pltpu.CompilerParams(vmem_limit_bytes=VMEM_BYTES),
        name="sketch",
    )(pieces, left)


def per_device(flow_field, left_x, last_x, last_y, right_y, right_m, last_m):
    x_cells, y_cells, m_cells = flow_field.shape
    rank_cols = left_x.shape[1]
    sketch_cols = right_m.shape[1]
    flat_field = flow_field.reshape(x_cells * y_cells, m_cells)
    blocks, shares = lax.axis_size("gx"), lax.axis_size("gz")

    khatri = (last_x.astype(jnp.float32)[:, None, :] * last_y.astype(jnp.float32)[None]).astype(
        jnp.bfloat16
    )
    khatri = khatri.reshape(x_cells * y_cells, rank_cols)
    last_part = jnp.dot(khatri.T, flat_field, preferred_element_type=jnp.float32)
    group = ("gx", "gy")
    own = rank_cols // lax.axis_size(group)
    last_rows = lax.all_to_all(last_part.reshape(-1, own, m_cells), group, 0, 0, tiled=True)
    last_rows = jnp.sum(last_rows, axis=0)
    both = jnp.dot(
        jnp.concatenate(split_terms(last_rows), axis=0), last_m, preferred_element_type=jnp.float32
    )
    system_shares = spread(both[:own] + both[own:], ALL).reshape(-1, shares, own, sketch_cols)
    if own % ROWS:
        system_shares = jnp.sum(system_shares, axis=1).reshape(-1, 1, ROWS, sketch_cols)
    core_last = lax.all_gather(last_rows, group, axis=0, tiled=True)

    first_terms = jnp.dot(flat_field, right_m, preferred_element_type=jnp.float32).reshape(
        x_cells, y_cells, sketch_cols
    )
    first_part = jnp.sum(first_terms * right_y.astype(jnp.float32)[None], axis=1)
    first_rows = pair_sum(pair_sum(first_part, "gy"), "gz")
    gathered = lax.all_gather(
        jnp.concatenate([first_rows, left_x.astype(jnp.float32)], axis=1), "gx", axis=0, tiled=True
    )
    first_all, left_all = gathered[:, :sketch_cols], gathered[:, sketch_cols:]

    y_share = y_cells // shares
    if shares == 2:
        here = lax.axis_index("gz")
        parts = flow_field.reshape(x_cells, 2, y_share, m_cells)
        kept, sent = (
            jnp.dot(
                lax.dynamic_index_in_dim(parts, at, 1, False).reshape(-1, m_cells),
                last_m,
                preferred_element_type=jnp.float32,
            ).reshape(x_cells, y_share, sketch_cols)
            for at in (here, 1 - here)
        )
        received = lax.ppermute(sent, "gz", [(0, 1), (1, 0)])
    else:
        terms = jnp.dot(flat_field, last_m, preferred_element_type=jnp.float32)
        terms = terms.reshape(x_cells, shares, y_share, sketch_cols).transpose(1, 0, 2, 3)
        terms = lax.all_to_all(terms, "gz", 0, 0, tiled=True)
        kept, received = terms[0], jnp.sum(terms[1:], axis=0)
    projected = solve_last(system_shares, kept, received)

    y_own = y_share // blocks
    pieces = projected.reshape(blocks, y_own, x_cells, rank_cols)
    pieces = lax.all_to_all(pieces, "gx", 0, 0, tiled=True)
    sketched = sketch(pieces, left_all)
    group = ("gx", "gz")
    devices = lax.axis_size(group)
    own = rank_cols // devices
    sketched = sketched.reshape(y_own, devices, own, rank_cols).transpose(1, 0, 2, 3)
    middle = lax.all_to_all(sketched, group, 0, 0, tiled=True)
    middle = middle.reshape(blocks, shares, y_own, own, rank_cols)
    core_middle = middle.transpose(3, 1, 0, 2, 4).reshape(own, y_cells, rank_cols)

    first_rows, _ = lax.optimization_barrier((first_rows, sketched))
    core_first = solve_first(first_rows, first_all, left_all)
    return (core_first, core_middle, core_last)


def solution(mesh):
    return jax.shard_map(
        per_device,
        mesh=mesh,
        in_specs=(
            P("gx", "gy", "gz"),
            P("gx", None),
            P("gx", None),
            P("gy", None),
            P("gy", None),
            P("gz", None),
            P("gz", None),
        ),
        out_specs=(P("gx", None), P(("gx", "gz"), "gy", None), P(None, "gz")),
        check_vma=False,
    )
```

```python
import functools

import jax
import jax.numpy as jnp
from jax import lax
from jax.experimental import pallas as pl
from jax.experimental.pallas import tpu as pltpu
from jax.sharding import PartitionSpec as P

ALL = ("gx", "gy", "gz")
HIGHEST = lax.Precision.HIGHEST
VMEM_BYTES = 48 * 1024 * 1024
ROWS = 8
LANES = 128
ROW_ROW = (((1,), (1,)), ((), ()))
COL_COL = (((0,), (0,)), ((), ()))


def axis_bits(axis):
    bit = lax.axis_size(axis) // 2
    while bit:
        yield bit
        bit //= 2


def swap(array, axis, bits):
    return lax.ppermute(array, axis, [(s, s ^ bits) for s in range(lax.axis_size(axis))])


def swap_sum(array, axis):
    for bit in axis_bits(axis):
        array = array + swap(array, axis, bit)
    return array


def swap_gather(array, axis):
    held, order = array[None], [0]
    for bit in axis_bits(axis):
        held = jnp.concatenate([held, swap(held, axis, bit)], axis=0)
        order += [o ^ bit for o in order]
    return held, order


def gather_rows(array, outer, inner):
    held = array[None, None]
    for dim, axis in ((0, outer), (1, inner)):
        shape = held.shape
        held = held.reshape(*shape[:dim], 1, 1, *shape[dim + 1 :])
        for bit in axis_bits(axis):
            other = swap(held, axis, bit)
            upper = (lax.axis_index(axis) & bit) != 0
            low = jnp.where(upper, other, held)
            high = jnp.where(upper, held, other)
            held = jnp.concatenate([low, high], axis=dim + 1)
            shape = held.shape
            held = held.reshape(*shape[:dim], shape[dim] * shape[dim + 1], 1, *shape[dim + 2 :])
        shape = held.shape
        held = held.reshape(*shape[: dim + 1], *shape[dim + 2 :])
    return held.reshape(-1, array.shape[-1])


def split_terms(array):
    high = lax.reduce_precision(array, 8, 7)
    return high.astype(jnp.bfloat16), (array - high).astype(jnp.bfloat16)


def invert(system):
    size = system.shape[0]
    lanes = lax.broadcasted_iota(jnp.int32, (ROWS, size), 1)
    subs = lax.broadcasted_iota(jnp.int32, (ROWS, size), 0)
    rows = [system[r : r + ROWS] for r in range(0, size, ROWS)]

    def column(block, at):
        return jnp.broadcast_to(block[:, at : at + 1], (ROWS, size))

    for panel in range(size // ROWS):
        first = panel * ROWS
        inside = (lanes >= first) & (lanes < first + ROWS)
        unit = (lanes - first == subs).astype(jnp.float32)
        pivots = [column(rows[panel], first + c) for c in range(ROWS)]
        solved = jnp.where(inside, unit, rows[panel])
        for k in range(ROWS):
            scale = 1.0 / pivots[k][k : k + 1]
            here = subs == k
            top = solved[k : k + 1] * scale
            solved = jnp.where(here, top, solved - pivots[k] * top)
            for c in range(k + 1, ROWS):
                top = pivots[c][k : k + 1] * scale
                pivots[c] = jnp.where(here, top, pivots[c] - pivots[k] * top)
        for r in range(len(rows)):
            if r == panel:
                continue
            old = rows[r]
            new = jnp.where(inside, 0.0, old)
            for c in range(ROWS):
                new = new - column(old, first + c) * solved[c : c + 1]
            rows[r] = new
        rows[panel] = solved
    return jnp.concatenate(rows, axis=0)


def spd_inverse(system):
    square = lax.dot_general(
        system, system, ROW_ROW, precision=HIGHEST, preferred_element_type=jnp.float32
    )
    return invert(square)


def local_kernel(
    shape, field, last_x, last_y, right_y, right_m, last_m, last_part, first_part, *outs
):
    shares, blocks, halves, y_piece = shape
    *terms, flat = outs
    x_cells, y_cells, m_cells = field.shape
    rows = field[...].reshape(x_cells * y_cells, m_cells)
    here = lax.axis_index("gz")

    term = jnp.dot(rows, last_m[...], preferred_element_type=jnp.float32)
    for c in range(flat.shape[0]):
        flat[c] = term[:, c * LANES : (c + 1) * LANES]
    for s in range(shares):
        start = (here ^ s) * (y_cells // shares)
        for h in range(halves):
            for b in range(blocks):
                for k in range(y_piece):
                    j = start + (b * halves + h) * y_piece + k
                    for c in range(flat.shape[0]):
                        terms[s * halves + h][b, k, :, c * LANES : (c + 1) * LANES] = flat[
                            c, pl.ds(j, x_cells, stride=y_cells), :
                        ]

    khatri = last_x[...].astype(jnp.float32)[:, None, :] * last_y[...].astype(jnp.float32)[None]
    khatri = khatri.astype(jnp.bfloat16).reshape(x_cells * y_cells, -1)
    part = lax.dot_general(khatri, rows, COL_COL, preferred_element_type=jnp.float32)

    @pl.when(pl.program_id(0) == 0)
    def _():
        last_part[...] = part

    @pl.when(pl.program_id(0) != 0)
    def _():
        last_part[...] += part

    first = jnp.dot(rows, right_m[...], preferred_element_type=jnp.float32)
    first = first.reshape(x_cells, y_cells, -1) * right_y[...].astype(jnp.float32)[None]
    first_part[...] = jnp.sum(first, axis=1)


def local_products(shape, field, last_x, last_y, right_y, right_m, last_m):
    shares, blocks, halves, y_piece = shape
    x_cells, y_cells, m_cells = field.shape
    rank, cols = last_x.shape[1], last_m.shape[1]
    whole = lambda *dims: pl.BlockSpec(dims, lambda i: (0,) * len(dims))
    term = jax.ShapeDtypeStruct((blocks, y_piece, x_cells, cols), jnp.float32)
    term_spec = pl.BlockSpec((blocks, y_piece, ROWS, cols), lambda i: (0, 0, i, 0))
    pieces = shares * halves
    return pl.pallas_call(
        functools.partial(local_kernel, shape),
        grid=(x_cells // ROWS,),
        in_specs=[
            pl.BlockSpec((ROWS, y_cells, m_cells), lambda i: (i, 0, 0)),
            pl.BlockSpec((ROWS, rank), lambda i: (i, 0)),
            whole(*last_y.shape),
            whole(*right_y.shape),
            whole(*right_m.shape),
            whole(*last_m.shape),
        ],
        out_specs=[
            whole(rank, m_cells),
            pl.BlockSpec((ROWS, cols), lambda i: (i, 0)),
            *([term_spec] * pieces),
        ],
        out_shape=[
            jax.ShapeDtypeStruct((rank, m_cells), jnp.float32),
            jax.ShapeDtypeStruct((x_cells, cols), jnp.float32),
            *([term] * pieces),
        ],
        scratch_shapes=[pltpu.VMEM((cols // LANES, ROWS * y_cells, LANES), jnp.float32)],
        compiler_params=pltpu.CompilerParams(vmem_limit_bytes=VMEM_BYTES),
        name="local_products",
    )(field, last_x, last_y, right_y, right_m, last_m)


def combine_kernel(shares, *refs):
    terms, outs = refs[:shares], refs[shares:]
    me = lax.axis_index("gx")
    for e, out in enumerate(outs):
        total = terms[0][me ^ e]
        for term in terms[1:]:
            total = total + term[me ^ e]
        out[...] = total


def combine(terms):
    blocks, *piece = terms[0].shape
    return pl.pallas_call(
        functools.partial(combine_kernel, len(terms)),
        out_shape=[jax.ShapeDtypeStruct(tuple(piece), jnp.float32)] * blocks,
        compiler_params=pltpu.CompilerParams(vmem_limit_bytes=VMEM_BYTES),
        name="combine",
    )(*terms)


def last_kernel(halves, shares, left, *refs):
    pieces, out = refs[:-1], refs[-1]
    blocks = len(pieces) // halves
    y_piece = pieces[0].shape[0]
    system = shares[:, 0]
    for k in range(1, shares.shape[1]):
        system = system + shares[:, k]
    system = system.reshape(-1, system.shape[-1])
    pinv = jnp.dot(
        spd_inverse(system), system, precision=HIGHEST, preferred_element_type=jnp.float32
    )
    weights = left[...].astype(jnp.bfloat16)
    for h in range(halves):
        for k in range(y_piece):
            column = jnp.concatenate(
                [piece[k] for piece in pieces[h * blocks : (h + 1) * blocks]], axis=0
            )
            high = column.astype(jnp.bfloat16)
            low = (column - high.astype(jnp.float32)).astype(jnp.bfloat16)
            sketched = lax.dot_general(
                weights, high, COL_COL, preferred_element_type=jnp.float32
            ) + lax.dot_general(weights, low, COL_COL, preferred_element_type=jnp.float32)
            core = lax.dot_general(
                sketched, pinv, ROW_ROW, precision=HIGHEST, preferred_element_type=jnp.float32
            )
            at = h * y_piece + k
            out[:, at] = core.reshape(out.shape[0], out.shape[2], out.shape[3])


def solve_last(halves, own, shares, left, pieces):
    y_own = halves * pieces[0].shape[0]
    rank = left.shape[1]
    return pl.pallas_call(
        functools.partial(last_kernel, halves),
        out_shape=jax.ShapeDtypeStruct((rank // own, y_own, own, rank), jnp.float32),
        compiler_params=pltpu.CompilerParams(vmem_limit_bytes=VMEM_BYTES),
        name="solve_last",
    )(shares, left, *pieces)


def first_kernel(rows, all_rows, left, core_first):
    system = lax.dot_general(
        left[...], all_rows[...], COL_COL, precision=HIGHEST, preferred_element_type=jnp.float32
    )
    inverse = spd_inverse(system)
    scores = lax.dot_general(
        rows[...], system, ROW_ROW, precision=HIGHEST, preferred_element_type=jnp.float32
    )
    core_first[...] = jnp.dot(
        scores, inverse, precision=HIGHEST, preferred_element_type=jnp.float32
    )


def solve_first(rows, all_rows, left):
    return pl.pallas_call(
        first_kernel,
        out_shape=jax.ShapeDtypeStruct((rows.shape[0], left.shape[1]), jnp.float32),
        compiler_params=pltpu.CompilerParams(vmem_limit_bytes=VMEM_BYTES),
        name="solve_first",
    )(rows, all_rows, left)


def per_device(flow_field, left_x, last_x, last_y, right_y, right_m, last_m):
    x_cells, y_cells, m_cells = flow_field.shape
    rank = left_x.shape[1]
    cols = right_m.shape[1]
    blocks, shares = lax.axis_size("gx"), lax.axis_size("gz")
    y_own = y_cells // shares // blocks
    halves = 2 if y_own % 2 == 0 else 1

    last_part, first_part, *terms = local_products(
        (shares, blocks, halves, y_own // halves),
        flow_field,
        last_x,
        last_y,
        right_y,
        right_m,
        last_m,
    )

    for at in range(halves, len(terms)):
        terms[at] = swap(terms[at], "gz", at // halves)
    left_all, order = swap_gather(left_x.astype(jnp.float32), "gx")
    left_all = left_all.reshape(-1, rank)
    pieces = []
    for h in range(halves):
        sent = combine(terms[h::halves])
        pieces += [swap(sent[e], "gx", e) if e else sent[e] for e in order]

    group = ("gx", "gy")
    own = rank // lax.axis_size(group)
    last_rows = lax.all_to_all(last_part.reshape(-1, own, m_cells), group, 0, 0, tiled=True)
    last_rows = jnp.sum(last_rows, axis=0)
    both = jnp.dot(
        jnp.concatenate(split_terms(last_rows), axis=0), last_m, preferred_element_type=jnp.float32
    )
    both = both[:own] + both[own:]
    count = lax.axis_size(ALL)
    copies = jnp.broadcast_to(both[None], (count, own, cols))
    system = lax.all_to_all(copies, ALL, 0, 0, tiled=True).reshape(-1, shares, own, cols)
    if own % ROWS:
        system = jnp.sum(system, axis=1).reshape(-1, 1, ROWS, cols)
    core_last = gather_rows(last_rows, *group)

    group = ("gx", "gz")
    devices = lax.axis_size(group)
    own = rank // devices
    if own % ROWS:
        middle = solve_last(halves, rank, system, left_all, pieces)
        middle = middle.reshape(y_own, devices, own, rank).transpose(1, 0, 2, 3)
    else:
        middle = solve_last(halves, own, system, left_all, pieces)
    received = lax.all_to_all(middle, group, 0, 0, tiled=True)
    received = received.reshape(blocks, shares, y_own, own, rank)
    core_middle = received.transpose(3, 1, 0, 2, 4).reshape(own, y_cells, rank)

    first_rows = swap_sum(swap_sum(first_part, "gy"), "gz")
    first_all = swap_gather(first_rows, "gx")[0].reshape(-1, cols)
    first_rows, _ = lax.optimization_barrier((first_rows, middle))
    core_first = solve_first(first_rows, first_all, left_all)
    return (core_first, core_middle, core_last)


def solution(mesh):
    return jax.shard_map(
        per_device,
        mesh=mesh,
        in_specs=(
            P("gx", "gy", "gz"),
            P("gx", None),
            P("gx", None),
            P("gy", None),
            P("gy", None),
            P("gz", None),
            P("gz", None),
        ),
        out_specs=(P("gx", None), P(("gx", "gz"), "gy", None), P(None, "gz")),
        check_vma=False,
    )
```

```python
import functools

import jax
import jax.numpy as jnp
from jax import lax
from jax.experimental import pallas as pl
from jax.experimental.pallas import tpu as pltpu
from jax.sharding import PartitionSpec as P

ALL = ("gx", "gy", "gz")
HIGHEST = lax.Precision.HIGHEST
VMEM_BYTES = 48 * 1024 * 1024
LOCAL_VMEM_BYTES = 63 * 1024 * 1024
ROWS = 8
LANES = 128
ROW_ROW = (((1,), (1,)), ((), ()))
COL_COL = (((0,), (0,)), ((), ()))


def axis_bits(axis):
    bit = lax.axis_size(axis) // 2
    while bit:
        yield bit
        bit //= 2


def swap(array, axis, bits):
    return lax.ppermute(array, axis, [(s, s ^ bits) for s in range(lax.axis_size(axis))])


def swap_sum(array, axis):
    for bit in axis_bits(axis):
        array = array + swap(array, axis, bit)
    return array


def swap_gather(array, axis):
    held, order = array[None], [0]
    for bit in axis_bits(axis):
        held = jnp.concatenate([held, swap(held, axis, bit)], axis=0)
        order += [o ^ bit for o in order]
    return held, order


def gather_rows(array, outer, inner):
    held = array[None, None]
    for dim, axis in ((0, outer), (1, inner)):
        shape = held.shape
        held = held.reshape(*shape[:dim], 1, 1, *shape[dim + 1 :])
        for bit in axis_bits(axis):
            other = swap(held, axis, bit)
            upper = (lax.axis_index(axis) & bit) != 0
            low = jnp.where(upper, other, held)
            high = jnp.where(upper, held, other)
            held = jnp.concatenate([low, high], axis=dim + 1)
            shape = held.shape
            held = held.reshape(*shape[:dim], shape[dim] * shape[dim + 1], 1, *shape[dim + 2 :])
        shape = held.shape
        held = held.reshape(*shape[: dim + 1], *shape[dim + 2 :])
    return held.reshape(-1, array.shape[-1])


def split_terms(array):
    high = lax.reduce_precision(array, 8, 7)
    return high.astype(jnp.bfloat16), (array - high).astype(jnp.bfloat16)


def invert(system):
    size = system.shape[0]
    lanes = lax.broadcasted_iota(jnp.int32, (ROWS, size), 1)
    subs = lax.broadcasted_iota(jnp.int32, (ROWS, size), 0)
    rows = [system[r : r + ROWS] for r in range(0, size, ROWS)]

    def column(block, at):
        return jnp.broadcast_to(block[:, at : at + 1], (ROWS, size))

    for panel in range(size // ROWS):
        first = panel * ROWS
        inside = (lanes >= first) & (lanes < first + ROWS)
        unit = (lanes - first == subs).astype(jnp.float32)
        pivots = [column(rows[panel], first + c) for c in range(ROWS)]
        solved = jnp.where(inside, unit, rows[panel])
        for k in range(ROWS):
            scale = 1.0 / pivots[k][k : k + 1]
            here = subs == k
            top = solved[k : k + 1] * scale
            solved = jnp.where(here, top, solved - pivots[k] * top)
            for c in range(k + 1, ROWS):
                top = pivots[c][k : k + 1] * scale
                pivots[c] = jnp.where(here, top, pivots[c] - pivots[k] * top)
        for r in range(len(rows)):
            if r == panel:
                continue
            old = rows[r]
            new = jnp.where(inside, 0.0, old)
            for c in range(ROWS):
                new = new - column(old, first + c) * solved[c : c + 1]
            rows[r] = new
        rows[panel] = solved
    return jnp.concatenate(rows, axis=0)


def spd_inverse(system):
    square = lax.dot_general(
        system, system, ROW_ROW, precision=HIGHEST, preferred_element_type=jnp.float32
    )
    return invert(square)


def local_kernel(
    chunks,
    shares,
    field_hbm,
    last_x_hbm,
    last_y_hbm,
    right_y_hbm,
    right_m_hbm,
    last_m_hbm,
    last_part,
    first_part,
    *refs,
):
    terms = refs[:shares]
    field, last_x, last_y, right_y, right_m, last_m, flat, sems = refs[shares:]
    x_cells, y_cells, m_cells = field.shape
    step = x_cells // chunks
    y_share = y_cells // shares
    parts = [pl.ds(n * step, step) for n in range(chunks)]
    copies = [
        pltpu.make_async_copy(last_m_hbm, last_m, sems.at[0]),
        pltpu.make_async_copy(field_hbm.at[parts[0]], field.at[parts[0]], sems.at[1]),
        pltpu.make_async_copy(last_x_hbm, last_x, sems.at[2]),
        pltpu.make_async_copy(last_y_hbm, last_y, sems.at[3]),
        pltpu.make_async_copy(right_m_hbm, right_m, sems.at[4]),
        pltpu.make_async_copy(right_y_hbm, right_y, sems.at[5]),
    ]
    for n in range(1, chunks):
        copies.append(
            pltpu.make_async_copy(field_hbm.at[parts[n]], field.at[parts[n]], sems.at[5 + n])
        )
    for copy in copies:
        copy.start()
    here = lax.axis_index("gz")
    for n in range(chunks):
        if n == 0:
            copies[0].wait()
            copies[1].wait()
        else:
            copies[5 + n].wait()
        rows = field[parts[n]].reshape(step * y_cells, m_cells)
        term = jnp.dot(rows, last_m[...], preferred_element_type=jnp.float32)
        for c in range(flat.shape[0]):
            flat[c] = term[:, c * LANES : (c + 1) * LANES]
        for s in range(shares):
            start = (here ^ s) * y_share
            for j in range(y_share):
                for c in range(flat.shape[0]):
                    terms[s][j, parts[n], c * LANES : (c + 1) * LANES] = flat[
                        c, pl.ds(start + j, step, stride=y_cells), :
                    ]

        if n == 0:
            copies[2].wait()
            copies[3].wait()
        left = last_x[parts[n]].astype(jnp.float32)[:, None, :]
        khatri = left * last_y[...].astype(jnp.float32)[None]
        khatri = khatri.astype(jnp.bfloat16).reshape(step * y_cells, -1)
        part = lax.dot_general(khatri, rows, COL_COL, preferred_element_type=jnp.float32)
        if n == 0:
            last_part[...] = part
            copies[4].wait()
            copies[5].wait()
        else:
            last_part[...] += part

        first = jnp.dot(rows, right_m[...], preferred_element_type=jnp.float32)
        first = first.reshape(step, y_cells, -1) * right_y[...].astype(jnp.float32)[None]
        first_part[parts[n], :] = jnp.sum(first, axis=1)


def local_products(shares, field, last_x, last_y, right_y, right_m, last_m):
    x_cells, y_cells, m_cells = field.shape
    rank, cols = last_x.shape[1], last_m.shape[1]
    chunks = max(x_cells // 16, 1)
    inputs = (field, last_x, last_y, right_y, right_m, last_m)
    term = jax.ShapeDtypeStruct((y_cells // shares, x_cells, cols), jnp.float32)
    return pl.pallas_call(
        functools.partial(local_kernel, chunks, shares),
        in_specs=[pl.BlockSpec(memory_space=pltpu.HBM)] * len(inputs),
        out_shape=[
            jax.ShapeDtypeStruct((rank, m_cells), jnp.float32),
            jax.ShapeDtypeStruct((x_cells, cols), jnp.float32),
            *([term] * shares),
        ],
        scratch_shapes=[
            *(pltpu.VMEM(x.shape, x.dtype) for x in inputs),
            pltpu.VMEM((cols // LANES, x_cells // chunks * y_cells, LANES), jnp.float32),
            pltpu.SemaphoreType.DMA((5 + chunks,)),
        ],
        compiler_params=pltpu.CompilerParams(vmem_limit_bytes=LOCAL_VMEM_BYTES),
        name="local_products",
    )(*inputs)


def last_kernel(system_shares, *refs):
    terms, projected = refs[:-1], refs[-1]
    system = system_shares[:, 0]
    for k in range(1, system_shares.shape[1]):
        system = system + system_shares[:, k]
    system = system.reshape(-1, system.shape[-1])
    pinv = jnp.dot(
        spd_inverse(system), system, precision=HIGHEST, preferred_element_type=jnp.float32
    )
    total = terms[0][...]
    for term in terms[1:]:
        total = total + term[...]
    core = lax.dot_general(
        total.reshape(-1, total.shape[-1]),
        pinv,
        ROW_ROW,
        precision=HIGHEST,
        preferred_element_type=jnp.float32,
    )
    projected[...] = core.reshape(projected.shape)


def solve_last(system_shares, terms):
    rank = system_shares.shape[0] * system_shares.shape[2]
    return pl.pallas_call(
        last_kernel,
        out_shape=jax.ShapeDtypeStruct((*terms[0].shape[:2], rank), jnp.float32),
        compiler_params=pltpu.CompilerParams(vmem_limit_bytes=VMEM_BYTES),
        name="solve_last",
    )(system_shares, *terms)


def sketch_kernel(order, left_at, pieces, packed, out):
    me = lax.axis_index("gx")
    blocks, y_own, x_cells, cols = pieces.shape
    weights = jnp.concatenate(
        [packed[k, left_at : left_at + x_cells] for k in range(blocks)], axis=0
    ).astype(jnp.bfloat16)
    for j in range(y_own):
        column = jnp.concatenate([pieces[me ^ o, j] for o in order], axis=0)
        high = column.astype(jnp.bfloat16)
        low = (column - high.astype(jnp.float32)).astype(jnp.bfloat16)
        both = lax.dot_general(
            weights,
            jnp.concatenate([high, low], axis=1),
            COL_COL,
            preferred_element_type=jnp.float32,
        )
        both = both[:, :cols] + both[:, cols:]
        out[:, j] = both.reshape(out.shape[0], out.shape[2], cols)


def sketch(order, left_at, own, pieces, packed):
    y_own, cols = pieces.shape[1], pieces.shape[3]
    rank = packed.shape[2]
    return pl.pallas_call(
        functools.partial(sketch_kernel, order, left_at),
        out_shape=jax.ShapeDtypeStruct((rank // own, y_own, own, cols), jnp.float32),
        compiler_params=pltpu.CompilerParams(vmem_limit_bytes=VMEM_BYTES),
        name="sketch",
    )(pieces, packed)


def first_kernel(first_at, left_at, rows, packed, core_first):
    x_cells, cols = rows.shape
    count = cols // LANES
    blocks = range(packed.shape[0])
    left = jnp.concatenate([packed[k, left_at : left_at + x_cells] for k in blocks], axis=0)
    all_rows = jnp.concatenate(
        [
            jnp.concatenate(
                [
                    packed[k, first_at + c * x_cells : first_at + (c + 1) * x_cells]
                    for c in range(count)
                ],
                axis=1,
            )
            for k in blocks
        ],
        axis=0,
    )
    system = lax.dot_general(
        left, all_rows, COL_COL, precision=HIGHEST, preferred_element_type=jnp.float32
    )
    inverse = spd_inverse(system)
    scores = lax.dot_general(
        rows[...], system, ROW_ROW, precision=HIGHEST, preferred_element_type=jnp.float32
    )
    core_first[...] = jnp.dot(
        scores, inverse, precision=HIGHEST, preferred_element_type=jnp.float32
    )


def solve_first(first_at, left_at, rows, packed):
    return pl.pallas_call(
        functools.partial(first_kernel, first_at, left_at),
        out_shape=jax.ShapeDtypeStruct((rows.shape[0], packed.shape[2]), jnp.float32),
        compiler_params=pltpu.CompilerParams(vmem_limit_bytes=VMEM_BYTES),
        name="solve_first",
    )(rows, packed)


def place_kernel(outer_order, inner_order, packed, core_last):
    own = packed.shape[3]
    outer, inner = lax.axis_index("gx"), lax.axis_index("gy")
    for n, i in enumerate(inner_order):
        for k, o in enumerate(outer_order):
            at = ((outer ^ o) * len(inner_order) + (inner ^ i)) * own
            for c in range(packed.shape[2]):
                core_last[pl.ds(pl.multiple_of(at, own), own), c * LANES : (c + 1) * LANES] = (
                    packed[n, k, c]
                )


def place(outer_order, inner_order, packed):
    inner, outer, count, own, lanes = packed.shape
    return pl.pallas_call(
        functools.partial(place_kernel, outer_order, inner_order),
        out_shape=jax.ShapeDtypeStruct((inner * outer * own, count * lanes), jnp.float32),
        compiler_params=pltpu.CompilerParams(vmem_limit_bytes=VMEM_BYTES),
        name="place",
    )(packed)


def per_device(flow_field, left_x, last_x, last_y, right_y, right_m, last_m):
    x_cells, y_cells, m_cells = flow_field.shape
    rank = left_x.shape[1]
    cols = right_m.shape[1]
    blocks, shares = lax.axis_size("gx"), lax.axis_size("gz")
    y_share = y_cells // shares
    y_own = y_share // blocks

    last_part, first_part, *terms = local_products(
        shares, flow_field, last_x, last_y, right_y, right_m, last_m
    )

    for s in range(1, shares):
        terms[s] = swap(terms[s], "gz", s)

    group = ("gx", "gy")
    own = rank // lax.axis_size(group)
    last_rows = lax.all_to_all(last_part.reshape(-1, own, m_cells), group, 0, 0, tiled=True)
    last_rows = jnp.sum(last_rows, axis=0)
    both = jnp.dot(
        jnp.concatenate(split_terms(last_rows), axis=0), last_m, preferred_element_type=jnp.float32
    )
    both = both[:own] + both[own:]
    count = lax.axis_size(ALL)
    copies = jnp.broadcast_to(both[None], (count, own, cols))
    system = lax.all_to_all(copies, ALL, 0, 0, tiled=True).reshape(-1, shares, own, cols)
    if own % ROWS:
        system = jnp.sum(system, axis=1).reshape(-1, 1, ROWS, cols)
    projected = solve_last(system, terms)

    first_rows = swap_sum(swap_sum(first_part, "gy"), "gz")
    packed = jnp.concatenate(
        [
            last_rows.reshape(own, -1, LANES).transpose(1, 0, 2).reshape(-1, LANES),
            first_rows.reshape(x_cells, -1, LANES).transpose(1, 0, 2).reshape(-1, LANES),
            left_x.astype(jnp.float32),
        ],
        axis=0,
    )
    first_at = own * m_cells // LANES
    left_at = first_at + x_cells * cols // LANES
    packed, order = swap_gather(packed, "gx")

    pieces = projected.reshape(blocks, y_own, x_cells, rank)
    pieces = lax.all_to_all(pieces, "gx", 0, 0, tiled=True)
    group = ("gx", "gz")
    devices = lax.axis_size(group)
    rank_own = rank // devices
    if rank_own % ROWS:
        middle = sketch(order, left_at, rank, pieces, packed)
        middle = middle.reshape(y_own, devices, rank_own, rank).transpose(1, 0, 2, 3)
    else:
        middle = sketch(order, left_at, rank_own, pieces, packed)
    received = lax.all_to_all(middle, group, 0, 0, tiled=True)
    received = received.reshape(blocks, shares, y_own, rank_own, rank)
    core_middle = received.transpose(3, 1, 0, 2, 4).reshape(rank_own, y_cells, rank)

    if own % ROWS:
        core_last = gather_rows(last_rows, "gx", "gy")
    else:
        core_last = packed[:, :first_at].reshape(blocks, -1, own, LANES)
        core_last, inner_order = swap_gather(core_last, "gy")
        core_last = place(order, inner_order, core_last)

    first_rows, _ = lax.optimization_barrier((first_rows, middle))
    core_first = solve_first(first_at, left_at, first_rows, packed)
    return (core_first, core_middle, core_last)


def solution(mesh):
    return jax.shard_map(
        per_device,
        mesh=mesh,
        in_specs=(
            P("gx", "gy", "gz"),
            P("gx", None),
            P("gx", None),
            P("gy", None),
            P("gy", None),
            P("gz", None),
            P("gz", None),
        ),
        out_specs=(P("gx", None), P(("gx", "gz"), "gy", None), P(None, "gz")),
        check_vma=False,
    )
```

```python
import functools

import jax
import jax.numpy as jnp
from jax import lax
from jax.experimental import pallas as pl
from jax.experimental.pallas import tpu as pltpu
from jax.sharding import PartitionSpec as P

ALL = ("gx", "gy", "gz")
HIGHEST = lax.Precision.HIGHEST
VMEM_BYTES = 48 * 1024 * 1024
LOCAL_VMEM_BYTES = 63 * 1024 * 1024
ROWS = 8
LANES = 128
ROW_ROW = (((1,), (1,)), ((), ()))
COL_COL = (((0,), (0,)), ((), ()))


def axis_bits(axis):
    bit = lax.axis_size(axis) // 2
    while bit:
        yield bit
        bit //= 2


def swap(array, axis, bits):
    return lax.ppermute(array, axis, [(s, s ^ bits) for s in range(lax.axis_size(axis))])


def swap_sum(array, axis):
    for bit in axis_bits(axis):
        array = array + swap(array, axis, bit)
    return array


def swap_gather(array, axis, gate=None):
    held, order = array[None], [0]
    for bit in axis_bits(axis):
        if bit == 1 and gate is not None:
            held, gate = lax.optimization_barrier((held, gate))
        held = jnp.concatenate([held, swap(held, axis, bit)], axis=0)
        order += [o ^ bit for o in order]
    return held, order, gate


def gather_rows(array, outer, inner):
    held = array[None, None]
    for dim, axis in ((0, outer), (1, inner)):
        shape = held.shape
        held = held.reshape(*shape[:dim], 1, 1, *shape[dim + 1 :])
        for bit in axis_bits(axis):
            other = swap(held, axis, bit)
            upper = (lax.axis_index(axis) & bit) != 0
            low = jnp.where(upper, other, held)
            high = jnp.where(upper, held, other)
            held = jnp.concatenate([low, high], axis=dim + 1)
            shape = held.shape
            held = held.reshape(*shape[:dim], shape[dim] * shape[dim + 1], 1, *shape[dim + 2 :])
        shape = held.shape
        held = held.reshape(*shape[: dim + 1], *shape[dim + 2 :])
    return held.reshape(-1, array.shape[-1])


def split_terms(array):
    high = lax.reduce_precision(array, 8, 7)
    return high.astype(jnp.bfloat16), (array - high).astype(jnp.bfloat16)


def invert(system):
    size = system.shape[0]
    lanes = lax.broadcasted_iota(jnp.int32, (ROWS, size), 1)
    subs = lax.broadcasted_iota(jnp.int32, (ROWS, size), 0)
    rows = [system[r : r + ROWS] for r in range(0, size, ROWS)]

    def column(block, at):
        return jnp.broadcast_to(block[:, at : at + 1], (ROWS, size))

    for panel in range(size // ROWS):
        first = panel * ROWS
        inside = (lanes >= first) & (lanes < first + ROWS)
        unit = (lanes - first == subs).astype(jnp.float32)
        pivots = [column(rows[panel], first + c) for c in range(ROWS)]
        solved = jnp.where(inside, unit, rows[panel])
        for k in range(ROWS):
            scale = 1.0 / pivots[k][k : k + 1]
            here = subs == k
            top = solved[k : k + 1] * scale
            solved = jnp.where(here, top, solved - pivots[k] * top)
            for c in range(k + 1, ROWS):
                top = pivots[c][k : k + 1] * scale
                pivots[c] = jnp.where(here, top, pivots[c] - pivots[k] * top)
        for r in range(len(rows)):
            if r == panel:
                continue
            old = rows[r]
            new = jnp.where(inside, 0.0, old)
            for c in range(ROWS):
                new = new - column(old, first + c) * solved[c : c + 1]
            rows[r] = new
        rows[panel] = solved
    return jnp.concatenate(rows, axis=0)


def spd_inverse(system):
    square = lax.dot_general(
        system, system, ROW_ROW, precision=HIGHEST, preferred_element_type=jnp.float32
    )
    return invert(square)


def local_kernel(
    chunks,
    shares,
    field_hbm,
    last_x_hbm,
    last_y_hbm,
    right_y_hbm,
    right_m_hbm,
    last_m_hbm,
    last_part,
    first_part,
    *refs,
):
    terms_hbm = refs[:shares]
    field, last_x, last_y, right_y, right_m, last_m, terms, sems, out_sems = refs[shares:]
    x_cells, y_cells, m_cells = field.shape
    step = x_cells // chunks
    y_share = y_cells // shares
    parts = [pl.ds(n * step, step) for n in range(chunks)]
    copies = [
        pltpu.make_async_copy(last_m_hbm, last_m, sems.at[0]),
        pltpu.make_async_copy(field_hbm.at[parts[0]], field.at[parts[0]], sems.at[1]),
        pltpu.make_async_copy(last_x_hbm, last_x, sems.at[2]),
        pltpu.make_async_copy(last_y_hbm, last_y, sems.at[3]),
        pltpu.make_async_copy(right_m_hbm, right_m, sems.at[4]),
        pltpu.make_async_copy(right_y_hbm, right_y, sems.at[5]),
    ]
    for n in range(1, chunks):
        copies.append(
            pltpu.make_async_copy(field_hbm.at[parts[n]], field.at[parts[n]], sems.at[5 + n])
        )
    for copy in copies:
        copy.start()
    here = lax.axis_index("gz")
    leaving = []
    copies[0].wait()
    for n in range(chunks):
        copies[5 + n if n else 1].wait()
        for s in reversed(range(shares)):
            start = pl.multiple_of((here ^ s) * y_share, y_share)
            rows = field[parts[n], pl.ds(start, y_share), :].reshape(step * y_share, m_cells)
            term = jnp.dot(rows, last_m[...], preferred_element_type=jnp.float32)
            terms[s, parts[n]] = term.reshape(step, y_share, -1)
            leaving.append(
                pltpu.make_async_copy(
                    terms.at[s, parts[n]], terms_hbm[s].at[parts[n]], out_sems.at[s, n]
                )
            )
            leaving[-1].start()

    for copy in copies[2:6]:
        copy.wait()
    for n in range(chunks):
        rows = field[parts[n]].reshape(step * y_cells, m_cells)
        left = last_x[parts[n]].astype(jnp.float32)[:, None, :]
        khatri = left * last_y[...].astype(jnp.float32)[None]
        khatri = khatri.astype(jnp.bfloat16).reshape(step * y_cells, -1)
        part = lax.dot_general(khatri, rows, COL_COL, preferred_element_type=jnp.float32)
        if n == 0:
            last_part[...] = part
        else:
            last_part[...] += part
        first = jnp.dot(rows, right_m[...], preferred_element_type=jnp.float32)
        first = first.reshape(step, y_cells, -1) * right_y[...].astype(jnp.float32)[None]
        first_part[parts[n], :] = jnp.sum(first, axis=1)
    for copy in leaving:
        copy.wait()


def local_products(shares, field, last_x, last_y, right_y, right_m, last_m):
    x_cells, y_cells, m_cells = field.shape
    rank, cols = last_x.shape[1], last_m.shape[1]
    chunks = max(x_cells // 8, 1)
    inputs = (field, last_x, last_y, right_y, right_m, last_m)
    dims = (x_cells, y_cells // shares, cols)
    hbm = pl.BlockSpec(memory_space=pltpu.HBM)
    vmem = pl.BlockSpec(memory_space=pltpu.VMEM)
    return pl.pallas_call(
        functools.partial(local_kernel, chunks, shares),
        in_specs=[hbm] * len(inputs),
        out_specs=[vmem, vmem, *([hbm] * shares)],
        out_shape=[
            jax.ShapeDtypeStruct((rank, m_cells), jnp.float32),
            jax.ShapeDtypeStruct((x_cells, cols), jnp.float32),
            *([jax.ShapeDtypeStruct(dims, jnp.float32)] * shares),
        ],
        scratch_shapes=[
            *(pltpu.VMEM(x.shape, x.dtype) for x in inputs),
            pltpu.VMEM((shares, *dims), jnp.float32),
            pltpu.SemaphoreType.DMA((5 + chunks,)),
            pltpu.SemaphoreType.DMA((shares, chunks)),
        ],
        compiler_params=pltpu.CompilerParams(vmem_limit_bytes=LOCAL_VMEM_BYTES),
        name="local_products",
    )(*inputs)


def last_kernel(system_shares, *refs):
    *terms, projected, flat = refs
    system = system_shares[:, 0]
    for k in range(1, system_shares.shape[1]):
        system = system + system_shares[:, k]
    system = system.reshape(-1, system.shape[-1])
    pinv = jnp.dot(
        spd_inverse(system), system, precision=HIGHEST, preferred_element_type=jnp.float32
    )
    total = terms[0][...]
    for term in terms[1:]:
        total = total + term[...]
    flat[...] = lax.dot_general(
        total.reshape(-1, total.shape[-1]),
        pinv,
        ROW_ROW,
        precision=HIGHEST,
        preferred_element_type=jnp.float32,
    )
    y_cells, x_cells, _ = projected.shape
    for j in range(y_cells):
        projected[j] = flat[pl.ds(j, x_cells, stride=y_cells), :]


def solve_last(system_shares, terms):
    rank = system_shares.shape[0] * system_shares.shape[2]
    x_cells, y_cells, _ = terms[0].shape
    return pl.pallas_call(
        last_kernel,
        out_shape=jax.ShapeDtypeStruct((y_cells, x_cells, rank), jnp.float32),
        scratch_shapes=[pltpu.VMEM((x_cells * y_cells, rank), jnp.float32)],
        compiler_params=pltpu.CompilerParams(vmem_limit_bytes=VMEM_BYTES),
        name="solve_last",
    )(system_shares, *terms)


def sketch_kernel(order, left_at, pieces, packed, out):
    me = lax.axis_index("gx")
    blocks, y_own, x_cells, cols = pieces.shape
    weights = jnp.concatenate(
        [packed[k, left_at : left_at + x_cells] for k in range(blocks)], axis=0
    ).astype(jnp.bfloat16)
    for j in range(y_own):
        column = jnp.concatenate([pieces[me ^ o, j] for o in order], axis=0)
        high = column.astype(jnp.bfloat16)
        low = (column - high.astype(jnp.float32)).astype(jnp.bfloat16)
        both = lax.dot_general(
            weights,
            jnp.concatenate([high, low], axis=1),
            COL_COL,
            preferred_element_type=jnp.float32,
        )
        both = both[:, :cols] + both[:, cols:]
        out[:, j] = both.reshape(out.shape[0], out.shape[2], cols)


def sketch(order, left_at, own, pieces, packed):
    y_own, cols = pieces.shape[1], pieces.shape[3]
    rank = packed.shape[2]
    return pl.pallas_call(
        functools.partial(sketch_kernel, order, left_at),
        out_shape=jax.ShapeDtypeStruct((rank // own, y_own, own, cols), jnp.float32),
        compiler_params=pltpu.CompilerParams(vmem_limit_bytes=VMEM_BYTES),
        name="sketch",
    )(pieces, packed)


def first_sums_kernel(first_at, left_at, rows, packed, sums):
    x_cells, cols = rows.shape
    blocks = range(packed.shape[0])
    left = jnp.concatenate([packed[k, left_at : left_at + x_cells] for k in blocks], axis=0)
    sums[:x_cells] = rows[...]
    for c in range(cols // LANES):
        at = first_at + c * x_cells
        sums[x_cells:, c * LANES : (c + 1) * LANES] = lax.dot_general(
            left,
            jnp.concatenate([packed[k, at : at + x_cells] for k in blocks], axis=0),
            COL_COL,
            precision=HIGHEST,
            preferred_element_type=jnp.float32,
        )


def first_sums(first_at, left_at, rows, packed):
    return pl.pallas_call(
        functools.partial(first_sums_kernel, first_at, left_at),
        out_shape=jax.ShapeDtypeStruct(
            (rows.shape[0] + packed.shape[2], rows.shape[1]), jnp.float32
        ),
        compiler_params=pltpu.CompilerParams(vmem_limit_bytes=VMEM_BYTES),
        name="first_sums",
    )(rows, packed)


def first_kernel(*refs):
    *sums, core_first = refs
    x_cells = core_first.shape[0]
    total = sums[0][...]
    for other in sums[1:]:
        total = total + other[...]
    system = total[x_cells:]
    inverse = spd_inverse(system)
    scores = lax.dot_general(
        total[:x_cells], system, ROW_ROW, precision=HIGHEST, preferred_element_type=jnp.float32
    )
    core_first[...] = jnp.dot(
        scores, inverse, precision=HIGHEST, preferred_element_type=jnp.float32
    )


def solve_first(x_cells, sums):
    return pl.pallas_call(
        first_kernel,
        out_shape=jax.ShapeDtypeStruct((x_cells, sums[0].shape[0] - x_cells), jnp.float32),
        compiler_params=pltpu.CompilerParams(vmem_limit_bytes=VMEM_BYTES),
        name="solve_first",
    )(*sums)


def place_kernel(outer_order, inner_order, packed, core_last):
    own = packed.shape[3]
    outer, inner = lax.axis_index("gx"), lax.axis_index("gy")
    for n, i in enumerate(inner_order):
        for k, o in enumerate(outer_order):
            at = ((outer ^ o) * len(inner_order) + (inner ^ i)) * own
            for c in range(packed.shape[2]):
                core_last[pl.ds(pl.multiple_of(at, own), own), c * LANES : (c + 1) * LANES] = (
                    packed[n, k, c]
                )


def place(outer_order, inner_order, packed):
    inner, outer, count, own, lanes = packed.shape
    return pl.pallas_call(
        functools.partial(place_kernel, outer_order, inner_order),
        out_shape=jax.ShapeDtypeStruct((inner * outer * own, count * lanes), jnp.float32),
        compiler_params=pltpu.CompilerParams(vmem_limit_bytes=VMEM_BYTES),
        name="place",
    )(packed)


def per_device(flow_field, left_x, last_x, last_y, right_y, right_m, last_m):
    x_cells, y_cells, m_cells = flow_field.shape
    rank = left_x.shape[1]
    cols = right_m.shape[1]
    blocks, shares = lax.axis_size("gx"), lax.axis_size("gz")
    y_share = y_cells // shares
    y_own = y_share // blocks

    last_part, first_part, *terms = local_products(
        shares, flow_field, last_x, last_y, right_y, right_m, last_m
    )

    for s in range(1, shares):
        terms[s] = swap(terms[s], "gz", s)

    group = ("gx", "gy")
    own = rank // lax.axis_size(group)
    last_rows = lax.all_to_all(last_part.reshape(-1, own, m_cells), group, 0, 0, tiled=True)
    last_rows = jnp.sum(last_rows, axis=0)
    both = jnp.dot(
        jnp.concatenate(split_terms(last_rows), axis=0), last_m, preferred_element_type=jnp.float32
    )
    both = both[:own] + both[own:]
    count = lax.axis_size(ALL)
    copies = jnp.broadcast_to(both[None], (count, own, cols))
    system = lax.all_to_all(copies, ALL, 0, 0, tiled=True).reshape(-1, shares, own, cols)
    if own % ROWS:
        system = jnp.sum(system, axis=1).reshape(-1, 1, ROWS, cols)

    first_rows = swap_sum(first_part, "gy")
    packed = jnp.concatenate(
        [
            last_rows.reshape(own, -1, LANES).transpose(1, 0, 2).reshape(-1, LANES),
            first_rows.reshape(x_cells, -1, LANES).transpose(1, 0, 2).reshape(-1, LANES),
            left_x.astype(jnp.float32),
        ],
        axis=0,
    )
    first_at = own * m_cells // LANES
    left_at = first_at + x_cells * cols // LANES
    packed, order, system = swap_gather(packed, "gx", system)
    projected = solve_last(system, terms)
    projected, packed = lax.optimization_barrier((projected, packed))

    pieces = projected.reshape(blocks, y_own, x_cells, rank)
    pieces = lax.all_to_all(pieces, "gx", 0, 0, tiled=True)
    group = ("gx", "gz")
    devices = lax.axis_size(group)
    rank_own = rank // devices
    if rank_own % ROWS:
        middle = sketch(order, left_at, rank, pieces, packed)
        middle = middle.reshape(y_own, devices, rank_own, rank).transpose(1, 0, 2, 3)
    else:
        middle = sketch(order, left_at, rank_own, pieces, packed)
    received = lax.all_to_all(middle, group, 0, 0, tiled=True)
    received = received.reshape(blocks, shares, y_own, rank_own, rank)
    core_middle = received.transpose(3, 1, 0, 2, 4).reshape(rank_own, y_cells, rank)

    if own % ROWS:
        core_last = gather_rows(last_rows, "gx", "gy")
    else:
        core_last = packed[:, :first_at].reshape(blocks, -1, own, LANES)
        core_last, inner_order, _ = swap_gather(core_last, "gy")
        core_last = place(order, inner_order, core_last)

    sums = first_sums(first_at, left_at, first_rows, packed)
    sums = [swap(sums, "gz", z) if z else sums for z in range(shares)]
    core_first = solve_first(x_cells, sums)
    return (core_first, core_middle, core_last)


def solution(mesh):
    return jax.shard_map(
        per_device,
        mesh=mesh,
        in_specs=(
            P("gx", "gy", "gz"),
            P("gx", None),
            P("gx", None),
            P("gy", None),
            P("gy", None),
            P("gz", None),
            P("gz", None),
        ),
        out_specs=(P("gx", None), P(("gx", "gz"), "gy", None), P(None, "gz")),
        check_vma=False,
    )
```

```python
import functools

import jax
import jax.numpy as jnp
from jax import lax
from jax.experimental import pallas as pl
from jax.experimental.pallas import tpu as pltpu
from jax.sharding import PartitionSpec as P

ALL = ("gx", "gy", "gz")
HIGHEST = lax.Precision.HIGHEST
VMEM_BYTES = 48 * 1024 * 1024
LOCAL_VMEM_BYTES = 63 * 1024 * 1024
ROWS = 8
LANES = 128
ROW_ROW = (((1,), (1,)), ((), ()))
COL_COL = (((0,), (0,)), ((), ()))


def axis_bits(axis):
    bit = lax.axis_size(axis) // 2
    while bit:
        yield bit
        bit //= 2


def swap(array, axis, bits):
    return lax.ppermute(array, axis, [(s, s ^ bits) for s in range(lax.axis_size(axis))])


def swap_sum(array, axis):
    for bit in axis_bits(axis):
        array = array + swap(array, axis, bit)
    return array


def after(value, *others):
    value, *_ = lax.optimization_barrier((value, *others))
    return value


def swap_order(axis):
    order = [0]
    for bit in axis_bits(axis):
        order += [o ^ bit for o in order]
    return order


def swap_step(held, axis, bit):
    return jnp.concatenate([held, swap(held, axis, bit)], axis=0)


def swap_gather(array, axis):
    held = array[None]
    for bit in axis_bits(axis):
        held = swap_step(held, axis, bit)
    return held


def gather_rows(array, outer, inner):
    held = array[None, None]
    for dim, axis in ((0, outer), (1, inner)):
        shape = held.shape
        held = held.reshape(*shape[:dim], 1, 1, *shape[dim + 1 :])
        for bit in axis_bits(axis):
            other = swap(held, axis, bit)
            upper = (lax.axis_index(axis) & bit) != 0
            low = jnp.where(upper, other, held)
            high = jnp.where(upper, held, other)
            held = jnp.concatenate([low, high], axis=dim + 1)
            shape = held.shape
            held = held.reshape(*shape[:dim], shape[dim] * shape[dim + 1], 1, *shape[dim + 2 :])
        shape = held.shape
        held = held.reshape(*shape[: dim + 1], *shape[dim + 2 :])
    return held.reshape(-1, array.shape[-1])


def split_terms(array):
    high = lax.reduce_precision(array, 8, 7)
    return high.astype(jnp.bfloat16), (array - high).astype(jnp.bfloat16)


def invert(system):
    size = system.shape[0]
    lanes = lax.broadcasted_iota(jnp.int32, (ROWS, size), 1)
    subs = lax.broadcasted_iota(jnp.int32, (ROWS, size), 0)
    rows = [system[r : r + ROWS] for r in range(0, size, ROWS)]

    def column(block, at):
        return jnp.broadcast_to(block[:, at : at + 1], (ROWS, size))

    for panel in range(size // ROWS):
        first = panel * ROWS
        inside = (lanes >= first) & (lanes < first + ROWS)
        unit = (lanes - first == subs).astype(jnp.float32)
        pivots = [column(rows[panel], first + c) for c in range(ROWS)]
        solved = jnp.where(inside, unit, rows[panel])
        for k in range(ROWS):
            scale = 1.0 / pivots[k][k : k + 1]
            here = subs == k
            top = solved[k : k + 1] * scale
            solved = jnp.where(here, top, solved - pivots[k] * top)
            for c in range(k + 1, ROWS):
                top = pivots[c][k : k + 1] * scale
                pivots[c] = jnp.where(here, top, pivots[c] - pivots[k] * top)
        for r in range(len(rows)):
            if r == panel:
                continue
            old = rows[r]
            new = jnp.where(inside, 0.0, old)
            for c in range(ROWS):
                new = new - column(old, first + c) * solved[c : c + 1]
            rows[r] = new
        rows[panel] = solved
    return jnp.concatenate(rows, axis=0)


def spd_inverse(system):
    square = lax.dot_general(
        system, system, ROW_ROW, precision=HIGHEST, preferred_element_type=jnp.float32
    )
    return invert(square)


def local_kernel(
    chunks,
    shares,
    field_hbm,
    last_x_hbm,
    last_y_hbm,
    right_y_hbm,
    right_m_hbm,
    last_m_hbm,
    last_part,
    first_part,
    *refs,
):
    terms_hbm = refs[:shares]
    field, last_x, last_y, right_y, right_m, last_m, terms, sems, out_sems = refs[shares:]
    x_cells, y_cells, m_cells = field.shape
    step = x_cells // chunks
    y_share = y_cells // shares
    parts = [pl.ds(n * step, step) for n in range(chunks)]
    copies = [
        pltpu.make_async_copy(last_m_hbm, last_m, sems.at[0]),
        pltpu.make_async_copy(field_hbm.at[parts[0]], field.at[parts[0]], sems.at[1]),
        pltpu.make_async_copy(last_x_hbm, last_x, sems.at[2]),
        pltpu.make_async_copy(last_y_hbm, last_y, sems.at[3]),
        pltpu.make_async_copy(right_m_hbm, right_m, sems.at[4]),
        pltpu.make_async_copy(right_y_hbm, right_y, sems.at[5]),
    ]
    for n in range(1, chunks):
        copies.append(
            pltpu.make_async_copy(field_hbm.at[parts[n]], field.at[parts[n]], sems.at[5 + n])
        )
    for copy in copies:
        copy.start()
    here = lax.axis_index("gz")
    leaving = []
    copies[0].wait()
    for n in range(chunks):
        copies[5 + n if n else 1].wait()
        for s in reversed(range(shares)):
            start = pl.multiple_of((here ^ s) * y_share, y_share)
            rows = field[parts[n], pl.ds(start, y_share), :].reshape(step * y_share, m_cells)
            term = jnp.dot(rows, last_m[...], preferred_element_type=jnp.float32)
            terms[s, parts[n]] = term.reshape(step, y_share, -1)
            leaving.append(
                pltpu.make_async_copy(
                    terms.at[s, parts[n]], terms_hbm[s].at[parts[n]], out_sems.at[s, n]
                )
            )
            leaving[-1].start()

    for copy in copies[2:6]:
        copy.wait()
    for n in range(chunks):
        rows = field[parts[n]].reshape(step * y_cells, m_cells)
        left = last_x[parts[n]].astype(jnp.float32)[:, None, :]
        khatri = left * last_y[...].astype(jnp.float32)[None]
        khatri = khatri.astype(jnp.bfloat16).reshape(step * y_cells, -1)
        part = lax.dot_general(khatri, rows, COL_COL, preferred_element_type=jnp.float32)
        if n == 0:
            last_part[...] = part
        else:
            last_part[...] += part
        first = jnp.dot(rows, right_m[...], preferred_element_type=jnp.float32)
        first = first.reshape(step, y_cells, -1) * right_y[...].astype(jnp.float32)[None]
        first_part[parts[n], :] = jnp.sum(first, axis=1)
    for copy in leaving:
        copy.wait()


def local_products(shares, field, last_x, last_y, right_y, right_m, last_m):
    x_cells, y_cells, m_cells = field.shape
    rank, cols = last_x.shape[1], last_m.shape[1]
    chunks = max(x_cells // 8, 1)
    inputs = (field, last_x, last_y, right_y, right_m, last_m)
    dims = (x_cells, y_cells // shares, cols)
    hbm = pl.BlockSpec(memory_space=pltpu.HBM)
    vmem = pl.BlockSpec(memory_space=pltpu.VMEM)
    return pl.pallas_call(
        functools.partial(local_kernel, chunks, shares),
        in_specs=[hbm] * len(inputs),
        out_specs=[vmem, vmem, *([hbm] * shares)],
        out_shape=[
            jax.ShapeDtypeStruct((rank, m_cells), jnp.float32),
            jax.ShapeDtypeStruct((x_cells, cols), jnp.float32),
            *([jax.ShapeDtypeStruct(dims, jnp.float32)] * shares),
        ],
        scratch_shapes=[
            *(pltpu.VMEM(x.shape, x.dtype) for x in inputs),
            pltpu.VMEM((shares, *dims), jnp.float32),
            pltpu.SemaphoreType.DMA((5 + chunks,)),
            pltpu.SemaphoreType.DMA((shares, chunks)),
        ],
        compiler_params=pltpu.CompilerParams(vmem_limit_bytes=LOCAL_VMEM_BYTES),
        name="local_products",
    )(*inputs)


def last_kernel(system_shares, *refs):
    *terms, projected, flat = refs
    system = system_shares[:, 0]
    for k in range(1, system_shares.shape[1]):
        system = system + system_shares[:, k]
    system = system.reshape(-1, system.shape[-1])
    pinv = jnp.dot(
        spd_inverse(system), system, precision=HIGHEST, preferred_element_type=jnp.float32
    )
    total = terms[0][...]
    for term in terms[1:]:
        total = total + term[...]
    flat[...] = lax.dot_general(
        total.reshape(-1, total.shape[-1]),
        pinv,
        ROW_ROW,
        precision=HIGHEST,
        preferred_element_type=jnp.float32,
    )
    y_cells, x_cells, _ = projected.shape
    for j in range(y_cells):
        projected[j] = flat[pl.ds(j, x_cells, stride=y_cells), :]


def solve_last(system_shares, terms):
    rank = system_shares.shape[0] * system_shares.shape[2]
    x_cells, y_cells, _ = terms[0].shape
    return pl.pallas_call(
        last_kernel,
        out_shape=jax.ShapeDtypeStruct((y_cells, x_cells, rank), jnp.float32),
        scratch_shapes=[pltpu.VMEM((x_cells * y_cells, rank), jnp.float32)],
        compiler_params=pltpu.CompilerParams(vmem_limit_bytes=VMEM_BYTES),
        name="solve_last",
    )(system_shares, *terms)


def sketch_kernel(order, left_at, pieces, packed, out):
    me = lax.axis_index("gx")
    blocks, y_own, x_cells, cols = pieces.shape
    weights = jnp.concatenate(
        [packed[k, left_at : left_at + x_cells] for k in range(blocks)], axis=0
    ).astype(jnp.bfloat16)
    for j in range(y_own):
        column = jnp.concatenate([pieces[me ^ o, j] for o in order], axis=0)
        high = column.astype(jnp.bfloat16)
        low = (column - high.astype(jnp.float32)).astype(jnp.bfloat16)
        both = lax.dot_general(
            weights,
            jnp.concatenate([high, low], axis=1),
            COL_COL,
            preferred_element_type=jnp.float32,
        )
        both = both[:, :cols] + both[:, cols:]
        out[:, j] = both.reshape(out.shape[0], out.shape[2], cols)


def sketch(order, left_at, own, pieces, packed):
    y_own, cols = pieces.shape[1], pieces.shape[3]
    rank = packed.shape[2]
    return pl.pallas_call(
        functools.partial(sketch_kernel, order, left_at),
        out_shape=jax.ShapeDtypeStruct((rank // own, y_own, own, cols), jnp.float32),
        compiler_params=pltpu.CompilerParams(vmem_limit_bytes=VMEM_BYTES),
        name="sketch",
    )(pieces, packed)


def first_sums_kernel(left_at, rows, packed, sums):
    x_cells, cols = rows.shape
    blocks = range(packed.shape[0])
    left = jnp.concatenate([packed[k, left_at : left_at + x_cells] for k in blocks], axis=0)
    sums[:x_cells] = rows[...]
    for c in range(cols // LANES):
        at = c * x_cells
        sums[x_cells:, c * LANES : (c + 1) * LANES] = lax.dot_general(
            left,
            jnp.concatenate([packed[k, at : at + x_cells] for k in blocks], axis=0),
            COL_COL,
            precision=HIGHEST,
            preferred_element_type=jnp.float32,
        )


def first_sums(left_at, rows, packed):
    return pl.pallas_call(
        functools.partial(first_sums_kernel, left_at),
        out_shape=jax.ShapeDtypeStruct(
            (rows.shape[0] + packed.shape[2], rows.shape[1]), jnp.float32
        ),
        compiler_params=pltpu.CompilerParams(vmem_limit_bytes=VMEM_BYTES),
        name="first_sums",
    )(rows, packed)


def first_kernel(*refs):
    *sums, core_first = refs
    x_cells = core_first.shape[0]
    total = sums[0][...]
    for other in sums[1:]:
        total = total + other[...]
    system = total[x_cells:]
    inverse = spd_inverse(system)
    scores = lax.dot_general(
        total[:x_cells], system, ROW_ROW, precision=HIGHEST, preferred_element_type=jnp.float32
    )
    core_first[...] = jnp.dot(
        scores, inverse, precision=HIGHEST, preferred_element_type=jnp.float32
    )


def solve_first(x_cells, *sums):
    return pl.pallas_call(
        first_kernel,
        out_shape=jax.ShapeDtypeStruct((x_cells, sums[0].shape[0] - x_cells), jnp.float32),
        compiler_params=pltpu.CompilerParams(vmem_limit_bytes=VMEM_BYTES),
        name="solve_first",
    )(*sums)


def place_kernel(outer_order, inner_order, packed, core_last):
    own = packed.shape[3]
    outer, inner = lax.axis_index("gx"), lax.axis_index("gy")
    for n, i in enumerate(inner_order):
        for k, o in enumerate(outer_order):
            at = ((outer ^ o) * len(inner_order) + (inner ^ i)) * own
            for c in range(packed.shape[2]):
                core_last[pl.ds(pl.multiple_of(at, own), own), c * LANES : (c + 1) * LANES] = (
                    packed[n, k, c]
                )


def place(outer_order, inner_order, packed):
    inner, outer, count, own, lanes = packed.shape
    return pl.pallas_call(
        functools.partial(place_kernel, outer_order, inner_order),
        out_shape=jax.ShapeDtypeStruct((inner * outer * own, count * lanes), jnp.float32),
        compiler_params=pltpu.CompilerParams(vmem_limit_bytes=VMEM_BYTES),
        name="place",
    )(packed)


def per_device(flow_field, left_x, last_x, last_y, right_y, right_m, last_m):
    x_cells, y_cells, m_cells = flow_field.shape
    rank = left_x.shape[1]
    cols = right_m.shape[1]
    blocks, shares = lax.axis_size("gx"), lax.axis_size("gz")
    y_share = y_cells // shares
    y_own = y_share // blocks

    last_part, first_part, *terms = local_products(
        shares, flow_field, last_x, last_y, right_y, right_m, last_m
    )

    for s in range(1, shares):
        terms[s] = swap(terms[s], "gz", s)

    order = swap_order("gx")
    first_rows = swap_sum(first_part, "gy")
    packed = jnp.concatenate(
        [
            first_rows.reshape(x_cells, -1, LANES).transpose(1, 0, 2).reshape(-1, LANES),
            left_x.astype(jnp.float32),
        ],
        axis=0,
    )[None]
    left_at = x_cells * cols // LANES
    first_bit, *bits = axis_bits("gx")
    packed = swap_step(packed, "gx", first_bit)

    group = ("gx", "gy")
    own = rank // lax.axis_size(group)
    last_rows = lax.all_to_all(last_part.reshape(-1, own, m_cells), group, 0, 0, tiled=True)
    last_rows = jnp.sum(last_rows, axis=0)
    both = jnp.dot(
        jnp.concatenate(split_terms(last_rows), axis=0), last_m, preferred_element_type=jnp.float32
    )
    both = after(both[:own] + both[own:], packed)
    count = lax.axis_size(ALL)
    copies = jnp.broadcast_to(both[None], (count, own, cols))
    system = lax.all_to_all(copies, ALL, 0, 0, tiled=True).reshape(-1, shares, own, cols)
    if own % ROWS:
        system = jnp.sum(system, axis=1).reshape(-1, 1, ROWS, cols)

    for bit in bits:
        packed = swap_step(packed, "gx", bit)
    sums = first_sums(left_at, first_rows, packed)
    projected = solve_last(after(system, sums), terms)
    sums = [swap(sums, "gz", z) if z else sums for z in range(shares)]
    projected = after(projected, *sums)

    pieces = projected.reshape(blocks, y_own, x_cells, rank)
    pieces = lax.all_to_all(pieces, "gx", 0, 0, tiled=True)
    group = ("gx", "gz")
    devices = lax.axis_size(group)
    rank_own = rank // devices
    if rank_own % ROWS:
        middle = sketch(order, left_at, rank, pieces, packed)
        middle = middle.reshape(y_own, devices, rank_own, rank).transpose(1, 0, 2, 3)
    else:
        middle = sketch(order, left_at, rank_own, pieces, packed)

    if own % ROWS:
        core_last = gather_rows(last_rows, "gx", "gy")
    else:
        core_last = last_rows.reshape(own, -1, LANES).transpose(1, 0, 2)
        core_last = swap_gather(core_last, "gx")
        middle = after(middle, core_last)
        core_last = swap_gather(core_last, "gy")
        core_last = place(order, swap_order("gy"), core_last)

    received = lax.all_to_all(middle, group, 0, 0, tiled=True)
    received = received.reshape(blocks, shares, y_own, rank_own, rank)
    core_middle = received.transpose(3, 1, 0, 2, 4).reshape(rank_own, y_cells, rank)
    core_first = solve_first(x_cells, after(sums[0], middle), *sums[1:])
    return (core_first, core_middle, core_last)


def solution(mesh):
    return jax.shard_map(
        per_device,
        mesh=mesh,
        in_specs=(
            P("gx", "gy", "gz"),
            P("gx", None),
            P("gx", None),
            P("gy", None),
            P("gy", None),
            P("gz", None),
            P("gz", None),
        ),
        out_specs=(P("gx", None), P(("gx", "gz"), "gy", None), P(None, "gz")),
        check_vma=False,
    )
```

```python
import functools

import jax
import jax.numpy as jnp
from jax import lax
from jax.experimental import pallas as pl
from jax.experimental.pallas import tpu as pltpu
from jax.sharding import PartitionSpec as P

ALL = ("gx", "gy", "gz")
HIGHEST = lax.Precision.HIGHEST
VMEM_BYTES = 48 * 1024 * 1024
LOCAL_VMEM_BYTES = 63 * 1024 * 1024
ROWS = 8
LANES = 128
ROW_ROW = (((1,), (1,)), ((), ()))
COL_COL = (((0,), (0,)), ((), ()))


def axis_bits(axis):
    bit = lax.axis_size(axis) // 2
    while bit:
        yield bit
        bit //= 2


def swap(array, axis, bits):
    return lax.ppermute(array, axis, [(s, s ^ bits) for s in range(lax.axis_size(axis))])


def swap_sum(array, axis):
    for bit in axis_bits(axis):
        array = array + swap(array, axis, bit)
    return array


def after(value, *others):
    value, *_ = lax.optimization_barrier((value, *others))
    return value


def swap_order(axis):
    order = [0]
    for bit in axis_bits(axis):
        order += [o ^ bit for o in order]
    return order


def swap_step(held, axis, bit):
    return jnp.concatenate([held, swap(held, axis, bit)], axis=0)


def gather_rows(array, outer, inner):
    held = array[None, None]
    for dim, axis in ((0, outer), (1, inner)):
        shape = held.shape
        held = held.reshape(*shape[:dim], 1, 1, *shape[dim + 1 :])
        for bit in axis_bits(axis):
            other = swap(held, axis, bit)
            upper = (lax.axis_index(axis) & bit) != 0
            low = jnp.where(upper, other, held)
            high = jnp.where(upper, held, other)
            held = jnp.concatenate([low, high], axis=dim + 1)
            shape = held.shape
            held = held.reshape(*shape[:dim], shape[dim] * shape[dim + 1], 1, *shape[dim + 2 :])
        shape = held.shape
        held = held.reshape(*shape[: dim + 1], *shape[dim + 2 :])
    return held.reshape(-1, array.shape[-1])


def split_terms(array):
    high = lax.reduce_precision(array, 8, 7)
    return high.astype(jnp.bfloat16), (array - high).astype(jnp.bfloat16)


def invert(system):
    size = system.shape[0]
    lanes = lax.broadcasted_iota(jnp.int32, (ROWS, size), 1)
    subs = lax.broadcasted_iota(jnp.int32, (ROWS, size), 0)
    rows = [system[r : r + ROWS] for r in range(0, size, ROWS)]

    def column(block, at):
        return jnp.broadcast_to(block[:, at : at + 1], (ROWS, size))

    for panel in range(size // ROWS):
        first = panel * ROWS
        inside = (lanes >= first) & (lanes < first + ROWS)
        unit = (lanes - first == subs).astype(jnp.float32)
        pivots = [column(rows[panel], first + c) for c in range(ROWS)]
        solved = jnp.where(inside, unit, rows[panel])
        for k in range(ROWS):
            scale = 1.0 / pivots[k][k : k + 1]
            here = subs == k
            top = solved[k : k + 1] * scale
            solved = jnp.where(here, top, solved - pivots[k] * top)
            for c in range(k + 1, ROWS):
                top = pivots[c][k : k + 1] * scale
                pivots[c] = jnp.where(here, top, pivots[c] - pivots[k] * top)
        for r in range(len(rows)):
            if r == panel:
                continue
            old = rows[r]
            new = jnp.where(inside, 0.0, old)
            for c in range(ROWS):
                new = new - column(old, first + c) * solved[c : c + 1]
            rows[r] = new
        rows[panel] = solved
    return jnp.concatenate(rows, axis=0)


def spd_inverse(system):
    square = lax.dot_general(
        system, system, ROW_ROW, precision=HIGHEST, preferred_element_type=jnp.float32
    )
    return invert(square)


def local_kernel(
    chunks,
    shares,
    field_hbm,
    last_x_hbm,
    last_y_hbm,
    right_y_hbm,
    right_m_hbm,
    last_m_hbm,
    last_part,
    first_part,
    *refs,
):
    terms_hbm = refs[:shares]
    field, last_x, last_y, right_y, right_m, last_m, terms, sems, out_sems = refs[shares:]
    x_cells, y_cells, m_cells = field.shape
    step = x_cells // chunks
    y_share = y_cells // shares
    parts = [pl.ds(n * step, step) for n in range(chunks)]
    copies = [
        pltpu.make_async_copy(last_m_hbm, last_m, sems.at[0]),
        pltpu.make_async_copy(field_hbm.at[parts[0]], field.at[parts[0]], sems.at[1]),
        pltpu.make_async_copy(last_x_hbm, last_x, sems.at[2]),
        pltpu.make_async_copy(last_y_hbm, last_y, sems.at[3]),
        pltpu.make_async_copy(right_m_hbm, right_m, sems.at[4]),
        pltpu.make_async_copy(right_y_hbm, right_y, sems.at[5]),
    ]
    for n in range(1, chunks):
        copies.append(
            pltpu.make_async_copy(field_hbm.at[parts[n]], field.at[parts[n]], sems.at[5 + n])
        )
    for copy in copies:
        copy.start()
    here = lax.axis_index("gz")
    leaving = []
    copies[0].wait()
    for n in range(chunks):
        copies[5 + n if n else 1].wait()
        for s in reversed(range(shares)):
            start = pl.multiple_of((here ^ s) * y_share, y_share)
            rows = field[parts[n], pl.ds(start, y_share), :].reshape(step * y_share, m_cells)
            term = jnp.dot(rows, last_m[...], preferred_element_type=jnp.float32)
            terms[s, parts[n]] = term.reshape(step, y_share, -1)
            leaving.append(
                pltpu.make_async_copy(
                    terms.at[s, parts[n]], terms_hbm[s].at[parts[n]], out_sems.at[s, n]
                )
            )
            leaving[-1].start()

    for copy in copies[2:6]:
        copy.wait()
    for n in range(chunks):
        rows = field[parts[n]].reshape(step * y_cells, m_cells)
        left = last_x[parts[n]].astype(jnp.float32)[:, None, :]
        khatri = left * last_y[...].astype(jnp.float32)[None]
        khatri = khatri.astype(jnp.bfloat16).reshape(step * y_cells, -1)
        part = lax.dot_general(khatri, rows, COL_COL, preferred_element_type=jnp.float32)
        if n == 0:
            last_part[...] = part
        else:
            last_part[...] += part
        first = jnp.dot(rows, right_m[...], preferred_element_type=jnp.float32)
        first = first.reshape(step, y_cells, -1) * right_y[...].astype(jnp.float32)[None]
        first_part[parts[n], :] = jnp.sum(first, axis=1)
    for copy in leaving:
        copy.wait()


def local_products(shares, field, last_x, last_y, right_y, right_m, last_m):
    x_cells, y_cells, m_cells = field.shape
    rank, cols = last_x.shape[1], last_m.shape[1]
    chunks = max(x_cells // 8, 1)
    inputs = (field, last_x, last_y, right_y, right_m, last_m)
    dims = (x_cells, y_cells // shares, cols)
    hbm = pl.BlockSpec(memory_space=pltpu.HBM)
    vmem = pl.BlockSpec(memory_space=pltpu.VMEM)
    return pl.pallas_call(
        functools.partial(local_kernel, chunks, shares),
        in_specs=[hbm] * len(inputs),
        out_specs=[vmem, vmem, *([hbm] * shares)],
        out_shape=[
            jax.ShapeDtypeStruct((rank, m_cells), jnp.float32),
            jax.ShapeDtypeStruct((x_cells, cols), jnp.float32),
            *([jax.ShapeDtypeStruct(dims, jnp.float32)] * shares),
        ],
        scratch_shapes=[
            *(pltpu.VMEM(x.shape, x.dtype) for x in inputs),
            pltpu.VMEM((shares, *dims), jnp.float32),
            pltpu.SemaphoreType.DMA((5 + chunks,)),
            pltpu.SemaphoreType.DMA((shares, chunks)),
        ],
        compiler_params=pltpu.CompilerParams(vmem_limit_bytes=LOCAL_VMEM_BYTES),
        name="local_products",
    )(*inputs)


def last_kernel(y_own, system_shares, *refs):
    extra, *terms, projected, flat = refs
    system = system_shares[:, 0]
    for k in range(1, system_shares.shape[1]):
        system = system + system_shares[:, k]
    system = system.reshape(-1, system.shape[-1])
    pinv = jnp.dot(
        spd_inverse(system), system, precision=HIGHEST, preferred_element_type=jnp.float32
    )
    total = terms[0][...]
    for term in terms[1:]:
        total = total + term[...]
    flat[...] = lax.dot_general(
        total.reshape(-1, total.shape[-1]),
        pinv,
        ROW_ROW,
        precision=HIGHEST,
        preferred_element_type=jnp.float32,
    )
    x_cells, y_cells, _ = terms[0].shape
    for b in range(projected.shape[0]):
        for j in range(y_own):
            projected[b, j * x_cells : (j + 1) * x_cells] = flat[
                pl.ds(b * y_own + j, x_cells, stride=y_cells), :
            ]
        projected[b, y_own * x_cells :] = extra[...]


def solve_last(blocks, system_shares, extra, terms):
    rank = system_shares.shape[0] * system_shares.shape[2]
    x_cells, y_cells, _ = terms[0].shape
    y_own = y_cells // blocks
    rows = y_own * x_cells + extra.shape[0]
    return pl.pallas_call(
        functools.partial(last_kernel, y_own),
        out_shape=jax.ShapeDtypeStruct((blocks, rows, rank), jnp.float32),
        scratch_shapes=[pltpu.VMEM((x_cells * y_cells, rank), jnp.float32)],
        compiler_params=pltpu.CompilerParams(vmem_limit_bytes=VMEM_BYTES),
        name="solve_last",
    )(system_shares, extra, *terms)


def sketch_kernel(order, left_at, y_own, pieces, packed, out, extra):
    me = lax.axis_index("gx")
    blocks, _, cols = pieces.shape
    x_cells = packed.shape[1] - left_at
    weights = jnp.concatenate([packed[k, left_at:] for k in range(blocks)], axis=0)
    weights = weights.astype(jnp.bfloat16)
    for j in range(y_own):
        column = jnp.concatenate(
            [pieces[me ^ o, j * x_cells : (j + 1) * x_cells] for o in order], axis=0
        )
        high = column.astype(jnp.bfloat16)
        low = (column - high.astype(jnp.float32)).astype(jnp.bfloat16)
        both = lax.dot_general(
            weights,
            jnp.concatenate([high, low], axis=1),
            COL_COL,
            preferred_element_type=jnp.float32,
        )
        both = both[:, :cols] + both[:, cols:]
        out[:, j] = both.reshape(out.shape[0], out.shape[2], cols)
    extra[...] = pieces[:, y_own * x_cells :]


def sketch(order, left_at, y_own, own, pieces, packed):
    blocks, rows, cols = pieces.shape
    rank = packed.shape[2]
    extra = rows - y_own * (packed.shape[1] - left_at)
    return pl.pallas_call(
        functools.partial(sketch_kernel, order, left_at, y_own),
        out_shape=(
            jax.ShapeDtypeStruct((rank // own, y_own, own, cols), jnp.float32),
            jax.ShapeDtypeStruct((blocks, extra, cols), jnp.float32),
        ),
        compiler_params=pltpu.CompilerParams(vmem_limit_bytes=VMEM_BYTES),
        name="sketch",
    )(pieces, packed)


def first_sums_kernel(left_at, rows, packed, sums):
    x_cells, cols = rows.shape
    blocks = range(packed.shape[0])
    left = jnp.concatenate([packed[k, left_at : left_at + x_cells] for k in blocks], axis=0)
    sums[:x_cells] = rows[...]
    for c in range(cols // LANES):
        at = c * x_cells
        sums[x_cells:, c * LANES : (c + 1) * LANES] = lax.dot_general(
            left,
            jnp.concatenate([packed[k, at : at + x_cells] for k in blocks], axis=0),
            COL_COL,
            precision=HIGHEST,
            preferred_element_type=jnp.float32,
        )


def first_sums(left_at, rows, packed):
    return pl.pallas_call(
        functools.partial(first_sums_kernel, left_at),
        out_shape=jax.ShapeDtypeStruct(
            (rows.shape[0] + packed.shape[2], rows.shape[1]), jnp.float32
        ),
        compiler_params=pltpu.CompilerParams(vmem_limit_bytes=VMEM_BYTES),
        name="first_sums",
    )(rows, packed)


def first_kernel(*refs):
    *sums, core_first = refs
    x_cells = core_first.shape[0]
    total = sums[0][...]
    for other in sums[1:]:
        total = total + other[...]
    system = total[x_cells:]
    inverse = spd_inverse(system)
    scores = lax.dot_general(
        total[:x_cells], system, ROW_ROW, precision=HIGHEST, preferred_element_type=jnp.float32
    )
    core_first[...] = jnp.dot(
        scores, inverse, precision=HIGHEST, preferred_element_type=jnp.float32
    )


def solve_first(x_cells, *sums):
    return pl.pallas_call(
        first_kernel,
        out_shape=jax.ShapeDtypeStruct((x_cells, sums[0].shape[0] - x_cells), jnp.float32),
        compiler_params=pltpu.CompilerParams(vmem_limit_bytes=VMEM_BYTES),
        name="solve_first",
    )(*sums)


def place_kernel(own, inner_order, *refs):
    *parts, core_last = refs
    inner = lax.axis_index("gy")
    for part, i in zip(parts, inner_order):
        for o in range(part.shape[0]):
            at = pl.multiple_of((o * len(parts) + (inner ^ i)) * own, own)
            for c in range(part.shape[1] // own):
                core_last[pl.ds(at, own), c * LANES : (c + 1) * LANES] = part[
                    o, c * own : (c + 1) * own
                ]


def place(own, inner_order, parts):
    outer, rows, lanes = parts[0].shape
    return pl.pallas_call(
        functools.partial(place_kernel, own, inner_order),
        out_shape=jax.ShapeDtypeStruct(
            (len(parts) * outer * own, rows // own * lanes), jnp.float32
        ),
        compiler_params=pltpu.CompilerParams(vmem_limit_bytes=VMEM_BYTES),
        name="place",
    )(*parts)


def per_device(flow_field, left_x, last_x, last_y, right_y, right_m, last_m):
    x_cells, y_cells, m_cells = flow_field.shape
    rank = left_x.shape[1]
    cols = right_m.shape[1]
    blocks, shares = lax.axis_size("gx"), lax.axis_size("gz")
    y_share = y_cells // shares
    y_own = y_share // blocks

    last_part, first_part, *terms = local_products(
        shares, flow_field, last_x, last_y, right_y, right_m, last_m
    )

    for s in range(1, shares):
        terms[s] = swap(terms[s], "gz", s)

    order = swap_order("gx")
    first_rows = swap_sum(first_part, "gy")
    packed = jnp.concatenate(
        [
            first_rows.reshape(x_cells, -1, LANES).transpose(1, 0, 2).reshape(-1, LANES),
            left_x.astype(jnp.float32),
        ],
        axis=0,
    )[None]
    left_at = x_cells * cols // LANES
    first_bit, *bits = axis_bits("gx")
    packed = swap_step(packed, "gx", first_bit)

    group = ("gx", "gy")
    own = rank // lax.axis_size(group)
    last_rows = lax.all_to_all(last_part.reshape(-1, own, m_cells), group, 0, 0, tiled=True)
    last_rows = jnp.sum(last_rows, axis=0)
    both = jnp.dot(
        jnp.concatenate(split_terms(last_rows), axis=0), last_m, preferred_element_type=jnp.float32
    )
    both = after(both[:own] + both[own:], packed)
    count = lax.axis_size(ALL)
    copies = jnp.broadcast_to(both[None], (count, own, cols))
    system = lax.all_to_all(copies, ALL, 0, 0, tiled=True).reshape(-1, shares, own, cols)
    if own % ROWS:
        system = jnp.sum(system, axis=1).reshape(-1, 1, ROWS, cols)

    for bit in bits:
        if bit == bits[-1]:
            packed = after(packed, *terms[1:])
        packed = swap_step(packed, "gx", bit)
    sums = first_sums(left_at, first_rows, packed)
    if own % ROWS:
        extra = jnp.zeros((ROWS, LANES), jnp.float32)
    else:
        extra = last_rows.reshape(own, -1, LANES).transpose(1, 0, 2).reshape(-1, LANES)
    projected = solve_last(blocks, after(system, sums), extra, terms)
    sums = [swap(sums, "gz", z) if z else sums for z in range(shares)]
    projected = after(projected, *sums)

    pieces = lax.all_to_all(projected, "gx", 0, 0, tiled=True)
    core_first = solve_first(x_cells, after(sums[0], projected), *sums[1:])
    group = ("gx", "gz")
    devices = lax.axis_size(group)
    rank_own = rank // devices
    if rank_own % ROWS:
        middle, extra = sketch(order, left_at, y_own, rank, pieces, packed)
        middle = middle.reshape(y_own, devices, rank_own, rank).transpose(1, 0, 2, 3)
    else:
        middle, extra = sketch(order, left_at, y_own, rank_own, pieces, packed)
    middle, core_first = lax.optimization_barrier((middle, core_first))
    received = lax.all_to_all(middle, group, 0, 0, tiled=True)
    received = received.reshape(blocks, shares, y_own, rank_own, rank)
    core_middle = received.transpose(3, 1, 0, 2, 4).reshape(rank_own, y_cells, rank)

    if own % ROWS:
        core_last = gather_rows(last_rows, "gx", "gy")
    else:
        inner = range(lax.axis_size("gy"))
        core_last = place(own, inner, [swap(extra, "gy", i) if i else extra for i in inner])
    return (core_first, core_middle, core_last)


def solution(mesh):
    return jax.shard_map(
        per_device,
        mesh=mesh,
        in_specs=(
            P("gx", "gy", "gz"),
            P("gx", None),
            P("gx", None),
            P("gy", None),
            P("gy", None),
            P("gz", None),
            P("gz", None),
        ),
        out_specs=(P("gx", None), P(("gx", "gz"), "gy", None), P(None, "gz")),
        check_vma=False,
    )
```

```python
import functools

import jax
import jax.numpy as jnp
from jax import lax
from jax.experimental import pallas as pl
from jax.experimental.pallas import tpu as pltpu
from jax.sharding import PartitionSpec as P

ALL = ("gx", "gy", "gz")
HIGHEST = lax.Precision.HIGHEST
VMEM_BYTES = 48 * 1024 * 1024
LOCAL_VMEM_BYTES = 63 * 1024 * 1024
ROWS = 8
LANES = 128
PARTS = 2
ROW_ROW = (((1,), (1,)), ((), ()))
COL_COL = (((0,), (0,)), ((), ()))


def axis_bits(axis):
    bit = lax.axis_size(axis) // 2
    while bit:
        yield bit
        bit //= 2


def swap(array, axis, bits):
    return lax.ppermute(array, axis, [(s, s ^ bits) for s in range(lax.axis_size(axis))])


def swap_sum(array, axis):
    for bit in axis_bits(axis):
        array = array + swap(array, axis, bit)
    return array


def after(value, *others):
    value, *_ = lax.optimization_barrier((value, *others))
    return value


def swap_order(axis):
    order = [0]
    for bit in axis_bits(axis):
        order += [o ^ bit for o in order]
    return order


def swap_step(held, axis, bit):
    return jnp.concatenate([held, swap(held, axis, bit)], axis=0)


def gather_rows(array, outer, inner):
    held = array[None, None]
    for dim, axis in ((0, outer), (1, inner)):
        shape = held.shape
        held = held.reshape(*shape[:dim], 1, 1, *shape[dim + 1 :])
        for bit in axis_bits(axis):
            other = swap(held, axis, bit)
            upper = (lax.axis_index(axis) & bit) != 0
            low = jnp.where(upper, other, held)
            high = jnp.where(upper, held, other)
            held = jnp.concatenate([low, high], axis=dim + 1)
            shape = held.shape
            held = held.reshape(*shape[:dim], shape[dim] * shape[dim + 1], 1, *shape[dim + 2 :])
        shape = held.shape
        held = held.reshape(*shape[: dim + 1], *shape[dim + 2 :])
    return held.reshape(-1, array.shape[-1])


def split_terms(array):
    high = lax.reduce_precision(array, 8, 7)
    return high.astype(jnp.bfloat16), (array - high).astype(jnp.bfloat16)


def invert(system):
    size = system.shape[0]
    lanes = lax.broadcasted_iota(jnp.int32, (ROWS, size), 1)
    subs = lax.broadcasted_iota(jnp.int32, (ROWS, size), 0)
    rows = [system[r : r + ROWS] for r in range(0, size, ROWS)]

    def column(block, at):
        return jnp.broadcast_to(block[:, at : at + 1], (ROWS, size))

    for panel in range(size // ROWS):
        first = panel * ROWS
        inside = (lanes >= first) & (lanes < first + ROWS)
        unit = (lanes - first == subs).astype(jnp.float32)
        pivots = [column(rows[panel], first + c) for c in range(ROWS)]
        solved = jnp.where(inside, unit, rows[panel])
        for k in range(ROWS):
            scale = 1.0 / pivots[k][k : k + 1]
            here = subs == k
            top = solved[k : k + 1] * scale
            solved = jnp.where(here, top, solved - pivots[k] * top)
            for c in range(k + 1, ROWS):
                top = pivots[c][k : k + 1] * scale
                pivots[c] = jnp.where(here, top, pivots[c] - pivots[k] * top)
        for r in range(len(rows)):
            if r == panel:
                continue
            old = rows[r]
            new = jnp.where(inside, 0.0, old)
            for c in range(ROWS):
                new = new - column(old, first + c) * solved[c : c + 1]
            rows[r] = new
        rows[panel] = solved
    return jnp.concatenate(rows, axis=0)


def spd_inverse(system):
    square = lax.dot_general(
        system, system, ROW_ROW, precision=HIGHEST, preferred_element_type=jnp.float32
    )
    return invert(square)


def local_kernel(
    chunks,
    shares,
    field_hbm,
    last_x_hbm,
    last_y_hbm,
    right_y_hbm,
    right_m_hbm,
    last_m_hbm,
    last_part,
    first_part,
    *refs,
):
    terms_hbm = refs[: shares * PARTS]
    field, last_x, last_y, right_y, right_m, last_m, terms, sems, out_sems = refs[shares * PARTS :]
    x_cells, y_cells, m_cells = field.shape
    step = x_cells // chunks
    y_share = y_cells // shares
    parts = [pl.ds(n * step, step) for n in range(chunks)]
    copies = [
        pltpu.make_async_copy(last_m_hbm, last_m, sems.at[0]),
        pltpu.make_async_copy(field_hbm.at[parts[0]], field.at[parts[0]], sems.at[1]),
        pltpu.make_async_copy(last_x_hbm, last_x, sems.at[2]),
        pltpu.make_async_copy(last_y_hbm, last_y, sems.at[3]),
        pltpu.make_async_copy(right_m_hbm, right_m, sems.at[4]),
        pltpu.make_async_copy(right_y_hbm, right_y, sems.at[5]),
    ]
    for n in range(1, chunks):
        copies.append(
            pltpu.make_async_copy(field_hbm.at[parts[n]], field.at[parts[n]], sems.at[5 + n])
        )
    for copy in copies:
        copy.start()
    here = lax.axis_index("gz")
    leaving = []
    copies[0].wait()
    for n in range(chunks):
        copies[5 + n if n else 1].wait()
        for s in reversed(range(shares)):
            start = pl.multiple_of((here ^ s) * y_share, y_share)
            rows = field[parts[n], pl.ds(start, y_share), :].reshape(step * y_share, m_cells)
            term = jnp.dot(rows, last_m[...], preferred_element_type=jnp.float32)
            terms[s, parts[n]] = term.reshape(step, y_share, -1)
            part, at = divmod(n * step, x_cells // PARTS)
            leaving.append(
                pltpu.make_async_copy(
                    terms.at[s, parts[n]],
                    terms_hbm[s * PARTS + part].at[pl.ds(at, step)],
                    out_sems.at[s, n],
                )
            )
            leaving[-1].start()

    for copy in copies[2:6]:
        copy.wait()
    for n in range(chunks):
        rows = field[parts[n]].reshape(step * y_cells, m_cells)
        left = last_x[parts[n]].astype(jnp.float32)[:, None, :]
        khatri = left * last_y[...].astype(jnp.float32)[None]
        khatri = khatri.astype(jnp.bfloat16).reshape(step * y_cells, -1)
        part = lax.dot_general(khatri, rows, COL_COL, preferred_element_type=jnp.float32)
        if n == 0:
            last_part[...] = part
        else:
            last_part[...] += part
        first = jnp.dot(rows, right_m[...], preferred_element_type=jnp.float32)
        first = first.reshape(step, y_cells, -1) * right_y[...].astype(jnp.float32)[None]
        first_part[parts[n], :] = jnp.sum(first, axis=1)
    for copy in leaving:
        copy.wait()


def local_products(shares, field, last_x, last_y, right_y, right_m, last_m):
    x_cells, y_cells, m_cells = field.shape
    rank, cols = last_x.shape[1], last_m.shape[1]
    chunks = max(x_cells // 8, 1)
    inputs = (field, last_x, last_y, right_y, right_m, last_m)
    dims = (x_cells, y_cells // shares, cols)
    part_dims = (x_cells // PARTS, *dims[1:])
    hbm = pl.BlockSpec(memory_space=pltpu.HBM)
    vmem = pl.BlockSpec(memory_space=pltpu.VMEM)
    return pl.pallas_call(
        functools.partial(local_kernel, chunks, shares),
        in_specs=[hbm] * len(inputs),
        out_specs=[vmem, vmem, *([hbm] * (shares * PARTS))],
        out_shape=[
            jax.ShapeDtypeStruct((rank, m_cells), jnp.float32),
            jax.ShapeDtypeStruct((x_cells, cols), jnp.float32),
            *([jax.ShapeDtypeStruct(part_dims, jnp.float32)] * (shares * PARTS)),
        ],
        scratch_shapes=[
            *(pltpu.VMEM(x.shape, x.dtype) for x in inputs),
            pltpu.VMEM((shares, *dims), jnp.float32),
            pltpu.SemaphoreType.DMA((5 + chunks,)),
            pltpu.SemaphoreType.DMA((shares, chunks)),
        ],
        compiler_params=pltpu.CompilerParams(vmem_limit_bytes=LOCAL_VMEM_BYTES),
        name="local_products",
    )(*inputs)


def inverse_kernel(system_shares, pinv):
    system = system_shares[:, 0]
    for k in range(1, system_shares.shape[1]):
        system = system + system_shares[:, k]
    system = system.reshape(-1, system.shape[-1])
    pinv[...] = jnp.dot(
        spd_inverse(system), system, precision=HIGHEST, preferred_element_type=jnp.float32
    )


def pseudo_inverse(system_shares):
    rank = system_shares.shape[0] * system_shares.shape[2]
    return pl.pallas_call(
        inverse_kernel,
        out_shape=jax.ShapeDtypeStruct((rank, system_shares.shape[3]), jnp.float32),
        compiler_params=pltpu.CompilerParams(vmem_limit_bytes=VMEM_BYTES),
        name="pseudo_inverse",
    )(system_shares)


def two_terms(array):
    high = array.astype(jnp.bfloat16)
    return high, (array - high.astype(jnp.float32)).astype(jnp.bfloat16)


def project_kernel(y_own, pinv, extra, *refs):
    *terms, projected, flat = refs
    rank = pinv.shape[0]
    pinv_high, pinv_low = two_terms(pinv[...])
    pinv_both = jnp.concatenate([pinv_high, pinv_low], axis=0)
    rows = flat.shape[0] // PARTS
    for part in range(PARTS):
        total = terms[part][...]
        for term in terms[part + PARTS :: PARTS]:
            total = total + term[...]
        high, low = two_terms(total.reshape(rows, -1))
        both = lax.dot_general(high, pinv_both, ROW_ROW, preferred_element_type=jnp.float32)
        rest = lax.dot_general(low, pinv_high, ROW_ROW, preferred_element_type=jnp.float32)
        flat[part * rows : (part + 1) * rows] = both[:, :rank] + (both[:, rank:] + rest)
    x_cells, y_cells, _ = terms[0].shape
    x_cells *= PARTS
    for b in range(projected.shape[0]):
        for j in range(y_own):
            projected[b, j * x_cells : (j + 1) * x_cells] = flat[
                pl.ds(b * y_own + j, x_cells, stride=y_cells), :
            ]
        projected[b, y_own * x_cells :] = extra[...]


def project(blocks, pinv, extra, terms):
    rank = pinv.shape[0]
    x_cells, y_cells, _ = terms[0].shape
    x_cells *= PARTS
    y_own = y_cells // blocks
    rows = y_own * x_cells + extra.shape[0]
    return pl.pallas_call(
        functools.partial(project_kernel, y_own),
        out_shape=jax.ShapeDtypeStruct((blocks, rows, rank), jnp.float32),
        scratch_shapes=[pltpu.VMEM((x_cells * y_cells, rank), jnp.float32)],
        compiler_params=pltpu.CompilerParams(vmem_limit_bytes=VMEM_BYTES),
        name="project",
    )(pinv, extra, *terms)


def sketch_kernel(order, left_at, y_own, pieces, packed, out, extra):
    me = lax.axis_index("gx")
    blocks, _, cols = pieces.shape
    x_cells = packed.shape[1] - left_at
    weights = jnp.concatenate([packed[k, left_at:] for k in range(blocks)], axis=0)
    weights = weights.astype(jnp.bfloat16)
    for j in range(y_own):
        column = jnp.concatenate(
            [pieces[me ^ o, j * x_cells : (j + 1) * x_cells] for o in order], axis=0
        )
        high = column.astype(jnp.bfloat16)
        low = (column - high.astype(jnp.float32)).astype(jnp.bfloat16)
        both = lax.dot_general(
            weights,
            jnp.concatenate([high, low], axis=1),
            COL_COL,
            preferred_element_type=jnp.float32,
        )
        both = both[:, :cols] + both[:, cols:]
        out[:, j] = both.reshape(out.shape[0], out.shape[2], cols)
    extra[...] = pieces[:, y_own * x_cells :]


def sketch(order, left_at, y_own, own, pieces, packed):
    blocks, rows, cols = pieces.shape
    rank = packed.shape[2]
    extra = rows - y_own * (packed.shape[1] - left_at)
    return pl.pallas_call(
        functools.partial(sketch_kernel, order, left_at, y_own),
        out_shape=(
            jax.ShapeDtypeStruct((rank // own, y_own, own, cols), jnp.float32),
            jax.ShapeDtypeStruct((blocks, extra, cols), jnp.float32),
        ),
        compiler_params=pltpu.CompilerParams(vmem_limit_bytes=VMEM_BYTES),
        name="sketch",
    )(pieces, packed)


def first_sums_kernel(left_at, rows, packed, sums):
    x_cells, cols = rows.shape
    blocks = range(packed.shape[0])
    left = jnp.concatenate([packed[k, left_at : left_at + x_cells] for k in blocks], axis=0)
    sums[:x_cells] = rows[...]
    for c in range(cols // LANES):
        at = c * x_cells
        sums[x_cells:, c * LANES : (c + 1) * LANES] = lax.dot_general(
            left,
            jnp.concatenate([packed[k, at : at + x_cells] for k in blocks], axis=0),
            COL_COL,
            precision=HIGHEST,
            preferred_element_type=jnp.float32,
        )


def first_sums(left_at, rows, packed):
    return pl.pallas_call(
        functools.partial(first_sums_kernel, left_at),
        out_shape=jax.ShapeDtypeStruct(
            (rows.shape[0] + packed.shape[2], rows.shape[1]), jnp.float32
        ),
        compiler_params=pltpu.CompilerParams(vmem_limit_bytes=VMEM_BYTES),
        name="first_sums",
    )(rows, packed)


def first_kernel(*refs):
    *sums, core_first = refs
    x_cells = core_first.shape[0]
    total = sums[0][...]
    for other in sums[1:]:
        total = total + other[...]
    system = total[x_cells:]
    inverse = spd_inverse(system)
    scores = lax.dot_general(
        total[:x_cells], system, ROW_ROW, precision=HIGHEST, preferred_element_type=jnp.float32
    )
    core_first[...] = jnp.dot(
        scores, inverse, precision=HIGHEST, preferred_element_type=jnp.float32
    )


def solve_first(x_cells, *sums):
    return pl.pallas_call(
        first_kernel,
        out_shape=jax.ShapeDtypeStruct((x_cells, sums[0].shape[0] - x_cells), jnp.float32),
        compiler_params=pltpu.CompilerParams(vmem_limit_bytes=VMEM_BYTES),
        name="solve_first",
    )(*sums)


def place_kernel(own, inner_order, *refs):
    *parts, core_last = refs
    inner = lax.axis_index("gy")
    for part, i in zip(parts, inner_order):
        for o in range(part.shape[0]):
            at = pl.multiple_of((o * len(parts) + (inner ^ i)) * own, own)
            for c in range(part.shape[1] // own):
                core_last[pl.ds(at, own), c * LANES : (c + 1) * LANES] = part[
                    o, c * own : (c + 1) * own
                ]


def place(own, inner_order, parts):
    outer, rows, lanes = parts[0].shape
    return pl.pallas_call(
        functools.partial(place_kernel, own, inner_order),
        out_shape=jax.ShapeDtypeStruct(
            (len(parts) * outer * own, rows // own * lanes), jnp.float32
        ),
        compiler_params=pltpu.CompilerParams(vmem_limit_bytes=VMEM_BYTES),
        name="place",
    )(*parts)


def per_device(flow_field, left_x, last_x, last_y, right_y, right_m, last_m):
    x_cells, y_cells, m_cells = flow_field.shape
    rank = left_x.shape[1]
    cols = right_m.shape[1]
    blocks, shares = lax.axis_size("gx"), lax.axis_size("gz")
    y_share = y_cells // shares
    y_own = y_share // blocks

    last_part, first_part, *terms = local_products(
        shares, flow_field, last_x, last_y, right_y, right_m, last_m
    )

    for s in range(1, shares):
        terms[s * PARTS] = swap(terms[s * PARTS], "gz", s)

    order = swap_order("gx")
    first_rows = swap_sum(first_part, "gy")
    packed = jnp.concatenate(
        [
            first_rows.reshape(x_cells, -1, LANES).transpose(1, 0, 2).reshape(-1, LANES),
            left_x.astype(jnp.float32),
        ],
        axis=0,
    )[None]
    left_at = x_cells * cols // LANES
    first_bit, *bits = axis_bits("gx")
    packed = swap_step(packed, "gx", first_bit)

    group = ("gx", "gy")
    own = rank // lax.axis_size(group)
    last_rows = lax.all_to_all(last_part.reshape(-1, own, m_cells), group, 0, 0, tiled=True)
    last_rows = jnp.sum(last_rows, axis=0)
    both = jnp.dot(
        jnp.concatenate(split_terms(last_rows), axis=0), last_m, preferred_element_type=jnp.float32
    )
    both = after(both[:own] + both[own:], packed)
    count = lax.axis_size(ALL)
    copies = jnp.broadcast_to(both[None], (count, own, cols))
    for s in range(1, shares):
        for part in range(1, PARTS):
            at = s * PARTS + part
            terms[at] = swap(after(terms[at], copies), "gz", s)
    system = lax.all_to_all(copies, ALL, 0, 0, tiled=True).reshape(-1, shares, own, cols)
    if own % ROWS:
        system = jnp.sum(system, axis=1).reshape(-1, 1, ROWS, cols)

    for bit in bits:
        packed = swap_step(packed, "gx", bit)
    sums = first_sums(left_at, first_rows, packed)
    if own % ROWS:
        extra = jnp.zeros((ROWS, LANES), jnp.float32)
    else:
        extra = last_rows.reshape(own, -1, LANES).transpose(1, 0, 2).reshape(-1, LANES)
    pinv = pseudo_inverse(after(system, packed))
    projected = project(blocks, pinv, extra, terms)
    sums = [swap(sums, "gz", z) if z else sums for z in range(shares)]

    pieces = lax.all_to_all(projected, "gx", 0, 0, tiled=True)
    core_first = solve_first(x_cells, after(sums[0], projected), *sums[1:])
    group = ("gx", "gz")
    devices = lax.axis_size(group)
    rank_own = rank // devices
    if rank_own % ROWS:
        middle, extra = sketch(order, left_at, y_own, rank, pieces, packed)
        middle = middle.reshape(y_own, devices, rank_own, rank).transpose(1, 0, 2, 3)
    else:
        middle, extra = sketch(order, left_at, y_own, rank_own, pieces, packed)
    middle, core_first = lax.optimization_barrier((middle, core_first))
    received = lax.all_to_all(middle, group, 0, 0, tiled=True)
    received = received.reshape(blocks, shares, y_own, rank_own, rank)
    core_middle = received.transpose(3, 1, 0, 2, 4).reshape(rank_own, y_cells, rank)

    if own % ROWS:
        core_last = gather_rows(last_rows, "gx", "gy")
    else:
        inner = range(lax.axis_size("gy"))
        core_last = place(own, inner, [swap(extra, "gy", i) if i else extra for i in inner])
    return (core_first, core_middle, core_last)


def solution(mesh):
    return jax.shard_map(
        per_device,
        mesh=mesh,
        in_specs=(
            P("gx", "gy", "gz"),
            P("gx", None),
            P("gx", None),
            P("gy", None),
            P("gy", None),
            P("gz", None),
            P("gz", None),
        ),
        out_specs=(P("gx", None), P(("gx", "gz"), "gy", None), P(None, "gz")),
        check_vma=False,
    )
```

```python
import functools

import jax
import jax.numpy as jnp
from jax import lax
from jax.experimental import pallas as pl
from jax.experimental.pallas import tpu as pltpu
from jax.sharding import PartitionSpec as P

ALL = ("gx", "gy", "gz")
HIGHEST = lax.Precision.HIGHEST
VMEM_BYTES = 48 * 1024 * 1024
LOCAL_VMEM_BYTES = 63 * 1024 * 1024
ROWS = 8
LANES = 128
PARTS = 2
ROW_ROW = (((1,), (1,)), ((), ()))
COL_COL = (((0,), (0,)), ((), ()))


def axis_bits(axis):
    bit = lax.axis_size(axis) // 2
    while bit:
        yield bit
        bit //= 2


def swap(array, axis, bits):
    return lax.ppermute(array, axis, [(s, s ^ bits) for s in range(lax.axis_size(axis))])


def swap_sum(array, axis):
    for bit in axis_bits(axis):
        array = array + swap(array, axis, bit)
    return array


def after(value, *others):
    value, *_ = lax.optimization_barrier((value, *others))
    return value


def swap_order(axis):
    order = [0]
    for bit in axis_bits(axis):
        order += [o ^ bit for o in order]
    return order


def swap_step(held, axis, bit):
    return jnp.concatenate([held, swap(held, axis, bit)], axis=0)


def gather_rows(array, outer, inner):
    held = array[None, None]
    for dim, axis in ((0, outer), (1, inner)):
        shape = held.shape
        held = held.reshape(*shape[:dim], 1, 1, *shape[dim + 1 :])
        for bit in axis_bits(axis):
            other = swap(held, axis, bit)
            upper = (lax.axis_index(axis) & bit) != 0
            low = jnp.where(upper, other, held)
            high = jnp.where(upper, held, other)
            held = jnp.concatenate([low, high], axis=dim + 1)
            shape = held.shape
            held = held.reshape(*shape[:dim], shape[dim] * shape[dim + 1], 1, *shape[dim + 2 :])
        shape = held.shape
        held = held.reshape(*shape[: dim + 1], *shape[dim + 2 :])
    return held.reshape(-1, array.shape[-1])


def split_terms(array):
    high = lax.reduce_precision(array, 8, 7)
    return high.astype(jnp.bfloat16), (array - high).astype(jnp.bfloat16)


def invert(system):
    size = system.shape[0]
    lanes = lax.broadcasted_iota(jnp.int32, (ROWS, size), 1)
    subs = lax.broadcasted_iota(jnp.int32, (ROWS, size), 0)
    rows = [system[r : r + ROWS] for r in range(0, size, ROWS)]

    def column(block, at):
        return jnp.broadcast_to(block[:, at : at + 1], (ROWS, size))

    for panel in range(size // ROWS):
        first = panel * ROWS
        inside = (lanes >= first) & (lanes < first + ROWS)
        unit = (lanes - first == subs).astype(jnp.float32)
        pivots = [column(rows[panel], first + c) for c in range(ROWS)]
        solved = jnp.where(inside, unit, rows[panel])
        for k in range(ROWS):
            scale = 1.0 / pivots[k][k : k + 1]
            here = subs == k
            top = solved[k : k + 1] * scale
            solved = jnp.where(here, top, solved - pivots[k] * top)
            for c in range(k + 1, ROWS):
                top = pivots[c][k : k + 1] * scale
                pivots[c] = jnp.where(here, top, pivots[c] - pivots[k] * top)
        for r in range(len(rows)):
            if r == panel:
                continue
            old = rows[r]
            new = jnp.where(inside, 0.0, old)
            for c in range(ROWS):
                new = new - column(old, first + c) * solved[c : c + 1]
            rows[r] = new
        rows[panel] = solved
    return jnp.concatenate(rows, axis=0)


def spd_inverse(system):
    square = lax.dot_general(
        system, system, ROW_ROW, precision=HIGHEST, preferred_element_type=jnp.float32
    )
    return invert(square)


def local_kernel(
    chunks,
    shares,
    field_hbm,
    last_x_hbm,
    last_y_hbm,
    right_y_hbm,
    right_m_hbm,
    last_m_hbm,
    last_part,
    first_part,
    *refs,
):
    terms_hbm = refs[: shares * PARTS]
    field, last_x, last_y, right_y, right_m, last_m, terms, sems, out_sems = refs[shares * PARTS :]
    x_cells, y_cells, m_cells = field.shape
    step = x_cells // chunks
    y_share = y_cells // shares
    parts = [pl.ds(n * step, step) for n in range(chunks)]
    copies = [
        pltpu.make_async_copy(last_m_hbm, last_m, sems.at[0]),
        pltpu.make_async_copy(field_hbm.at[parts[0]], field.at[parts[0]], sems.at[1]),
        pltpu.make_async_copy(last_x_hbm, last_x, sems.at[2]),
        pltpu.make_async_copy(last_y_hbm, last_y, sems.at[3]),
        pltpu.make_async_copy(right_m_hbm, right_m, sems.at[4]),
        pltpu.make_async_copy(right_y_hbm, right_y, sems.at[5]),
    ]
    for n in range(1, chunks):
        copies.append(
            pltpu.make_async_copy(field_hbm.at[parts[n]], field.at[parts[n]], sems.at[5 + n])
        )
    for copy in copies:
        copy.start()
    here = lax.axis_index("gz")
    leaving = []
    copies[0].wait()
    for n in range(chunks):
        copies[5 + n if n else 1].wait()
        for s in reversed(range(shares)):
            start = pl.multiple_of((here ^ s) * y_share, y_share)
            rows = field[parts[n], pl.ds(start, y_share), :].reshape(step * y_share, m_cells)
            term = jnp.dot(rows, last_m[...], preferred_element_type=jnp.float32)
            terms[s, parts[n]] = term.reshape(step, y_share, -1)
            part, at = divmod(n * step, x_cells // PARTS)
            leaving.append(
                pltpu.make_async_copy(
                    terms.at[s, parts[n]],
                    terms_hbm[s * PARTS + part].at[pl.ds(at, step)],
                    out_sems.at[s, n],
                )
            )
            leaving[-1].start()

    for copy in copies[2:6]:
        copy.wait()
    for n in range(chunks):
        rows = field[parts[n]].reshape(step * y_cells, m_cells)
        left = last_x[parts[n]].astype(jnp.float32)[:, None, :]
        khatri = left * last_y[...].astype(jnp.float32)[None]
        khatri = khatri.astype(jnp.bfloat16).reshape(step * y_cells, -1)
        part = lax.dot_general(khatri, rows, COL_COL, preferred_element_type=jnp.float32)
        if n == 0:
            last_part[...] = part
        else:
            last_part[...] += part
        first = jnp.dot(rows, right_m[...], preferred_element_type=jnp.float32)
        first = first.reshape(step, y_cells, -1) * right_y[...].astype(jnp.float32)[None]
        first_part[parts[n], :] = jnp.sum(first, axis=1)
    for copy in leaving:
        copy.wait()


def local_products(shares, field, last_x, last_y, right_y, right_m, last_m):
    x_cells, y_cells, m_cells = field.shape
    rank, cols = last_x.shape[1], last_m.shape[1]
    chunks = max(x_cells // 8, 1)
    inputs = (field, last_x, last_y, right_y, right_m, last_m)
    dims = (x_cells, y_cells // shares, cols)
    part_dims = (x_cells // PARTS, *dims[1:])
    hbm = pl.BlockSpec(memory_space=pltpu.HBM)
    vmem = pl.BlockSpec(memory_space=pltpu.VMEM)
    return pl.pallas_call(
        functools.partial(local_kernel, chunks, shares),
        in_specs=[hbm] * len(inputs),
        out_specs=[vmem, vmem, *([hbm] * (shares * PARTS))],
        out_shape=[
            jax.ShapeDtypeStruct((rank, m_cells), jnp.float32),
            jax.ShapeDtypeStruct((x_cells, cols), jnp.float32),
            *([jax.ShapeDtypeStruct(part_dims, jnp.float32)] * (shares * PARTS)),
        ],
        scratch_shapes=[
            *(pltpu.VMEM(x.shape, x.dtype) for x in inputs),
            pltpu.VMEM((shares, *dims), jnp.float32),
            pltpu.SemaphoreType.DMA((5 + chunks,)),
            pltpu.SemaphoreType.DMA((shares, chunks)),
        ],
        compiler_params=pltpu.CompilerParams(vmem_limit_bytes=LOCAL_VMEM_BYTES),
        name="local_products",
    )(*inputs)


def inverse_kernel(system_shares, pinv):
    system = system_shares[:, 0]
    for k in range(1, system_shares.shape[1]):
        system = system + system_shares[:, k]
    system = system.reshape(-1, system.shape[-1])
    pinv[...] = jnp.dot(
        spd_inverse(system), system, precision=HIGHEST, preferred_element_type=jnp.float32
    )


def pseudo_inverse(system_shares):
    rank = system_shares.shape[0] * system_shares.shape[2]
    return pl.pallas_call(
        inverse_kernel,
        out_shape=jax.ShapeDtypeStruct((rank, system_shares.shape[3]), jnp.float32),
        compiler_params=pltpu.CompilerParams(vmem_limit_bytes=VMEM_BYTES),
        name="pseudo_inverse",
    )(system_shares)


def two_terms(array):
    high = array.astype(jnp.bfloat16)
    return high, (array - high.astype(jnp.float32)).astype(jnp.bfloat16)


def project_kernel(y_own, pinv, extra, *refs):
    *terms, projected, flat = refs
    rank = pinv.shape[0]
    pinv_high, pinv_low = two_terms(pinv[...])
    pinv_both = jnp.concatenate([pinv_high, pinv_low], axis=0)
    rows = flat.shape[0] // PARTS
    for part in range(PARTS):
        total = terms[part][...]
        for term in terms[part + PARTS :: PARTS]:
            total = total + term[...]
        high, low = two_terms(total.reshape(rows, -1))
        both = lax.dot_general(high, pinv_both, ROW_ROW, preferred_element_type=jnp.float32)
        rest = lax.dot_general(low, pinv_high, ROW_ROW, preferred_element_type=jnp.float32)
        flat[part * rows : (part + 1) * rows] = both[:, :rank] + (both[:, rank:] + rest)
    x_cells, y_cells, _ = terms[0].shape
    x_cells *= PARTS
    for b in range(projected.shape[0]):
        for j in range(y_own):
            projected[b, j * x_cells : (j + 1) * x_cells] = flat[
                pl.ds(b * y_own + j, x_cells, stride=y_cells), :
            ]
        projected[b, y_own * x_cells :] = extra[...]


def project(blocks, pinv, extra, terms):
    rank = pinv.shape[0]
    x_cells, y_cells, _ = terms[0].shape
    x_cells *= PARTS
    y_own = y_cells // blocks
    rows = y_own * x_cells + extra.shape[0]
    return pl.pallas_call(
        functools.partial(project_kernel, y_own),
        out_shape=jax.ShapeDtypeStruct((blocks, rows, rank), jnp.float32),
        scratch_shapes=[pltpu.VMEM((x_cells * y_cells, rank), jnp.float32)],
        compiler_params=pltpu.CompilerParams(vmem_limit_bytes=VMEM_BYTES),
        name="project",
    )(pinv, extra, *terms)


def sketch_kernel(order, left_at, y_own, pieces, packed, out, extra):
    me = lax.axis_index("gx")
    blocks, _, cols = pieces.shape
    x_cells = packed.shape[1] - left_at
    weights = jnp.concatenate([packed[k, left_at:] for k in range(blocks)], axis=0)
    weights = weights.astype(jnp.bfloat16)
    for j in range(y_own):
        column = jnp.concatenate(
            [pieces[me ^ o, j * x_cells : (j + 1) * x_cells] for o in order], axis=0
        )
        high = column.astype(jnp.bfloat16)
        low = (column - high.astype(jnp.float32)).astype(jnp.bfloat16)
        both = lax.dot_general(
            weights,
            jnp.concatenate([high, low], axis=1),
            COL_COL,
            preferred_element_type=jnp.float32,
        )
        both = both[:, :cols] + both[:, cols:]
        out[:, j] = both.reshape(out.shape[0], out.shape[2], cols)
    extra[...] = pieces[:, y_own * x_cells :]


def sketch(order, left_at, y_own, own, pieces, packed):
    blocks, rows, cols = pieces.shape
    rank = packed.shape[2]
    extra = rows - y_own * (packed.shape[1] - left_at)
    return pl.pallas_call(
        functools.partial(sketch_kernel, order, left_at, y_own),
        out_shape=(
            jax.ShapeDtypeStruct((rank // own, y_own, own, cols), jnp.float32),
            jax.ShapeDtypeStruct((blocks, extra, cols), jnp.float32),
        ),
        compiler_params=pltpu.CompilerParams(vmem_limit_bytes=VMEM_BYTES),
        name="sketch",
    )(pieces, packed)


def first_sums_kernel(left_at, rows, packed, sums):
    x_cells, cols = rows.shape
    blocks = range(packed.shape[0])
    left = jnp.concatenate([packed[k, left_at : left_at + x_cells] for k in blocks], axis=0)
    sums[:x_cells] = rows[...]
    for c in range(cols // LANES):
        at = c * x_cells
        sums[x_cells:, c * LANES : (c + 1) * LANES] = lax.dot_general(
            left,
            jnp.concatenate([packed[k, at : at + x_cells] for k in blocks], axis=0),
            COL_COL,
            precision=HIGHEST,
            preferred_element_type=jnp.float32,
        )


def first_sums(left_at, rows, packed):
    return pl.pallas_call(
        functools.partial(first_sums_kernel, left_at),
        out_shape=jax.ShapeDtypeStruct(
            (rows.shape[0] + packed.shape[2], rows.shape[1]), jnp.float32
        ),
        compiler_params=pltpu.CompilerParams(vmem_limit_bytes=VMEM_BYTES),
        name="first_sums",
    )(rows, packed)


def first_kernel(*refs):
    *sums, core_first = refs
    x_cells = core_first.shape[0]
    total = sums[0][...]
    for other in sums[1:]:
        total = total + other[...]
    system = total[x_cells:]
    inverse = spd_inverse(system)
    scores = lax.dot_general(
        total[:x_cells], system, ROW_ROW, precision=HIGHEST, preferred_element_type=jnp.float32
    )
    core_first[...] = jnp.dot(
        scores, inverse, precision=HIGHEST, preferred_element_type=jnp.float32
    )


def solve_first(x_cells, *sums):
    return pl.pallas_call(
        first_kernel,
        out_shape=jax.ShapeDtypeStruct((x_cells, sums[0].shape[0] - x_cells), jnp.float32),
        compiler_params=pltpu.CompilerParams(vmem_limit_bytes=VMEM_BYTES),
        name="solve_first",
    )(*sums)


def place_kernel(own, inner_order, *refs):
    *parts, core_last = refs
    inner = lax.axis_index("gy")
    for part, i in zip(parts, inner_order):
        for o in range(part.shape[0]):
            at = pl.multiple_of((o * len(parts) + (inner ^ i)) * own, own)
            for c in range(part.shape[1] // own):
                core_last[pl.ds(at, own), c * LANES : (c + 1) * LANES] = part[
                    o, c * own : (c + 1) * own
                ]


def place(own, inner_order, parts):
    outer, rows, lanes = parts[0].shape
    return pl.pallas_call(
        functools.partial(place_kernel, own, inner_order),
        out_shape=jax.ShapeDtypeStruct(
            (len(parts) * outer * own, rows // own * lanes), jnp.float32
        ),
        compiler_params=pltpu.CompilerParams(vmem_limit_bytes=VMEM_BYTES),
        name="place",
    )(*parts)


def per_device(flow_field, left_x, last_x, last_y, right_y, right_m, last_m):
    x_cells, y_cells, m_cells = flow_field.shape
    rank = left_x.shape[1]
    cols = right_m.shape[1]
    blocks, shares = lax.axis_size("gx"), lax.axis_size("gz")
    y_share = y_cells // shares
    y_own = y_share // blocks

    last_part, first_part, *terms = local_products(
        shares, flow_field, last_x, last_y, right_y, right_m, last_m
    )

    for s in range(1, shares):
        for part in range(PARTS):
            terms[s * PARTS + part] = swap(terms[s * PARTS + part], "gz", s)

    order = swap_order("gx")
    first_rows = swap_sum(first_part, "gy")
    packed = jnp.concatenate(
        [
            first_rows.reshape(x_cells, -1, LANES).transpose(1, 0, 2).reshape(-1, LANES),
            left_x.astype(jnp.float32),
        ],
        axis=0,
    )[None]
    left_at = x_cells * cols // LANES
    first_bit, *bits = axis_bits("gx")
    packed = swap_step(packed, "gx", first_bit)

    group = ("gx", "gy")
    own = rank // lax.axis_size(group)
    last_rows = lax.all_to_all(last_part.reshape(-1, own, m_cells), group, 0, 0, tiled=True)
    last_rows = jnp.sum(after(last_rows, *terms[PARTS::PARTS]), axis=0)
    both = jnp.dot(
        jnp.concatenate(split_terms(last_rows), axis=0), last_m, preferred_element_type=jnp.float32
    )
    both = after(both[:own] + both[own:], packed)
    count = lax.axis_size(ALL)
    copies = jnp.broadcast_to(both[None], (count, own, cols))
    system = lax.all_to_all(copies, ALL, 0, 0, tiled=True).reshape(-1, shares, own, cols)
    if own % ROWS:
        system = jnp.sum(system, axis=1).reshape(-1, 1, ROWS, cols)

    for bit in bits:
        packed = swap_step(packed, "gx", bit)
    sums = first_sums(left_at, first_rows, packed)
    if own % ROWS:
        extra = jnp.zeros((ROWS, LANES), jnp.float32)
    else:
        extra = last_rows.reshape(own, -1, LANES).transpose(1, 0, 2).reshape(-1, LANES)
    pinv = pseudo_inverse(after(system, packed, *terms[PARTS:]))
    projected = project(blocks, pinv, extra, terms)
    sums = [swap(sums, "gz", z) if z else sums for z in range(shares)]

    pieces = lax.all_to_all(projected, "gx", 0, 0, tiled=True)
    core_first = solve_first(x_cells, after(sums[0], projected), *sums[1:])
    group = ("gx", "gz")
    devices = lax.axis_size(group)
    rank_own = rank // devices
    if rank_own % ROWS:
        middle, extra = sketch(order, left_at, y_own, rank, pieces, packed)
        middle = middle.reshape(y_own, devices, rank_own, rank).transpose(1, 0, 2, 3)
    else:
        middle, extra = sketch(order, left_at, y_own, rank_own, pieces, packed)
    middle, core_first = lax.optimization_barrier((middle, core_first))
    received = lax.all_to_all(middle, group, 0, 0, tiled=True)
    received = received.reshape(blocks, shares, y_own, rank_own, rank)
    core_middle = received.transpose(3, 1, 0, 2, 4).reshape(rank_own, y_cells, rank)

    if own % ROWS:
        core_last = gather_rows(last_rows, "gx", "gy")
    else:
        inner = range(lax.axis_size("gy"))
        core_last = place(own, inner, [swap(extra, "gy", i) if i else extra for i in inner])
    return (core_first, core_middle, core_last)


def solution(mesh):
    return jax.shard_map(
        per_device,
        mesh=mesh,
        in_specs=(
            P("gx", "gy", "gz"),
            P("gx", None),
            P("gx", None),
            P("gy", None),
            P("gy", None),
            P("gz", None),
            P("gz", None),
        ),
        out_specs=(P("gx", None), P(("gx", "gz"), "gy", None), P(None, "gz")),
        check_vma=False,
    )
```

```python
import functools

import jax
import jax.numpy as jnp
from jax import lax
from jax.experimental import pallas as pl
from jax.experimental.pallas import tpu as pltpu
from jax.sharding import PartitionSpec as P

ALL = ("gx", "gy", "gz")
HIGHEST = lax.Precision.HIGHEST
VMEM_BYTES = 48 * 1024 * 1024
LOCAL_VMEM_BYTES = 63 * 1024 * 1024
ROWS = 8
LANES = 128
PARTS = 2
ROW_ROW = (((1,), (1,)), ((), ()))
COL_COL = (((0,), (0,)), ((), ()))


def axis_bits(axis):
    bit = lax.axis_size(axis) // 2
    while bit:
        yield bit
        bit //= 2


def swap(array, axis, bits):
    return lax.ppermute(array, axis, [(s, s ^ bits) for s in range(lax.axis_size(axis))])


def swap_sum(array, axis):
    for bit in axis_bits(axis):
        array = array + swap(array, axis, bit)
    return array


def after(value, *others):
    value, *_ = lax.optimization_barrier((value, *others))
    return value


def swap_order(axis):
    order = [0]
    for bit in axis_bits(axis):
        order += [o ^ bit for o in order]
    return order


def swap_step(held, axis, bit):
    return jnp.concatenate([held, swap(held, axis, bit)], axis=0)


def gather_rows(array, outer, inner):
    held = array[None, None]
    for dim, axis in ((0, outer), (1, inner)):
        shape = held.shape
        held = held.reshape(*shape[:dim], 1, 1, *shape[dim + 1 :])
        for bit in axis_bits(axis):
            other = swap(held, axis, bit)
            upper = (lax.axis_index(axis) & bit) != 0
            low = jnp.where(upper, other, held)
            high = jnp.where(upper, held, other)
            held = jnp.concatenate([low, high], axis=dim + 1)
            shape = held.shape
            held = held.reshape(*shape[:dim], shape[dim] * shape[dim + 1], 1, *shape[dim + 2 :])
        shape = held.shape
        held = held.reshape(*shape[: dim + 1], *shape[dim + 2 :])
    return held.reshape(-1, array.shape[-1])


def split_terms(array):
    high = lax.reduce_precision(array, 8, 7)
    return high.astype(jnp.bfloat16), (array - high).astype(jnp.bfloat16)


def invert(system):
    size = system.shape[0]
    lanes = lax.broadcasted_iota(jnp.int32, (ROWS, size), 1)
    subs = lax.broadcasted_iota(jnp.int32, (ROWS, size), 0)
    rows = [system[r : r + ROWS] for r in range(0, size, ROWS)]

    def column(block, at):
        return jnp.broadcast_to(block[:, at : at + 1], (ROWS, size))

    for panel in range(size // ROWS):
        first = panel * ROWS
        inside = (lanes >= first) & (lanes < first + ROWS)
        unit = (lanes - first == subs).astype(jnp.float32)
        work = [column(rows[panel], first + c) for c in range(ROWS)]
        work.append(jnp.where(inside, unit, rows[panel]))
        for k in range(0, ROWS, 2):
            p, q = work[k], work[k + 1]
            a, b, d = p[k : k + 1], q[k : k + 1], q[k + 1 : k + 2]
            scale = 1.0 / (a * d - b * b)
            a, b, d = a * scale, b * scale, d * scale
            for c in range(k + 2, ROWS + 1):
                upper, lower = work[c][k : k + 1], work[c][k + 1 : k + 2]
                top = d * upper - b * lower
                low = a * lower - b * upper
                rest = work[c] - p * top - q * low
                work[c] = jnp.where(subs == k, top, jnp.where(subs == k + 1, low, rest))
        solved = work[ROWS]
        for r in range(len(rows)):
            if r == panel:
                continue
            old = rows[r]
            new = jnp.where(inside, 0.0, old)
            for c in range(ROWS):
                new = new - column(old, first + c) * solved[c : c + 1]
            rows[r] = new
        rows[panel] = solved
    return jnp.concatenate(rows, axis=0)


def spd_inverse(system):
    square = lax.dot_general(
        system, system, ROW_ROW, precision=HIGHEST, preferred_element_type=jnp.float32
    )
    return invert(square)


def local_kernel(
    chunks,
    shares,
    field_hbm,
    last_x_hbm,
    last_y_hbm,
    right_y_hbm,
    right_m_hbm,
    last_m_hbm,
    last_part,
    first_part,
    *refs,
):
    count = (shares - 1) * PARTS
    terms_hbm = refs[:count]
    field, last_x, last_y, right_y, right_m, last_m, terms, sems, out_sems = refs[count:]
    x_cells, y_cells, m_cells = field.shape
    step = x_cells // chunks
    y_share = y_cells // shares
    parts = [pl.ds(n * step, step) for n in range(chunks)]
    copies = [
        pltpu.make_async_copy(last_m_hbm, last_m, sems.at[0]),
        pltpu.make_async_copy(field_hbm.at[parts[0]], field.at[parts[0]], sems.at[1]),
        pltpu.make_async_copy(last_x_hbm, last_x, sems.at[2]),
        pltpu.make_async_copy(last_y_hbm, last_y, sems.at[3]),
        pltpu.make_async_copy(right_m_hbm, right_m, sems.at[4]),
        pltpu.make_async_copy(right_y_hbm, right_y, sems.at[5]),
    ]
    for n in range(1, chunks):
        copies.append(
            pltpu.make_async_copy(field_hbm.at[parts[n]], field.at[parts[n]], sems.at[5 + n])
        )
    for copy in copies:
        copy.start()
    here = lax.axis_index("gz")
    leaving = []
    copies[0].wait()
    for n in range(chunks):
        copies[5 + n if n else 1].wait()
        for s in range(1, shares):
            start = pl.multiple_of((here ^ s) * y_share, y_share)
            rows = field[parts[n], pl.ds(start, y_share), :].reshape(step * y_share, m_cells)
            term = jnp.dot(rows, last_m[...], preferred_element_type=jnp.float32)
            terms[s - 1, parts[n]] = term.reshape(step, y_share, -1)
            part, at = divmod(n * step, x_cells // PARTS)
            leaving.append(
                pltpu.make_async_copy(
                    terms.at[s - 1, parts[n]],
                    terms_hbm[(s - 1) * PARTS + part].at[pl.ds(at, step)],
                    out_sems.at[s - 1, n],
                )
            )
            leaving[-1].start()

    for copy in copies[2:6]:
        copy.wait()
    for n in range(chunks):
        rows = field[parts[n]].reshape(step * y_cells, m_cells)
        left = last_x[parts[n]].astype(jnp.float32)[:, None, :]
        khatri = left * last_y[...].astype(jnp.float32)[None]
        khatri = khatri.astype(jnp.bfloat16).reshape(step * y_cells, -1)
        part = lax.dot_general(khatri, rows, COL_COL, preferred_element_type=jnp.float32)
        if n == 0:
            last_part[...] = part
        else:
            last_part[...] += part
        first = jnp.dot(rows, right_m[...], preferred_element_type=jnp.float32)
        first = first.reshape(step, y_cells, -1) * right_y[...].astype(jnp.float32)[None]
        first_part[parts[n], :] = jnp.sum(first, axis=1)
    for copy in leaving:
        copy.wait()


def local_products(shares, field, last_x, last_y, right_y, right_m, last_m):
    x_cells, y_cells, m_cells = field.shape
    rank, cols = last_x.shape[1], last_m.shape[1]
    chunks = max(x_cells // 8, 1)
    inputs = (field, last_x, last_y, right_y, right_m, last_m)
    dims = (x_cells, y_cells // shares, cols)
    part_dims = (x_cells // PARTS, *dims[1:])
    hbm = pl.BlockSpec(memory_space=pltpu.HBM)
    vmem = pl.BlockSpec(memory_space=pltpu.VMEM)
    return pl.pallas_call(
        functools.partial(local_kernel, chunks, shares),
        in_specs=[hbm] * len(inputs),
        out_specs=[vmem, vmem, *([hbm] * ((shares - 1) * PARTS))],
        out_shape=[
            jax.ShapeDtypeStruct((rank, m_cells), jnp.float32),
            jax.ShapeDtypeStruct((x_cells, cols), jnp.float32),
            *([jax.ShapeDtypeStruct(part_dims, jnp.float32)] * ((shares - 1) * PARTS)),
        ],
        scratch_shapes=[
            *(pltpu.VMEM(x.shape, x.dtype) for x in inputs),
            pltpu.VMEM((shares - 1, *dims), jnp.float32),
            pltpu.SemaphoreType.DMA((5 + chunks,)),
            pltpu.SemaphoreType.DMA((shares - 1, chunks)),
        ],
        compiler_params=pltpu.CompilerParams(vmem_limit_bytes=LOCAL_VMEM_BYTES),
        name="local_products",
    )(*inputs)


def two_terms(array):
    high = array.astype(jnp.bfloat16)
    return high, (array - high.astype(jnp.float32)).astype(jnp.bfloat16)


def inverse_kernel(system_shares, pinv):
    system = system_shares[:, 0]
    for k in range(1, system_shares.shape[1]):
        system = system + system_shares[:, k]
    system = system.reshape(-1, system.shape[-1])
    cols = system.shape[1]
    high, low = two_terms(spd_inverse(system))
    system_high, system_low = two_terms(system)
    both = jnp.dot(
        high,
        jnp.concatenate([system_high, system_low], axis=1),
        preferred_element_type=jnp.float32,
    )
    rest = jnp.dot(low, system_high, preferred_element_type=jnp.float32)
    pinv[...] = both[:, :cols] + (both[:, cols:] + rest)


def pseudo_inverse(system_shares):
    rank = system_shares.shape[0] * system_shares.shape[2]
    return pl.pallas_call(
        inverse_kernel,
        out_shape=jax.ShapeDtypeStruct((rank, system_shares.shape[3]), jnp.float32),
        compiler_params=pltpu.CompilerParams(vmem_limit_bytes=VMEM_BYTES),
        name="pseudo_inverse",
    )(system_shares)


def project_kernel(y_own, pinv, extra, kept, *refs):
    *terms, projected, flat = refs
    rank = pinv.shape[0]
    pinv_high, pinv_low = two_terms(pinv[...])
    pinv_both = jnp.concatenate([pinv_high, pinv_low], axis=0)
    rows = flat.shape[0] // PARTS
    x_cells, y_cells, _ = kept.shape
    x_part = x_cells // PARTS
    for part in range(PARTS):
        total = kept[part * x_part : (part + 1) * x_part]
        for term in terms[part::PARTS]:
            total = total + term[...]
        high, low = two_terms(total.reshape(rows, -1))
        both = lax.dot_general(high, pinv_both, ROW_ROW, preferred_element_type=jnp.float32)
        rest = lax.dot_general(low, pinv_high, ROW_ROW, preferred_element_type=jnp.float32)
        flat[part * rows : (part + 1) * rows] = both[:, :rank] + (both[:, rank:] + rest)
    for b in range(projected.shape[0]):
        for j in range(y_own):
            projected[b, j * x_cells : (j + 1) * x_cells] = flat[
                pl.ds(b * y_own + j, x_cells, stride=y_cells), :
            ]
        projected[b, y_own * x_cells :] = extra[...]


def project(blocks, pinv, extra, kept, terms):
    rank = pinv.shape[0]
    x_cells, y_cells, _ = kept.shape
    y_own = y_cells // blocks
    rows = y_own * x_cells + extra.shape[0]
    return pl.pallas_call(
        functools.partial(project_kernel, y_own),
        out_shape=jax.ShapeDtypeStruct((blocks, rows, rank), jnp.float32),
        scratch_shapes=[pltpu.VMEM((x_cells * y_cells, rank), jnp.float32)],
        compiler_params=pltpu.CompilerParams(vmem_limit_bytes=VMEM_BYTES),
        name="project",
    )(pinv, extra, kept, *terms)


def sketch_kernel(order, left_at, y_own, pieces, packed, out, extra):
    me = lax.axis_index("gx")
    blocks, _, cols = pieces.shape
    x_cells = packed.shape[1] - left_at
    weights = jnp.concatenate([packed[k, left_at:] for k in range(blocks)], axis=0)
    weights = weights.astype(jnp.bfloat16)
    for j in range(y_own):
        column = jnp.concatenate(
            [pieces[me ^ o, j * x_cells : (j + 1) * x_cells] for o in order], axis=0
        )
        high = column.astype(jnp.bfloat16)
        low = (column - high.astype(jnp.float32)).astype(jnp.bfloat16)
        both = lax.dot_general(
            weights,
            jnp.concatenate([high, low], axis=1),
            COL_COL,
            preferred_element_type=jnp.float32,
        )
        both = both[:, :cols] + both[:, cols:]
        out[:, j] = both.reshape(out.shape[0], out.shape[2], cols)
    extra[...] = pieces[:, y_own * x_cells :]


def sketch(order, left_at, y_own, own, pieces, packed):
    blocks, rows, cols = pieces.shape
    rank = packed.shape[2]
    extra = rows - y_own * (packed.shape[1] - left_at)
    return pl.pallas_call(
        functools.partial(sketch_kernel, order, left_at, y_own),
        out_shape=(
            jax.ShapeDtypeStruct((rank // own, y_own, own, cols), jnp.float32),
            jax.ShapeDtypeStruct((blocks, extra, cols), jnp.float32),
        ),
        compiler_params=pltpu.CompilerParams(vmem_limit_bytes=VMEM_BYTES),
        name="sketch",
    )(pieces, packed)


def first_sums_kernel(left_at, rows, packed, sums):
    x_cells, cols = rows.shape
    blocks = range(packed.shape[0])
    left = jnp.concatenate([packed[k, left_at : left_at + x_cells] for k in blocks], axis=0)
    sums[:x_cells] = rows[...]
    for c in range(cols // LANES):
        at = c * x_cells
        sums[x_cells:, c * LANES : (c + 1) * LANES] = lax.dot_general(
            left,
            jnp.concatenate([packed[k, at : at + x_cells] for k in blocks], axis=0),
            COL_COL,
            precision=HIGHEST,
            preferred_element_type=jnp.float32,
        )


def first_sums(left_at, rows, packed):
    return pl.pallas_call(
        functools.partial(first_sums_kernel, left_at),
        out_shape=jax.ShapeDtypeStruct(
            (rows.shape[0] + packed.shape[2], rows.shape[1]), jnp.float32
        ),
        compiler_params=pltpu.CompilerParams(vmem_limit_bytes=VMEM_BYTES),
        name="first_sums",
    )(rows, packed)


def first_kernel(*refs):
    *sums, core_first = refs
    x_cells = core_first.shape[0]
    total = sums[0][...]
    for other in sums[1:]:
        total = total + other[...]
    system = total[x_cells:]
    inverse = spd_inverse(system)
    scores = lax.dot_general(
        total[:x_cells], system, ROW_ROW, precision=HIGHEST, preferred_element_type=jnp.float32
    )
    core_first[...] = jnp.dot(
        scores, inverse, precision=HIGHEST, preferred_element_type=jnp.float32
    )


def solve_first(x_cells, *sums):
    return pl.pallas_call(
        first_kernel,
        out_shape=jax.ShapeDtypeStruct((x_cells, sums[0].shape[0] - x_cells), jnp.float32),
        compiler_params=pltpu.CompilerParams(vmem_limit_bytes=VMEM_BYTES),
        name="solve_first",
    )(*sums)


def place_kernel(own, inner_order, *refs):
    *parts, core_last = refs
    inner = lax.axis_index("gy")
    for part, i in zip(parts, inner_order):
        for o in range(part.shape[0]):
            at = pl.multiple_of((o * len(parts) + (inner ^ i)) * own, own)
            for c in range(part.shape[1] // own):
                core_last[pl.ds(at, own), c * LANES : (c + 1) * LANES] = part[
                    o, c * own : (c + 1) * own
                ]


def place(own, inner_order, parts):
    outer, rows, lanes = parts[0].shape
    return pl.pallas_call(
        functools.partial(place_kernel, own, inner_order),
        out_shape=jax.ShapeDtypeStruct(
            (len(parts) * outer * own, rows // own * lanes), jnp.float32
        ),
        compiler_params=pltpu.CompilerParams(vmem_limit_bytes=VMEM_BYTES),
        name="place",
    )(*parts)


def per_device(flow_field, left_x, last_x, last_y, right_y, right_m, last_m):
    x_cells, y_cells, m_cells = flow_field.shape
    rank = left_x.shape[1]
    cols = right_m.shape[1]
    blocks, shares = lax.axis_size("gx"), lax.axis_size("gz")
    y_share = y_cells // shares
    y_own = y_share // blocks

    last_part, first_part, *terms = local_products(
        shares, flow_field, last_x, last_y, right_y, right_m, last_m
    )

    terms = [swap(term, "gz", 1 + at // PARTS) for at, term in enumerate(terms)]
    here = lax.axis_index("gz")
    kept = flow_field.reshape(x_cells, shares, y_share, m_cells)
    kept = lax.dynamic_index_in_dim(kept, here, 1, False).reshape(-1, m_cells)
    kept = jnp.dot(kept, last_m, preferred_element_type=jnp.float32)
    kept = kept.reshape(x_cells, y_share, cols)

    order = swap_order("gx")
    packed = jnp.concatenate(
        [
            first_part.reshape(x_cells, -1, LANES).transpose(1, 0, 2).reshape(-1, LANES),
            left_x.astype(jnp.float32),
        ],
        axis=0,
    )[None]
    left_at = x_cells * cols // LANES
    first_bit, *bits = axis_bits("gx")
    packed = swap_step(packed, "gx", first_bit)

    group = ("gx", "gy")
    own = rank // lax.axis_size(group)
    last_rows = lax.all_to_all(last_part.reshape(-1, own, m_cells), group, 0, 0, tiled=True)
    last_rows = jnp.sum(after(last_rows, *terms[::PARTS]), axis=0)
    both = jnp.dot(
        jnp.concatenate(split_terms(last_rows), axis=0), last_m, preferred_element_type=jnp.float32
    )
    both = after(both[:own] + both[own:], packed, kept)
    count = lax.axis_size(ALL)
    copies = jnp.broadcast_to(both[None], (count, own, cols))
    system = lax.all_to_all(copies, ALL, 0, 0, tiled=True).reshape(-1, shares, own, cols)
    if own % ROWS:
        system = jnp.sum(system, axis=1).reshape(-1, 1, ROWS, cols)

    for bit in bits:
        packed = swap_step(packed, "gx", bit)
    sums = first_sums(left_at, first_part, packed)
    if own % ROWS:
        extra = jnp.zeros((ROWS, LANES), jnp.float32)
    else:
        extra = last_rows.reshape(own, -1, LANES).transpose(1, 0, 2).reshape(-1, LANES)
    pinv = pseudo_inverse(after(system, packed, *terms))
    projected = project(blocks, pinv, extra, kept, terms)
    sums = swap_sum(sums, "gz")
    sums = [swap(sums, "gy", y) if y else sums for y in range(lax.axis_size("gy"))]

    pieces = lax.all_to_all(projected, "gx", 0, 0, tiled=True)
    core_first = solve_first(x_cells, after(sums[0], projected), *sums[1:])
    group = ("gx", "gz")
    devices = lax.axis_size(group)
    rank_own = rank // devices
    if rank_own % ROWS:
        middle, extra = sketch(order, left_at, y_own, rank, pieces, packed)
        middle = middle.reshape(y_own, devices, rank_own, rank).transpose(1, 0, 2, 3)
    else:
        middle, extra = sketch(order, left_at, y_own, rank_own, pieces, packed)
    middle, core_first = lax.optimization_barrier((middle, core_first))
    received = lax.all_to_all(middle, group, 0, 0, tiled=True)
    received = received.reshape(blocks, shares, y_own, rank_own, rank)
    core_middle = received.transpose(3, 1, 0, 2, 4).reshape(rank_own, y_cells, rank)

    if own % ROWS:
        core_last = gather_rows(last_rows, "gx", "gy")
    else:
        inner = range(lax.axis_size("gy"))
        core_last = place(own, inner, [swap(extra, "gy", i) if i else extra for i in inner])
    return (core_first, core_middle, core_last)


def solution(mesh):
    return jax.shard_map(
        per_device,
        mesh=mesh,
        in_specs=(
            P("gx", "gy", "gz"),
            P("gx", None),
            P("gx", None),
            P("gy", None),
            P("gy", None),
            P("gz", None),
            P("gz", None),
        ),
        out_specs=(P("gx", None), P(("gx", "gz"), "gy", None), P(None, "gz")),
        check_vma=False,
    )
```

```python
import functools

import jax
import jax.numpy as jnp
from jax import lax
from jax.experimental import pallas as pl
from jax.experimental.pallas import tpu as pltpu
from jax.sharding import PartitionSpec as P

ALL = ("gx", "gy", "gz")
HIGHEST = lax.Precision.HIGHEST
VMEM_BYTES = 48 * 1024 * 1024
LOCAL_VMEM_BYTES = 63 * 1024 * 1024
ROWS = 8
LANES = 128
PARTS = 2
ROW_ROW = (((1,), (1,)), ((), ()))
COL_COL = (((0,), (0,)), ((), ()))


def axis_bits(axis):
    bit = lax.axis_size(axis) // 2
    while bit:
        yield bit
        bit //= 2


def swap(array, axis, bits):
    return lax.ppermute(array, axis, [(s, s ^ bits) for s in range(lax.axis_size(axis))])


def swap_sum(array, axis):
    for bit in axis_bits(axis):
        array = array + swap(array, axis, bit)
    return array


def after(value, *others):
    value, *_ = lax.optimization_barrier((value, *others))
    return value


def swap_order(axis):
    order = [0]
    for bit in axis_bits(axis):
        order += [o ^ bit for o in order]
    return order


def swap_step(held, axis, bit):
    return jnp.concatenate([held, swap(held, axis, bit)], axis=0)


def gather_rows(array, outer, inner):
    held = array[None, None]
    for dim, axis in ((0, outer), (1, inner)):
        shape = held.shape
        held = held.reshape(*shape[:dim], 1, 1, *shape[dim + 1 :])
        for bit in axis_bits(axis):
            other = swap(held, axis, bit)
            upper = (lax.axis_index(axis) & bit) != 0
            low = jnp.where(upper, other, held)
            high = jnp.where(upper, held, other)
            held = jnp.concatenate([low, high], axis=dim + 1)
            shape = held.shape
            held = held.reshape(*shape[:dim], shape[dim] * shape[dim + 1], 1, *shape[dim + 2 :])
        shape = held.shape
        held = held.reshape(*shape[: dim + 1], *shape[dim + 2 :])
    return held.reshape(-1, array.shape[-1])


def split_terms(array):
    high = lax.reduce_precision(array, 8, 7)
    return high.astype(jnp.bfloat16), (array - high).astype(jnp.bfloat16)


def invert(system):
    size = system.shape[0]
    lanes = lax.broadcasted_iota(jnp.int32, (ROWS, size), 1)
    subs = lax.broadcasted_iota(jnp.int32, (ROWS, size), 0)
    rows = [system[r : r + ROWS] for r in range(0, size, ROWS)]

    def column(block, at):
        return jnp.broadcast_to(block[:, at : at + 1], (ROWS, size))

    for panel in range(size // ROWS):
        first = panel * ROWS
        inside = (lanes >= first) & (lanes < first + ROWS)
        unit = (lanes - first == subs).astype(jnp.float32)
        work = [column(rows[panel], first + c) for c in range(ROWS)]
        work.append(jnp.where(inside, unit, rows[panel]))
        for k in range(0, ROWS, 2):
            p, q = work[k], work[k + 1]
            a, b, d = p[k : k + 1], q[k : k + 1], q[k + 1 : k + 2]
            scale = 1.0 / (a * d - b * b)
            a, b, d = a * scale, b * scale, d * scale
            for c in range(k + 2, ROWS + 1):
                upper, lower = work[c][k : k + 1], work[c][k + 1 : k + 2]
                top = d * upper - b * lower
                low = a * lower - b * upper
                rest = work[c] - p * top - q * low
                work[c] = jnp.where(subs == k, top, jnp.where(subs == k + 1, low, rest))
        solved = work[ROWS]
        for r in range(len(rows)):
            if r == panel:
                continue
            old = rows[r]
            new = jnp.where(inside, 0.0, old)
            for c in range(ROWS):
                new = new - column(old, first + c) * solved[c : c + 1]
            rows[r] = new
        rows[panel] = solved
    return jnp.concatenate(rows, axis=0)


def spd_inverse(system):
    square = lax.dot_general(
        system, system, ROW_ROW, precision=HIGHEST, preferred_element_type=jnp.float32
    )
    return invert(square)


def local_kernel(
    chunks,
    shares,
    field_hbm,
    last_x_hbm,
    last_y_hbm,
    right_y_hbm,
    right_m_hbm,
    last_m_hbm,
    last_part,
    first_part,
    *refs,
):
    count = (shares - 1) * PARTS
    terms_hbm = refs[:count]
    field, last_x, last_y, right_y, right_m, last_m, terms, sems, out_sems = refs[count:]
    x_cells, y_cells, m_cells = field.shape
    step = x_cells // chunks
    y_share = y_cells // shares
    parts = [pl.ds(n * step, step) for n in range(chunks)]
    copies = [
        pltpu.make_async_copy(last_m_hbm, last_m, sems.at[0]),
        pltpu.make_async_copy(field_hbm.at[parts[0]], field.at[parts[0]], sems.at[1]),
        pltpu.make_async_copy(last_x_hbm, last_x, sems.at[2]),
        pltpu.make_async_copy(last_y_hbm, last_y, sems.at[3]),
        pltpu.make_async_copy(right_m_hbm, right_m, sems.at[4]),
        pltpu.make_async_copy(right_y_hbm, right_y, sems.at[5]),
    ]
    for n in range(1, chunks):
        copies.append(
            pltpu.make_async_copy(field_hbm.at[parts[n]], field.at[parts[n]], sems.at[5 + n])
        )
    for copy in copies:
        copy.start()
    here = lax.axis_index("gz")
    leaving = []
    copies[0].wait()
    for n in range(chunks):
        copies[5 + n if n else 1].wait()
        for s in range(1, shares):
            start = pl.multiple_of((here ^ s) * y_share, y_share)
            rows = field[parts[n], pl.ds(start, y_share), :].reshape(step * y_share, m_cells)
            term = jnp.dot(rows, last_m[...], preferred_element_type=jnp.float32)
            terms[s - 1, parts[n]] = term.reshape(step, y_share, -1)
            part, at = divmod(n * step, x_cells // PARTS)
            leaving.append(
                pltpu.make_async_copy(
                    terms.at[s - 1, parts[n]],
                    terms_hbm[(s - 1) * PARTS + part].at[pl.ds(at, step)],
                    out_sems.at[s - 1, n],
                )
            )
            leaving[-1].start()

    for copy in copies[2:6]:
        copy.wait()
    for n in range(chunks):
        rows = field[parts[n]].reshape(step * y_cells, m_cells)
        left = last_x[parts[n]].astype(jnp.float32)[:, None, :]
        khatri = left * last_y[...].astype(jnp.float32)[None]
        khatri = khatri.astype(jnp.bfloat16).reshape(step * y_cells, -1)
        part = lax.dot_general(khatri, rows, COL_COL, preferred_element_type=jnp.float32)
        if n == 0:
            last_part[...] = part
        else:
            last_part[...] += part
        first = jnp.dot(rows, right_m[...], preferred_element_type=jnp.float32)
        first = first.reshape(step, y_cells, -1) * right_y[...].astype(jnp.float32)[None]
        first_part[parts[n], :] = jnp.sum(first, axis=1)
    for copy in leaving:
        copy.wait()


def local_products(shares, field, last_x, last_y, right_y, right_m, last_m):
    x_cells, y_cells, m_cells = field.shape
    rank, cols = last_x.shape[1], last_m.shape[1]
    chunks = max(x_cells // 8, 1)
    inputs = (field, last_x, last_y, right_y, right_m, last_m)
    dims = (x_cells, y_cells // shares, cols)
    part_dims = (x_cells // PARTS, *dims[1:])
    hbm = pl.BlockSpec(memory_space=pltpu.HBM)
    vmem = pl.BlockSpec(memory_space=pltpu.VMEM)
    return pl.pallas_call(
        functools.partial(local_kernel, chunks, shares),
        in_specs=[hbm] * len(inputs),
        out_specs=[vmem, vmem, *([hbm] * ((shares - 1) * PARTS))],
        out_shape=[
            jax.ShapeDtypeStruct((rank, m_cells), jnp.float32),
            jax.ShapeDtypeStruct((x_cells, cols), jnp.float32),
            *([jax.ShapeDtypeStruct(part_dims, jnp.float32)] * ((shares - 1) * PARTS)),
        ],
        scratch_shapes=[
            *(pltpu.VMEM(x.shape, x.dtype) for x in inputs),
            pltpu.VMEM((shares - 1, *dims), jnp.float32),
            pltpu.SemaphoreType.DMA((5 + chunks,)),
            pltpu.SemaphoreType.DMA((shares - 1, chunks)),
        ],
        compiler_params=pltpu.CompilerParams(vmem_limit_bytes=LOCAL_VMEM_BYTES),
        name="local_products",
    )(*inputs)


def two_terms(array):
    high = array.astype(jnp.bfloat16)
    return high, (array - high.astype(jnp.float32)).astype(jnp.bfloat16)


def inverse_kernel(system_shares, pinv):
    system = system_shares[:, 0]
    for k in range(1, system_shares.shape[1]):
        system = system + system_shares[:, k]
    system = system.reshape(-1, system.shape[-1])
    cols = system.shape[1]
    high, low = two_terms(spd_inverse(system))
    system_high, system_low = two_terms(system)
    both = jnp.dot(
        high,
        jnp.concatenate([system_high, system_low], axis=1),
        preferred_element_type=jnp.float32,
    )
    rest = jnp.dot(low, system_high, preferred_element_type=jnp.float32)
    pinv[...] = both[:, :cols] + (both[:, cols:] + rest)


def pseudo_inverse(system_shares):
    rank = system_shares.shape[0] * system_shares.shape[2]
    return pl.pallas_call(
        inverse_kernel,
        out_shape=jax.ShapeDtypeStruct((rank, system_shares.shape[3]), jnp.float32),
        compiler_params=pltpu.CompilerParams(vmem_limit_bytes=VMEM_BYTES),
        name="pseudo_inverse",
    )(system_shares)


def project_kernel(y_own, pinv, kept, *refs):
    *terms, projected, flat = refs
    rank = pinv.shape[0]
    pinv_high, pinv_low = two_terms(pinv[...])
    pinv_both = jnp.concatenate([pinv_high, pinv_low], axis=0)
    rows = flat.shape[0] // PARTS
    x_cells, y_cells, _ = kept.shape
    x_part = x_cells // PARTS
    for part in range(PARTS):
        total = kept[part * x_part : (part + 1) * x_part]
        for term in terms[part::PARTS]:
            total = total + term[...]
        high, low = two_terms(total.reshape(rows, -1))
        both = lax.dot_general(high, pinv_both, ROW_ROW, preferred_element_type=jnp.float32)
        rest = lax.dot_general(low, pinv_high, ROW_ROW, preferred_element_type=jnp.float32)
        flat[part * rows : (part + 1) * rows] = both[:, :rank] + (both[:, rank:] + rest)
    for b in range(projected.shape[0]):
        for j in range(y_own):
            projected[b, j * x_cells : (j + 1) * x_cells] = flat[
                pl.ds(b * y_own + j, x_cells, stride=y_cells), :
            ]


def project(blocks, pinv, kept, terms):
    rank = pinv.shape[0]
    x_cells, y_cells, _ = kept.shape
    y_own = y_cells // blocks
    rows = y_own * x_cells
    return pl.pallas_call(
        functools.partial(project_kernel, y_own),
        out_shape=jax.ShapeDtypeStruct((blocks, rows, rank), jnp.float32),
        scratch_shapes=[pltpu.VMEM((x_cells * y_cells, rank), jnp.float32)],
        compiler_params=pltpu.CompilerParams(vmem_limit_bytes=VMEM_BYTES),
        name="project",
    )(pinv, kept, *terms)


def packed_units(packed, unit):
    return [(k, n * unit) for k in range(packed.shape[0]) for n in range(2)]


def sketch_kernel(order, left_at, unit, pieces, packed, out):
    me = lax.axis_index("gx")
    _, rows, cols = pieces.shape
    x_cells = unit - left_at
    weights = jnp.concatenate(
        [packed[k, at + left_at : at + unit] for k, at in packed_units(packed, unit)], axis=0
    )
    weights = weights.astype(jnp.bfloat16)
    for j in range(rows // x_cells):
        column = jnp.concatenate(
            [pieces[me ^ o, j * x_cells : (j + 1) * x_cells] for o in order], axis=0
        )
        both = lax.dot_general(
            weights,
            jnp.concatenate(two_terms(column), axis=1),
            COL_COL,
            preferred_element_type=jnp.float32,
        )
        both = both[:, :cols] + both[:, cols:]
        out[:, j] = both.reshape(out.shape[0], out.shape[2], cols)


def sketch(order, left_at, unit, own, pieces, packed):
    _, rows, cols = pieces.shape
    rank = packed.shape[2]
    y_own = rows // (unit - left_at)
    return pl.pallas_call(
        functools.partial(sketch_kernel, order, left_at, unit),
        out_shape=jax.ShapeDtypeStruct((rank // own, y_own, own, cols), jnp.float32),
        compiler_params=pltpu.CompilerParams(vmem_limit_bytes=VMEM_BYTES),
        name="sketch",
    )(pieces, packed)


def first_sums_kernel(left_at, unit, rows, packed, sums, extra):
    x_cells, cols = rows.shape
    units = packed_units(packed, unit)
    left = jnp.concatenate([packed[k, at + left_at : at + unit] for k, at in units], axis=0)
    sums[:x_cells] = rows[...]
    for c in range(cols // LANES):
        first = c * x_cells
        sums[x_cells:, c * LANES : (c + 1) * LANES] = lax.dot_general(
            left,
            jnp.concatenate(
                [packed[k, at + first : at + first + x_cells] for k, at in units], axis=0
            ),
            COL_COL,
            precision=HIGHEST,
            preferred_element_type=jnp.float32,
        )
    extra[...] = packed[:, 2 * unit :]


def first_sums(left_at, unit, rows, packed):
    entries, height, rank = packed.shape
    return pl.pallas_call(
        functools.partial(first_sums_kernel, left_at, unit),
        out_shape=(
            jax.ShapeDtypeStruct((rows.shape[0] + rank, rows.shape[1]), jnp.float32),
            jax.ShapeDtypeStruct((entries, height - 2 * unit, rank), jnp.float32),
        ),
        compiler_params=pltpu.CompilerParams(vmem_limit_bytes=VMEM_BYTES),
        name="first_sums",
    )(rows, packed)


def first_kernel(*refs):
    *sums, core_first = refs
    x_cells = core_first.shape[0]
    total = sums[0][...]
    for other in sums[1:]:
        total = total + other[...]
    system = total[x_cells:]
    inverse = spd_inverse(system)
    scores = lax.dot_general(
        total[:x_cells], system, ROW_ROW, precision=HIGHEST, preferred_element_type=jnp.float32
    )
    core_first[...] = jnp.dot(
        scores, inverse, precision=HIGHEST, preferred_element_type=jnp.float32
    )


def solve_first(x_cells, *sums):
    return pl.pallas_call(
        first_kernel,
        out_shape=jax.ShapeDtypeStruct((x_cells, sums[0].shape[0] - x_cells), jnp.float32),
        compiler_params=pltpu.CompilerParams(vmem_limit_bytes=VMEM_BYTES),
        name="solve_first",
    )(*sums)


def place_kernel(own, outer_order, *refs):
    *parts, core_last = refs
    outer, inner = lax.axis_index("gx"), lax.axis_index("gy")
    for i, part in enumerate(parts):
        for k, o in enumerate(outer_order):
            at = ((outer ^ o) * len(parts) + (inner ^ i)) * own
            at = pl.multiple_of(at, own)
            for c in range(part.shape[1] // own):
                core_last[pl.ds(at, own), c * LANES : (c + 1) * LANES] = part[
                    k, c * own : (c + 1) * own
                ]


def place(own, outer_order, parts):
    outer, rows, lanes = parts[0].shape
    return pl.pallas_call(
        functools.partial(place_kernel, own, outer_order),
        out_shape=jax.ShapeDtypeStruct(
            (len(parts) * outer * own, rows // own * lanes), jnp.float32
        ),
        compiler_params=pltpu.CompilerParams(vmem_limit_bytes=VMEM_BYTES),
        name="place",
    )(*parts)


def per_device(flow_field, left_x, last_x, last_y, right_y, right_m, last_m):
    x_cells, y_cells, m_cells = flow_field.shape
    rank = left_x.shape[1]
    cols = right_m.shape[1]
    blocks, shares = lax.axis_size("gx"), lax.axis_size("gz")
    y_share = y_cells // shares
    y_own = y_share // blocks

    last_part, first_part, *terms = local_products(
        shares, flow_field, last_x, last_y, right_y, right_m, last_m
    )

    terms = [swap(term, "gz", 1 + at // PARTS) for at, term in enumerate(terms)]
    here = lax.axis_index("gz")
    kept = flow_field.reshape(x_cells, shares, y_share, m_cells)
    kept = lax.dynamic_index_in_dim(kept, here, 1, False).reshape(-1, m_cells)
    kept = jnp.dot(kept, last_m, preferred_element_type=jnp.float32)
    kept = kept.reshape(x_cells, y_share, cols)

    packed = jnp.concatenate(
        [
            first_part.reshape(x_cells, -1, LANES).transpose(1, 0, 2).reshape(-1, LANES),
            left_x.astype(jnp.float32),
        ],
        axis=0,
    )
    unit = packed.shape[0]
    left_at = unit - x_cells
    packed = jnp.concatenate([packed, swap(packed, "gx", 1)], axis=0)

    group = ("gx", "gy")
    own = rank // lax.axis_size(group)
    last_rows = lax.all_to_all(last_part.reshape(-1, own, m_cells), group, 0, 0, tiled=True)
    last_rows = jnp.sum(after(last_rows, *terms[::PARTS]), axis=0)
    both = jnp.dot(
        jnp.concatenate(split_terms(last_rows), axis=0), last_m, preferred_element_type=jnp.float32
    )
    both = after(both[:own] + both[own:], packed, kept)
    count = lax.axis_size(ALL)
    copies = jnp.broadcast_to(both[None], (count, own, cols))
    system = lax.all_to_all(copies, ALL, 0, 0, tiled=True).reshape(-1, shares, own, cols)
    if own % ROWS:
        system = jnp.sum(system, axis=1).reshape(-1, 1, ROWS, cols)

    if own % ROWS:
        extra = jnp.zeros((ROWS, LANES), jnp.float32)
    else:
        extra = last_rows.reshape(own, -1, LANES).transpose(1, 0, 2).reshape(-1, LANES)
    packed = jnp.concatenate([packed, extra], axis=0)[None]
    *bits, _ = axis_bits("gx")
    others = [0]
    for bit in bits:
        if bit == bits[-1]:
            system = after(system, packed)
        packed = swap_step(packed, "gx", bit)
        others += [o ^ bit for o in others]
    order = [o ^ n for o in others for n in range(2)]

    pinv = pseudo_inverse(after(system, *terms))
    projected = after(project(blocks, pinv, kept, terms), packed)
    sums, extra = first_sums(left_at, unit, first_part, packed)
    sums = swap_sum(sums, "gz")
    sums = [swap(sums, "gy", y) if y else sums for y in range(lax.axis_size("gy"))]

    pieces = lax.all_to_all(projected, "gx", 0, 0, tiled=True)
    group = ("gx", "gz")
    devices = lax.axis_size(group)
    rank_own = rank // devices
    if rank_own % ROWS:
        middle = sketch(order, left_at, unit, rank, pieces, packed)
        middle = middle.reshape(y_own, devices, rank_own, rank).transpose(1, 0, 2, 3)
    else:
        middle = sketch(order, left_at, unit, rank_own, pieces, packed)
    extra = jnp.concatenate([extra, swap(extra, "gx", 1)], axis=0)
    middle = after(middle, extra, *sums)
    received = lax.all_to_all(middle, group, 0, 0, tiled=True)
    received = received.reshape(blocks, shares, y_own, rank_own, rank)
    core_middle = received.transpose(3, 1, 0, 2, 4).reshape(rank_own, y_cells, rank)

    if own % ROWS:
        core_last = gather_rows(last_rows, "gx", "gy")
    else:
        outer = [o ^ n for n in range(2) for o in others]
        inner = range(lax.axis_size("gy"))
        core_last = place(own, outer, [swap(extra, "gy", i) if i else extra for i in inner])
    core_first = solve_first(x_cells, after(sums[0], middle), *sums[1:])
    return (core_first, core_middle, core_last)


def solution(mesh):
    return jax.shard_map(
        per_device,
        mesh=mesh,
        in_specs=(
            P("gx", "gy", "gz"),
            P("gx", None),
            P("gx", None),
            P("gy", None),
            P("gy", None),
            P("gz", None),
            P("gz", None),
        ),
        out_specs=(P("gx", None), P(("gx", "gz"), "gy", None), P(None, "gz")),
        check_vma=False,
    )
```

```python
import functools

import jax
import jax.numpy as jnp
from jax import lax
from jax.experimental import pallas as pl
from jax.experimental.pallas import tpu as pltpu
from jax.sharding import PartitionSpec as P

ALL = ("gx", "gy", "gz")
HIGHEST = lax.Precision.HIGHEST
VMEM_BYTES = 48 * 1024 * 1024
LOCAL_VMEM_BYTES = 63 * 1024 * 1024
ROWS = 8
LANES = 128
PARTS = 2
ROW_ROW = (((1,), (1,)), ((), ()))
COL_COL = (((0,), (0,)), ((), ()))


def gather_bits(axis):
    *bits, last = axis_bits(axis)
    return [last, *bits]


def axis_bits(axis):
    bit = lax.axis_size(axis) // 2
    while bit:
        yield bit
        bit //= 2


def swap(array, axis, bits):
    return lax.ppermute(array, axis, [(s, s ^ bits) for s in range(lax.axis_size(axis))])


def swap_sum(array, axis):
    for bit in axis_bits(axis):
        array = array + swap(array, axis, bit)
    return array


def after(value, *others):
    value, *_ = lax.optimization_barrier((value, *others))
    return value


def swap_order(axis):
    order = [0]
    for bit in gather_bits(axis):
        order += [o ^ bit for o in order]
    return order


def swap_step(held, axis, bit):
    return jnp.concatenate([held, swap(held, axis, bit)], axis=0)


def gather_rows(array, outer, inner):
    held = array[None, None]
    for dim, axis in ((0, outer), (1, inner)):
        shape = held.shape
        held = held.reshape(*shape[:dim], 1, 1, *shape[dim + 1 :])
        for bit in axis_bits(axis):
            other = swap(held, axis, bit)
            upper = (lax.axis_index(axis) & bit) != 0
            low = jnp.where(upper, other, held)
            high = jnp.where(upper, held, other)
            held = jnp.concatenate([low, high], axis=dim + 1)
            shape = held.shape
            held = held.reshape(*shape[:dim], shape[dim] * shape[dim + 1], 1, *shape[dim + 2 :])
        shape = held.shape
        held = held.reshape(*shape[: dim + 1], *shape[dim + 2 :])
    return held.reshape(-1, array.shape[-1])


def split_terms(array):
    high = lax.reduce_precision(array, 8, 7)
    return high.astype(jnp.bfloat16), (array - high).astype(jnp.bfloat16)


def invert(system):
    size = system.shape[0]
    lanes = lax.broadcasted_iota(jnp.int32, (ROWS, size), 1)
    subs = lax.broadcasted_iota(jnp.int32, (ROWS, size), 0)
    rows = [system[r : r + ROWS] for r in range(0, size, ROWS)]

    def column(block, at):
        return jnp.broadcast_to(block[:, at : at + 1], (ROWS, size))

    for panel in range(size // ROWS):
        first = panel * ROWS
        inside = (lanes >= first) & (lanes < first + ROWS)
        unit = (lanes - first == subs).astype(jnp.float32)
        work = [column(rows[panel], first + c) for c in range(ROWS)]
        work.append(jnp.where(inside, unit, rows[panel]))
        for k in range(0, ROWS, 2):
            p, q = work[k], work[k + 1]
            a, b, d = p[k : k + 1], q[k : k + 1], q[k + 1 : k + 2]
            scale = 1.0 / (a * d - b * b)
            a, b, d = a * scale, b * scale, d * scale
            for c in range(k + 2, ROWS + 1):
                upper, lower = work[c][k : k + 1], work[c][k + 1 : k + 2]
                top = d * upper - b * lower
                low = a * lower - b * upper
                rest = work[c] - p * top - q * low
                work[c] = jnp.where(subs == k, top, jnp.where(subs == k + 1, low, rest))
        solved = work[ROWS]
        signs = jnp.where(inside, 0.0, jnp.where(lanes < first, -1.0, 1.0))
        update = lax.dot_general(
            signs * rows[panel],
            solved,
            COL_COL,
            precision=HIGHEST,
            preferred_element_type=jnp.float32,
        )
        for r in range(len(rows)):
            if r == panel:
                rows[r] = solved
                continue
            old = rows[r]
            new = jnp.where(inside, 0.0, old)
            if r == panel + 1:
                for c in range(ROWS):
                    new = new - column(old, first + c) * solved[c : c + 1]
            else:
                new = new - update[r * ROWS : (r + 1) * ROWS]
            rows[r] = new
    return jnp.concatenate(rows, axis=0)


def spd_inverse(system):
    square = lax.dot_general(
        system, system, ROW_ROW, precision=HIGHEST, preferred_element_type=jnp.float32
    )
    return invert(square)


def local_kernel(
    chunks,
    shares,
    field_hbm,
    last_x_hbm,
    last_y_hbm,
    right_y_hbm,
    right_m_hbm,
    last_m_hbm,
    last_part,
    first_part,
    *refs,
):
    count = (shares - 1) * PARTS
    terms_hbm = refs[:count]
    field, last_x, last_y, right_y, right_m, last_m, terms, sems, out_sems = refs[count:]
    x_cells, y_cells, m_cells = field.shape
    step = x_cells // chunks
    y_share = y_cells // shares
    parts = [pl.ds(n * step, step) for n in range(chunks)]
    copies = [
        pltpu.make_async_copy(last_m_hbm, last_m, sems.at[0]),
        pltpu.make_async_copy(field_hbm.at[parts[0]], field.at[parts[0]], sems.at[1]),
        pltpu.make_async_copy(last_x_hbm, last_x, sems.at[2]),
        pltpu.make_async_copy(last_y_hbm, last_y, sems.at[3]),
        pltpu.make_async_copy(right_m_hbm, right_m, sems.at[4]),
        pltpu.make_async_copy(right_y_hbm, right_y, sems.at[5]),
    ]
    for n in range(1, chunks):
        copies.append(
            pltpu.make_async_copy(field_hbm.at[parts[n]], field.at[parts[n]], sems.at[5 + n])
        )
    for copy in copies:
        copy.start()
    here = lax.axis_index("gz")
    leaving = []
    copies[0].wait()
    for n in range(chunks):
        copies[5 + n if n else 1].wait()
        for s in range(1, shares):
            start = pl.multiple_of((here ^ s) * y_share, y_share)
            rows = field[parts[n], pl.ds(start, y_share), :].reshape(step * y_share, m_cells)
            term = jnp.dot(rows, last_m[...], preferred_element_type=jnp.float32)
            terms[s - 1, parts[n]] = term.reshape(step, y_share, -1)
            part, at = divmod(n * step, x_cells // PARTS)
            leaving.append(
                pltpu.make_async_copy(
                    terms.at[s - 1, parts[n]],
                    terms_hbm[(s - 1) * PARTS + part].at[pl.ds(at, step)],
                    out_sems.at[s - 1, n],
                )
            )
            leaving[-1].start()

    for copy in copies[2:6]:
        copy.wait()
    for n in range(chunks):
        rows = field[parts[n]].reshape(step * y_cells, m_cells)
        left = last_x[parts[n]].astype(jnp.float32)[:, None, :]
        khatri = left * last_y[...].astype(jnp.float32)[None]
        khatri = khatri.astype(jnp.bfloat16).reshape(step * y_cells, -1)
        part = lax.dot_general(khatri, rows, COL_COL, preferred_element_type=jnp.float32)
        if n == 0:
            last_part[...] = part
        else:
            last_part[...] += part
        first = jnp.dot(rows, right_m[...], preferred_element_type=jnp.float32)
        first = first.reshape(step, y_cells, -1) * right_y[...].astype(jnp.float32)[None]
        first_part[parts[n], :] = jnp.sum(first, axis=1)
    for copy in leaving:
        copy.wait()


def local_products(shares, field, last_x, last_y, right_y, right_m, last_m):
    x_cells, y_cells, m_cells = field.shape
    rank, cols = last_x.shape[1], last_m.shape[1]
    chunks = max(x_cells // 8, 1)
    inputs = (field, last_x, last_y, right_y, right_m, last_m)
    dims = (x_cells, y_cells // shares, cols)
    part_dims = (x_cells // PARTS, *dims[1:])
    hbm = pl.BlockSpec(memory_space=pltpu.HBM)
    vmem = pl.BlockSpec(memory_space=pltpu.VMEM)
    return pl.pallas_call(
        functools.partial(local_kernel, chunks, shares),
        in_specs=[hbm] * len(inputs),
        out_specs=[vmem, vmem, *([hbm] * ((shares - 1) * PARTS))],
        out_shape=[
            jax.ShapeDtypeStruct((rank, m_cells), jnp.float32),
            jax.ShapeDtypeStruct((x_cells, cols), jnp.float32),
            *([jax.ShapeDtypeStruct(part_dims, jnp.float32)] * ((shares - 1) * PARTS)),
        ],
        scratch_shapes=[
            *(pltpu.VMEM(x.shape, x.dtype) for x in inputs),
            pltpu.VMEM((shares - 1, *dims), jnp.float32),
            pltpu.SemaphoreType.DMA((5 + chunks,)),
            pltpu.SemaphoreType.DMA((shares - 1, chunks)),
        ],
        compiler_params=pltpu.CompilerParams(vmem_limit_bytes=LOCAL_VMEM_BYTES),
        name="local_products",
    )(*inputs)


def two_terms(array):
    high = array.astype(jnp.bfloat16)
    return high, (array - high.astype(jnp.float32)).astype(jnp.bfloat16)


def inverse_kernel(system_shares, pinv):
    system = system_shares[:, 0]
    for k in range(1, system_shares.shape[1]):
        system = system + system_shares[:, k]
    system = system.reshape(-1, system.shape[-1])
    cols = system.shape[1]
    high, low = two_terms(spd_inverse(system))
    system_high, system_low = two_terms(system)
    both = jnp.dot(
        high,
        jnp.concatenate([system_high, system_low], axis=1),
        preferred_element_type=jnp.float32,
    )
    rest = jnp.dot(low, system_high, preferred_element_type=jnp.float32)
    pinv[...] = both[:, :cols] + (both[:, cols:] + rest)


def pseudo_inverse(system_shares):
    rank = system_shares.shape[0] * system_shares.shape[2]
    return pl.pallas_call(
        inverse_kernel,
        out_shape=jax.ShapeDtypeStruct((rank, system_shares.shape[3]), jnp.float32),
        compiler_params=pltpu.CompilerParams(vmem_limit_bytes=VMEM_BYTES),
        name="pseudo_inverse",
    )(system_shares)


def project_kernel(y_own, pinv, extra, kept, *refs):
    *terms, projected, flat = refs
    rank = pinv.shape[0]
    pinv_high, pinv_low = two_terms(pinv[...])
    pinv_both = jnp.concatenate([pinv_high, pinv_low], axis=0)
    rows = flat.shape[0] // PARTS
    x_cells, y_cells, _ = kept.shape
    x_part = x_cells // PARTS
    for part in range(PARTS):
        total = kept[part * x_part : (part + 1) * x_part]
        for term in terms[part::PARTS]:
            total = total + term[...]
        high, low = two_terms(total.reshape(rows, -1))
        both = lax.dot_general(high, pinv_both, ROW_ROW, preferred_element_type=jnp.float32)
        rest = lax.dot_general(low, pinv_high, ROW_ROW, preferred_element_type=jnp.float32)
        flat[part * rows : (part + 1) * rows] = both[:, :rank] + (both[:, rank:] + rest)
    for b in range(projected.shape[0]):
        for j in range(y_own):
            projected[b, j * x_cells : (j + 1) * x_cells] = flat[
                pl.ds(b * y_own + j, x_cells, stride=y_cells), :
            ]
        projected[b, y_own * x_cells :] = extra[...]


def project(blocks, pinv, extra, kept, terms):
    rank = pinv.shape[0]
    x_cells, y_cells, _ = kept.shape
    y_own = y_cells // blocks
    rows = y_own * x_cells + extra.shape[0]
    return pl.pallas_call(
        functools.partial(project_kernel, y_own),
        out_shape=jax.ShapeDtypeStruct((blocks, rows, rank), jnp.float32),
        scratch_shapes=[pltpu.VMEM((x_cells * y_cells, rank), jnp.float32)],
        compiler_params=pltpu.CompilerParams(vmem_limit_bytes=VMEM_BYTES),
        name="project",
    )(pinv, extra, kept, *terms)


def sketch_kernel(order, left_at, y_own, pieces, packed, out, extra):
    me = lax.axis_index("gx")
    blocks, _, cols = pieces.shape
    x_cells = packed.shape[1] - left_at
    weights = jnp.concatenate([packed[k, left_at:] for k in range(blocks)], axis=0)
    weights = weights.astype(jnp.bfloat16)
    for j in range(y_own):
        column = jnp.concatenate(
            [pieces[me ^ o, j * x_cells : (j + 1) * x_cells] for o in order], axis=0
        )
        high = column.astype(jnp.bfloat16)
        low = (column - high.astype(jnp.float32)).astype(jnp.bfloat16)
        both = lax.dot_general(
            weights,
            jnp.concatenate([high, low], axis=1),
            COL_COL,
            preferred_element_type=jnp.float32,
        )
        both = both[:, :cols] + both[:, cols:]
        out[:, j] = both.reshape(out.shape[0], out.shape[2], cols)
    extra[...] = pieces[:, y_own * x_cells :]


def sketch(order, left_at, y_own, own, pieces, packed):
    blocks, rows, cols = pieces.shape
    rank = packed.shape[2]
    extra = rows - y_own * (packed.shape[1] - left_at)
    return pl.pallas_call(
        functools.partial(sketch_kernel, order, left_at, y_own),
        out_shape=(
            jax.ShapeDtypeStruct((rank // own, y_own, own, cols), jnp.float32),
            jax.ShapeDtypeStruct((blocks, extra, cols), jnp.float32),
        ),
        compiler_params=pltpu.CompilerParams(vmem_limit_bytes=VMEM_BYTES),
        name="sketch",
    )(pieces, packed)


def first_sums_kernel(left_at, rows, packed, sums):
    x_cells, cols = rows.shape
    blocks = range(packed.shape[0])
    left = jnp.concatenate([packed[k, left_at : left_at + x_cells] for k in blocks], axis=0)
    sums[:x_cells] = rows[...]
    for c in range(cols // LANES):
        at = c * x_cells
        sums[x_cells:, c * LANES : (c + 1) * LANES] = lax.dot_general(
            left,
            jnp.concatenate([packed[k, at : at + x_cells] for k in blocks], axis=0),
            COL_COL,
            precision=HIGHEST,
            preferred_element_type=jnp.float32,
        )


def first_sums(left_at, rows, packed):
    return pl.pallas_call(
        functools.partial(first_sums_kernel, left_at),
        out_shape=jax.ShapeDtypeStruct(
            (rows.shape[0] + packed.shape[2], rows.shape[1]), jnp.float32
        ),
        compiler_params=pltpu.CompilerParams(vmem_limit_bytes=VMEM_BYTES),
        name="first_sums",
    )(rows, packed)


def first_kernel(*refs):
    *sums, core_first = refs
    x_cells = core_first.shape[0]
    total = sums[0][...]
    for other in sums[1:]:
        total = total + other[...]
    system = total[x_cells:]
    inverse = spd_inverse(system)
    scores = lax.dot_general(
        total[:x_cells], system, ROW_ROW, precision=HIGHEST, preferred_element_type=jnp.float32
    )
    core_first[...] = jnp.dot(
        scores, inverse, precision=HIGHEST, preferred_element_type=jnp.float32
    )


def solve_first(x_cells, *sums):
    return pl.pallas_call(
        first_kernel,
        out_shape=jax.ShapeDtypeStruct((x_cells, sums[0].shape[0] - x_cells), jnp.float32),
        compiler_params=pltpu.CompilerParams(vmem_limit_bytes=VMEM_BYTES),
        name="solve_first",
    )(*sums)


def place_kernel(own, inner_order, *refs):
    *parts, core_last = refs
    inner = lax.axis_index("gy")
    for part, i in zip(parts, inner_order):
        for o in range(part.shape[0]):
            at = pl.multiple_of((o * len(parts) + (inner ^ i)) * own, own)
            for c in range(part.shape[1] // own):
                core_last[pl.ds(at, own), c * LANES : (c + 1) * LANES] = part[
                    o, c * own : (c + 1) * own
                ]


def place(own, inner_order, parts):
    outer, rows, lanes = parts[0].shape
    return pl.pallas_call(
        functools.partial(place_kernel, own, inner_order),
        out_shape=jax.ShapeDtypeStruct(
            (len(parts) * outer * own, rows // own * lanes), jnp.float32
        ),
        compiler_params=pltpu.CompilerParams(vmem_limit_bytes=VMEM_BYTES),
        name="place",
    )(*parts)


def per_device(flow_field, left_x, last_x, last_y, right_y, right_m, last_m):
    x_cells, y_cells, m_cells = flow_field.shape
    rank = left_x.shape[1]
    cols = right_m.shape[1]
    blocks, shares = lax.axis_size("gx"), lax.axis_size("gz")
    y_share = y_cells // shares
    y_own = y_share // blocks

    last_part, first_part, *terms = local_products(
        shares, flow_field, last_x, last_y, right_y, right_m, last_m
    )

    terms = [swap(term, "gz", 1 + at // PARTS) for at, term in enumerate(terms)]
    here = lax.axis_index("gz")
    kept = flow_field.reshape(x_cells, shares, y_share, m_cells)
    kept = lax.dynamic_index_in_dim(kept, here, 1, False).reshape(-1, m_cells)
    kept = jnp.dot(kept, last_m, preferred_element_type=jnp.float32)
    kept = kept.reshape(x_cells, y_share, cols)

    order = swap_order("gx")
    packed = jnp.concatenate(
        [
            first_part.reshape(x_cells, -1, LANES).transpose(1, 0, 2).reshape(-1, LANES),
            left_x.astype(jnp.float32),
        ],
        axis=0,
    )[None]
    left_at = x_cells * cols // LANES
    first_bit, *bits = gather_bits("gx")
    packed = swap_step(packed, "gx", first_bit)

    group = ("gx", "gy")
    own = rank // lax.axis_size(group)
    last_rows = lax.all_to_all(last_part.reshape(-1, own, m_cells), group, 0, 0, tiled=True)
    last_rows = jnp.sum(after(last_rows, *terms[::PARTS]), axis=0)
    both = jnp.dot(
        jnp.concatenate(split_terms(last_rows), axis=0), last_m, preferred_element_type=jnp.float32
    )
    both = after(both[:own] + both[own:], packed, kept)
    count = lax.axis_size(ALL)
    copies = jnp.broadcast_to(both[None], (count, own, cols))
    system = lax.all_to_all(copies, ALL, 0, 0, tiled=True).reshape(-1, shares, own, cols)
    if own % ROWS:
        system = jnp.sum(system, axis=1).reshape(-1, 1, ROWS, cols)

    for bit in bits:
        packed = swap_step(packed, "gx", bit)
    sums = first_sums(left_at, first_part, packed)
    if own % ROWS:
        extra = jnp.zeros((ROWS, LANES), jnp.float32)
    else:
        extra = last_rows.reshape(own, -1, LANES).transpose(1, 0, 2).reshape(-1, LANES)
    pinv = pseudo_inverse(after(system, packed, *terms))
    projected = project(blocks, pinv, extra, kept, terms)
    sums = swap_sum(sums, "gz")
    sums = [swap(sums, "gy", y) if y else sums for y in range(lax.axis_size("gy"))]

    pieces = lax.all_to_all(projected, "gx", 0, 0, tiled=True)
    core_first = solve_first(x_cells, after(sums[0], projected), *sums[1:])
    group = ("gx", "gz")
    devices = lax.axis_size(group)
    rank_own = rank // devices
    if rank_own % ROWS:
        middle, extra = sketch(order, left_at, y_own, rank, pieces, packed)
        middle = middle.reshape(y_own, devices, rank_own, rank).transpose(1, 0, 2, 3)
    else:
        middle, extra = sketch(order, left_at, y_own, rank_own, pieces, packed)
    middle, core_first = lax.optimization_barrier((middle, core_first))
    received = lax.all_to_all(middle, group, 0, 0, tiled=True)
    received = received.reshape(blocks, shares, y_own, rank_own, rank)
    core_middle = received.transpose(3, 1, 0, 2, 4).reshape(rank_own, y_cells, rank)

    if own % ROWS:
        core_last = gather_rows(last_rows, "gx", "gy")
    else:
        inner = range(lax.axis_size("gy"))
        core_last = place(own, inner, [swap(extra, "gy", i) if i else extra for i in inner])
    return (core_first, core_middle, core_last)


def solution(mesh):
    return jax.shard_map(
        per_device,
        mesh=mesh,
        in_specs=(
            P("gx", "gy", "gz"),
            P("gx", None),
            P("gx", None),
            P("gy", None),
            P("gy", None),
            P("gz", None),
            P("gz", None),
        ),
        out_specs=(P("gx", None), P(("gx", "gz"), "gy", None), P(None, "gz")),
        check_vma=False,
    )
```

```python
import functools

import jax
import jax.numpy as jnp
from jax import lax
from jax.experimental import pallas as pl
from jax.experimental.pallas import tpu as pltpu
from jax.sharding import PartitionSpec as P

ALL = ("gx", "gy", "gz")
HIGHEST = lax.Precision.HIGHEST
VMEM_BYTES = 48 * 1024 * 1024
LOCAL_VMEM_BYTES = 63 * 1024 * 1024
ROWS = 8
LANES = 128
PARTS = 2
ROW_ROW = (((1,), (1,)), ((), ()))
COL_COL = (((0,), (0,)), ((), ()))


def gather_bits(axis):
    *bits, last = axis_bits(axis)
    return [last, *bits]


def axis_bits(axis):
    bit = lax.axis_size(axis) // 2
    while bit:
        yield bit
        bit //= 2


def swap(array, axis, bits):
    return lax.ppermute(array, axis, [(s, s ^ bits) for s in range(lax.axis_size(axis))])


def swap_sum(array, axis):
    for bit in axis_bits(axis):
        array = array + swap(array, axis, bit)
    return array


def after(value, *others):
    value, *_ = lax.optimization_barrier((value, *others))
    return value


def swap_order(axis):
    order = [0]
    for bit in gather_bits(axis):
        order += [o ^ bit for o in order]
    return order


def swap_step(held, axis, bit):
    return jnp.concatenate([held, swap(held, axis, bit)], axis=0)


def gather_rows(array, outer, inner):
    held = array[None, None]
    for dim, axis in ((0, outer), (1, inner)):
        shape = held.shape
        held = held.reshape(*shape[:dim], 1, 1, *shape[dim + 1 :])
        for bit in axis_bits(axis):
            other = swap(held, axis, bit)
            upper = (lax.axis_index(axis) & bit) != 0
            low = jnp.where(upper, other, held)
            high = jnp.where(upper, held, other)
            held = jnp.concatenate([low, high], axis=dim + 1)
            shape = held.shape
            held = held.reshape(*shape[:dim], shape[dim] * shape[dim + 1], 1, *shape[dim + 2 :])
        shape = held.shape
        held = held.reshape(*shape[: dim + 1], *shape[dim + 2 :])
    return held.reshape(-1, array.shape[-1])


def split_terms(array):
    high = lax.reduce_precision(array, 8, 7)
    return high.astype(jnp.bfloat16), (array - high).astype(jnp.bfloat16)


def invert(system):
    size = system.shape[0]
    lanes = lax.broadcasted_iota(jnp.int32, (ROWS, size), 1)
    subs = lax.broadcasted_iota(jnp.int32, (ROWS, size), 0)
    rows = [system[r : r + ROWS] for r in range(0, size, ROWS)]

    def column(block, at):
        return jnp.broadcast_to(block[:, at : at + 1], (ROWS, size))

    for panel in range(size // ROWS):
        first = panel * ROWS
        inside = (lanes >= first) & (lanes < first + ROWS)
        unit = (lanes - first == subs).astype(jnp.float32)
        work = [column(rows[panel], first + c) for c in range(ROWS)]
        work.append(jnp.where(inside, unit, rows[panel]))
        for k in range(0, ROWS, 2):
            p, q = work[k], work[k + 1]
            a, b, d = p[k : k + 1], q[k : k + 1], q[k + 1 : k + 2]
            scale = 1.0 / (a * d - b * b)
            a, b, d = a * scale, b * scale, d * scale
            for c in range(k + 2, ROWS + 1):
                upper, lower = work[c][k : k + 1], work[c][k + 1 : k + 2]
                top = d * upper - b * lower
                low = a * lower - b * upper
                rest = work[c] - p * top - q * low
                work[c] = jnp.where(subs == k, top, jnp.where(subs == k + 1, low, rest))
        solved = work[ROWS]
        for r in range(len(rows)):
            if r == panel:
                continue
            old = rows[r]
            new = jnp.where(inside, 0.0, old)
            for c in range(ROWS):
                new = new - column(old, first + c) * solved[c : c + 1]
            rows[r] = new
        rows[panel] = solved
    return jnp.concatenate(rows, axis=0)


def spd_inverse(system):
    square = lax.dot_general(
        system, system, ROW_ROW, precision=HIGHEST, preferred_element_type=jnp.float32
    )
    return invert(square)


def local_kernel(
    chunks,
    shares,
    field_hbm,
    last_x_hbm,
    last_y_hbm,
    right_y_hbm,
    right_m_hbm,
    last_m_hbm,
    last_part,
    first_part,
    *refs,
):
    count = (shares - 1) * PARTS
    terms_hbm = refs[:count]
    field, last_x, last_y, right_y, right_m, last_m, terms, sems, out_sems = refs[count:]
    x_cells, y_cells, m_cells = field.shape
    step = x_cells // chunks
    y_share = y_cells // shares
    parts = [pl.ds(n * step, step) for n in range(chunks)]
    copies = [
        pltpu.make_async_copy(last_m_hbm, last_m, sems.at[0]),
        pltpu.make_async_copy(field_hbm.at[parts[0]], field.at[parts[0]], sems.at[1]),
        pltpu.make_async_copy(last_x_hbm, last_x, sems.at[2]),
        pltpu.make_async_copy(last_y_hbm, last_y, sems.at[3]),
        pltpu.make_async_copy(right_m_hbm, right_m, sems.at[4]),
        pltpu.make_async_copy(right_y_hbm, right_y, sems.at[5]),
    ]
    for n in range(1, chunks):
        copies.append(
            pltpu.make_async_copy(field_hbm.at[parts[n]], field.at[parts[n]], sems.at[5 + n])
        )
    for copy in copies:
        copy.start()
    here = lax.axis_index("gz")
    leaving = []
    copies[0].wait()
    for n in range(chunks):
        copies[5 + n if n else 1].wait()
        for s in range(1, shares):
            start = pl.multiple_of((here ^ s) * y_share, y_share)
            rows = field[parts[n], pl.ds(start, y_share), :].reshape(step * y_share, m_cells)
            term = jnp.dot(rows, last_m[...], preferred_element_type=jnp.float32)
            terms[s - 1, parts[n]] = term.reshape(step, y_share, -1)
            part, at = divmod(n * step, x_cells // PARTS)
            leaving.append(
                pltpu.make_async_copy(
                    terms.at[s - 1, parts[n]],
                    terms_hbm[(s - 1) * PARTS + part].at[pl.ds(at, step)],
                    out_sems.at[s - 1, n],
                )
            )
            leaving[-1].start()

    for copy in copies[2:6]:
        copy.wait()
    for n in range(chunks):
        rows = field[parts[n]].reshape(step * y_cells, m_cells)
        left = last_x[parts[n]].astype(jnp.float32)[:, None, :]
        khatri = left * last_y[...].astype(jnp.float32)[None]
        khatri = khatri.astype(jnp.bfloat16).reshape(step * y_cells, -1)
        part = lax.dot_general(khatri, rows, COL_COL, preferred_element_type=jnp.float32)
        if n == 0:
            last_part[...] = part
        else:
            last_part[...] += part
        first = jnp.dot(rows, right_m[...], preferred_element_type=jnp.float32)
        first = first.reshape(step, y_cells, -1) * right_y[...].astype(jnp.float32)[None]
        first_part[parts[n], :] = jnp.sum(first, axis=1)
    for copy in leaving:
        copy.wait()


def local_products(shares, field, last_x, last_y, right_y, right_m, last_m):
    x_cells, y_cells, m_cells = field.shape
    rank, cols = last_x.shape[1], last_m.shape[1]
    chunks = max(x_cells // 8, 1)
    inputs = (field, last_x, last_y, right_y, right_m, last_m)
    dims = (x_cells, y_cells // shares, cols)
    part_dims = (x_cells // PARTS, *dims[1:])
    hbm = pl.BlockSpec(memory_space=pltpu.HBM)
    vmem = pl.BlockSpec(memory_space=pltpu.VMEM)
    return pl.pallas_call(
        functools.partial(local_kernel, chunks, shares),
        in_specs=[hbm] * len(inputs),
        out_specs=[vmem, vmem, *([hbm] * ((shares - 1) * PARTS))],
        out_shape=[
            jax.ShapeDtypeStruct((rank, m_cells), jnp.float32),
            jax.ShapeDtypeStruct((x_cells, cols), jnp.float32),
            *([jax.ShapeDtypeStruct(part_dims, jnp.float32)] * ((shares - 1) * PARTS)),
        ],
        scratch_shapes=[
            *(pltpu.VMEM(x.shape, x.dtype) for x in inputs),
            pltpu.VMEM((shares - 1, *dims), jnp.float32),
            pltpu.SemaphoreType.DMA((5 + chunks,)),
            pltpu.SemaphoreType.DMA((shares - 1, chunks)),
        ],
        compiler_params=pltpu.CompilerParams(vmem_limit_bytes=LOCAL_VMEM_BYTES),
        name="local_products",
    )(*inputs)


def two_terms(array):
    high = array.astype(jnp.bfloat16)
    return high, (array - high.astype(jnp.float32)).astype(jnp.bfloat16)


def inverse_kernel(system_shares, pinv):
    system = system_shares[:, 0]
    for k in range(1, system_shares.shape[1]):
        system = system + system_shares[:, k]
    system = system.reshape(-1, system.shape[-1])
    cols = system.shape[1]
    high, low = two_terms(spd_inverse(system))
    system_high, system_low = two_terms(system)
    both = jnp.dot(
        high,
        jnp.concatenate([system_high, system_low], axis=1),
        preferred_element_type=jnp.float32,
    )
    rest = jnp.dot(low, system_high, preferred_element_type=jnp.float32)
    pinv[...] = both[:, :cols] + (both[:, cols:] + rest)


def pseudo_inverse(system_shares):
    rank = system_shares.shape[0] * system_shares.shape[2]
    return pl.pallas_call(
        inverse_kernel,
        out_shape=jax.ShapeDtypeStruct((rank, system_shares.shape[3]), jnp.float32),
        cost_estimate=pl.CostEstimate(flops=5 * 10**9, bytes_accessed=0, transcendentals=0),
        compiler_params=pltpu.CompilerParams(vmem_limit_bytes=VMEM_BYTES),
        name="pseudo_inverse",
    )(system_shares)


def project_kernel(y_own, pinv, extra, kept, *refs):
    *terms, projected, flat = refs
    rank = pinv.shape[0]
    pinv_high, pinv_low = two_terms(pinv[...])
    pinv_both = jnp.concatenate([pinv_high, pinv_low], axis=0)
    rows = flat.shape[0] // PARTS
    x_cells, y_cells, _ = kept.shape
    x_part = x_cells // PARTS
    for part in range(PARTS):
        total = kept[part * x_part : (part + 1) * x_part]
        for term in terms[part::PARTS]:
            total = total + term[...]
        high, low = two_terms(total.reshape(rows, -1))
        both = lax.dot_general(high, pinv_both, ROW_ROW, preferred_element_type=jnp.float32)
        rest = lax.dot_general(low, pinv_high, ROW_ROW, preferred_element_type=jnp.float32)
        flat[part * rows : (part + 1) * rows] = both[:, :rank] + (both[:, rank:] + rest)
    for b in range(projected.shape[0]):
        for j in range(y_own):
            projected[b, j * x_cells : (j + 1) * x_cells] = flat[
                pl.ds(b * y_own + j, x_cells, stride=y_cells), :
            ]
        projected[b, y_own * x_cells :] = extra[...]


def project(blocks, pinv, extra, kept, terms):
    rank = pinv.shape[0]
    x_cells, y_cells, _ = kept.shape
    y_own = y_cells // blocks
    rows = y_own * x_cells + extra.shape[0]
    return pl.pallas_call(
        functools.partial(project_kernel, y_own),
        out_shape=jax.ShapeDtypeStruct((blocks, rows, rank), jnp.float32),
        scratch_shapes=[pltpu.VMEM((x_cells * y_cells, rank), jnp.float32)],
        cost_estimate=pl.CostEstimate(flops=2 * 10**9, bytes_accessed=0, transcendentals=0),
        compiler_params=pltpu.CompilerParams(vmem_limit_bytes=VMEM_BYTES),
        name="project",
    )(pinv, extra, kept, *terms)


def sketch_kernel(order, left_at, y_own, pieces, packed, out, extra):
    me = lax.axis_index("gx")
    blocks, _, cols = pieces.shape
    x_cells = packed.shape[1] - left_at
    weights = jnp.concatenate([packed[k, left_at:] for k in range(blocks)], axis=0)
    weights = weights.astype(jnp.bfloat16)
    for j in range(y_own):
        column = jnp.concatenate(
            [pieces[me ^ o, j * x_cells : (j + 1) * x_cells] for o in order], axis=0
        )
        high = column.astype(jnp.bfloat16)
        low = (column - high.astype(jnp.float32)).astype(jnp.bfloat16)
        both = lax.dot_general(
            weights,
            jnp.concatenate([high, low], axis=1),
            COL_COL,
            preferred_element_type=jnp.float32,
        )
        both = both[:, :cols] + both[:, cols:]
        out[:, j] = both.reshape(out.shape[0], out.shape[2], cols)
    extra[...] = pieces[:, y_own * x_cells :]


def sketch(order, left_at, y_own, own, pieces, packed):
    blocks, rows, cols = pieces.shape
    rank = packed.shape[2]
    extra = rows - y_own * (packed.shape[1] - left_at)
    return pl.pallas_call(
        functools.partial(sketch_kernel, order, left_at, y_own),
        out_shape=(
            jax.ShapeDtypeStruct((rank // own, y_own, own, cols), jnp.float32),
            jax.ShapeDtypeStruct((blocks, extra, cols), jnp.float32),
        ),
        compiler_params=pltpu.CompilerParams(vmem_limit_bytes=VMEM_BYTES),
        name="sketch",
    )(pieces, packed)


def first_sums_kernel(left_at, rows, packed, sums):
    x_cells, cols = rows.shape
    blocks = range(packed.shape[0])
    left = jnp.concatenate([packed[k, left_at : left_at + x_cells] for k in blocks], axis=0)
    sums[:x_cells] = rows[...]
    for c in range(cols // LANES):
        at = c * x_cells
        sums[x_cells:, c * LANES : (c + 1) * LANES] = lax.dot_general(
            left,
            jnp.concatenate([packed[k, at : at + x_cells] for k in blocks], axis=0),
            COL_COL,
            precision=HIGHEST,
            preferred_element_type=jnp.float32,
        )


def first_sums(left_at, rows, packed):
    return pl.pallas_call(
        functools.partial(first_sums_kernel, left_at),
        out_shape=jax.ShapeDtypeStruct(
            (rows.shape[0] + packed.shape[2], rows.shape[1]), jnp.float32
        ),
        compiler_params=pltpu.CompilerParams(vmem_limit_bytes=VMEM_BYTES),
        name="first_sums",
    )(rows, packed)


def first_kernel(*refs):
    *sums, core_first = refs
    x_cells = core_first.shape[0]
    total = sums[0][...]
    for other in sums[1:]:
        total = total + other[...]
    system = total[x_cells:]
    inverse = spd_inverse(system)
    scores = lax.dot_general(
        total[:x_cells], system, ROW_ROW, precision=HIGHEST, preferred_element_type=jnp.float32
    )
    core_first[...] = jnp.dot(
        scores, inverse, precision=HIGHEST, preferred_element_type=jnp.float32
    )


def solve_first(x_cells, *sums):
    return pl.pallas_call(
        first_kernel,
        out_shape=jax.ShapeDtypeStruct((x_cells, sums[0].shape[0] - x_cells), jnp.float32),
        compiler_params=pltpu.CompilerParams(vmem_limit_bytes=VMEM_BYTES),
        name="solve_first",
    )(*sums)


def place_kernel(own, inner_order, *refs):
    *parts, core_last = refs
    inner = lax.axis_index("gy")
    for part, i in zip(parts, inner_order):
        for o in range(part.shape[0]):
            at = pl.multiple_of((o * len(parts) + (inner ^ i)) * own, own)
            for c in range(part.shape[1] // own):
                core_last[pl.ds(at, own), c * LANES : (c + 1) * LANES] = part[
                    o, c * own : (c + 1) * own
                ]


def place(own, inner_order, parts):
    outer, rows, lanes = parts[0].shape
    return pl.pallas_call(
        functools.partial(place_kernel, own, inner_order),
        out_shape=jax.ShapeDtypeStruct(
            (len(parts) * outer * own, rows // own * lanes), jnp.float32
        ),
        compiler_params=pltpu.CompilerParams(vmem_limit_bytes=VMEM_BYTES),
        name="place",
    )(*parts)


def per_device(flow_field, left_x, last_x, last_y, right_y, right_m, last_m):
    x_cells, y_cells, m_cells = flow_field.shape
    rank = left_x.shape[1]
    cols = right_m.shape[1]
    blocks, shares = lax.axis_size("gx"), lax.axis_size("gz")
    y_share = y_cells // shares
    y_own = y_share // blocks

    last_part, first_part, *terms = local_products(
        shares, flow_field, last_x, last_y, right_y, right_m, last_m
    )

    terms = [swap(term, "gz", 1 + at // PARTS) for at, term in enumerate(terms)]
    here = lax.axis_index("gz")
    kept = flow_field.reshape(x_cells, shares, y_share, m_cells)
    kept = lax.dynamic_index_in_dim(kept, here, 1, False).reshape(-1, m_cells)
    kept = jnp.dot(kept, last_m, preferred_element_type=jnp.float32)
    kept = kept.reshape(x_cells, y_share, cols)

    order = swap_order("gx")
    packed = jnp.concatenate(
        [
            first_part.reshape(x_cells, -1, LANES).transpose(1, 0, 2).reshape(-1, LANES),
            left_x.astype(jnp.float32),
        ],
        axis=0,
    )[None]
    left_at = x_cells * cols // LANES
    first_bit, *bits = gather_bits("gx")
    packed = swap_step(packed, "gx", first_bit)

    group = ("gx", "gy")
    own = rank // lax.axis_size(group)
    last_rows = lax.all_to_all(last_part.reshape(-1, own, m_cells), group, 0, 0, tiled=True)
    last_rows = jnp.sum(after(last_rows, *terms[::PARTS]), axis=0)
    both = jnp.dot(
        jnp.concatenate(split_terms(last_rows), axis=0), last_m, preferred_element_type=jnp.float32
    )
    both = after(both[:own] + both[own:], packed, kept)
    count = lax.axis_size(ALL)
    copies = jnp.broadcast_to(both[None], (count, own, cols))
    system = lax.all_to_all(copies, ALL, 0, 0, tiled=True).reshape(-1, shares, own, cols)
    if own % ROWS:
        system = jnp.sum(system, axis=1).reshape(-1, 1, ROWS, cols)

    for bit in bits:
        if bit == bits[-1]:
            system = after(system, packed)
        packed = swap_step(packed, "gx", bit)
    sums = first_sums(left_at, first_part, packed)
    if own % ROWS:
        extra = jnp.zeros((ROWS, LANES), jnp.float32)
    else:
        extra = last_rows.reshape(own, -1, LANES).transpose(1, 0, 2).reshape(-1, LANES)
    pinv = pseudo_inverse(after(system, *terms))
    projected = after(project(blocks, pinv, extra, kept, terms), packed)
    sums = swap_sum(sums, "gz")
    sums = [swap(sums, "gy", y) if y else sums for y in range(lax.axis_size("gy"))]

    pieces = lax.all_to_all(projected, "gx", 0, 0, tiled=True)
    core_first = solve_first(x_cells, after(sums[0], projected), *sums[1:])
    group = ("gx", "gz")
    devices = lax.axis_size(group)
    rank_own = rank // devices
    if rank_own % ROWS:
        middle, extra = sketch(order, left_at, y_own, rank, pieces, packed)
        middle = middle.reshape(y_own, devices, rank_own, rank).transpose(1, 0, 2, 3)
    else:
        middle, extra = sketch(order, left_at, y_own, rank_own, pieces, packed)
    middle, core_first = lax.optimization_barrier((middle, core_first))
    received = lax.all_to_all(middle, group, 0, 0, tiled=True)
    received = received.reshape(blocks, shares, y_own, rank_own, rank)
    core_middle = received.transpose(3, 1, 0, 2, 4).reshape(rank_own, y_cells, rank)

    if own % ROWS:
        core_last = gather_rows(last_rows, "gx", "gy")
    else:
        inner = range(lax.axis_size("gy"))
        core_last = place(own, inner, [swap(extra, "gy", i) if i else extra for i in inner])
    return (core_first, core_middle, core_last)


def solution(mesh):
    return jax.shard_map(
        per_device,
        mesh=mesh,
        in_specs=(
            P("gx", "gy", "gz"),
            P("gx", None),
            P("gx", None),
            P("gy", None),
            P("gy", None),
            P("gz", None),
            P("gz", None),
        ),
        out_specs=(P("gx", None), P(("gx", "gz"), "gy", None), P(None, "gz")),
        check_vma=False,
    )
```

```python
import functools

import jax
import jax.numpy as jnp
from jax import lax
from jax.experimental import pallas as pl
from jax.experimental.pallas import tpu as pltpu
from jax.sharding import PartitionSpec as P

ALL = ("gx", "gy", "gz")
HIGHEST = lax.Precision.HIGHEST
VMEM_BYTES = 48 * 1024 * 1024
LOCAL_VMEM_BYTES = 63 * 1024 * 1024
ROWS = 8
LANES = 128
PARTS = 2
ROW_ROW = (((1,), (1,)), ((), ()))
COL_COL = (((0,), (0,)), ((), ()))


def gather_bits(axis):
    *bits, last = axis_bits(axis)
    return [last, *bits]


def axis_bits(axis):
    bit = lax.axis_size(axis) // 2
    while bit:
        yield bit
        bit //= 2


def swap(array, axis, bits):
    return lax.ppermute(array, axis, [(s, s ^ bits) for s in range(lax.axis_size(axis))])


def swap_sum(array, axis):
    for bit in axis_bits(axis):
        array = array + swap(array, axis, bit)
    return array


def after(value, *others):
    value, *_ = lax.optimization_barrier((value, *others))
    return value


def swap_order(axis):
    order = [0]
    for bit in gather_bits(axis):
        order += [o ^ bit for o in order]
    return order


def swap_step(held, axis, bit):
    return jnp.concatenate([held, swap(held, axis, bit)], axis=0)


def gather_rows(array, outer, inner):
    held = array[None, None]
    for dim, axis in ((0, outer), (1, inner)):
        shape = held.shape
        held = held.reshape(*shape[:dim], 1, 1, *shape[dim + 1 :])
        for bit in axis_bits(axis):
            other = swap(held, axis, bit)
            upper = (lax.axis_index(axis) & bit) != 0
            low = jnp.where(upper, other, held)
            high = jnp.where(upper, held, other)
            held = jnp.concatenate([low, high], axis=dim + 1)
            shape = held.shape
            held = held.reshape(*shape[:dim], shape[dim] * shape[dim + 1], 1, *shape[dim + 2 :])
        shape = held.shape
        held = held.reshape(*shape[: dim + 1], *shape[dim + 2 :])
    return held.reshape(-1, array.shape[-1])


def split_terms(array):
    high = lax.reduce_precision(array, 8, 7)
    return high.astype(jnp.bfloat16), (array - high).astype(jnp.bfloat16)


def invert(system):
    size = system.shape[0]
    lanes = lax.broadcasted_iota(jnp.int32, (ROWS, size), 1)
    subs = lax.broadcasted_iota(jnp.int32, (ROWS, size), 0)
    rows = [system[r : r + ROWS] for r in range(0, size, ROWS)]

    def column(block, at):
        return jnp.broadcast_to(block[:, at : at + 1], (ROWS, size))

    for panel in range(size // ROWS):
        first = panel * ROWS
        inside = (lanes >= first) & (lanes < first + ROWS)
        unit = (lanes - first == subs).astype(jnp.float32)
        work = [column(rows[panel], first + c) for c in range(ROWS)]
        work.append(jnp.where(inside, unit, rows[panel]))
        for k in range(0, ROWS, 2):
            p, q = work[k], work[k + 1]
            a, b, d = p[k : k + 1], q[k : k + 1], q[k + 1 : k + 2]
            scale = 1.0 / (a * d - b * b)
            a, b, d = a * scale, b * scale, d * scale
            for c in range(k + 2, ROWS + 1):
                upper, lower = work[c][k : k + 1], work[c][k + 1 : k + 2]
                top = d * upper - b * lower
                low = a * lower - b * upper
                rest = work[c] - p * top - q * low
                work[c] = jnp.where(subs == k, top, jnp.where(subs == k + 1, low, rest))
        solved = work[ROWS]
        for r in range(len(rows)):
            if r == panel:
                continue
            old = rows[r]
            new = jnp.where(inside, 0.0, old)
            for c in range(ROWS):
                new = new - column(old, first + c) * solved[c : c + 1]
            rows[r] = new
        rows[panel] = solved
    return jnp.concatenate(rows, axis=0)


def spd_inverse(system):
    square = lax.dot_general(
        system, system, ROW_ROW, precision=HIGHEST, preferred_element_type=jnp.float32
    )
    return invert(square)


def local_kernel(
    chunks,
    shares,
    field_hbm,
    last_x_hbm,
    last_y_hbm,
    right_y_hbm,
    right_m_hbm,
    last_m_hbm,
    last_part,
    first_part,
    *refs,
):
    count = (shares - 1) * PARTS
    terms_hbm = refs[:count]
    field, last_x, last_y, right_y, right_m, last_m, terms, sems, out_sems = refs[count:]
    x_cells, y_cells, m_cells = field.shape
    step = x_cells // chunks
    y_share = y_cells // shares
    parts = [pl.ds(n * step, step) for n in range(chunks)]
    copies = [
        pltpu.make_async_copy(last_m_hbm, last_m, sems.at[0]),
        pltpu.make_async_copy(field_hbm.at[parts[0]], field.at[parts[0]], sems.at[1]),
        pltpu.make_async_copy(last_x_hbm, last_x, sems.at[2]),
        pltpu.make_async_copy(last_y_hbm, last_y, sems.at[3]),
        pltpu.make_async_copy(right_m_hbm, right_m, sems.at[4]),
        pltpu.make_async_copy(right_y_hbm, right_y, sems.at[5]),
    ]
    for n in range(1, chunks):
        copies.append(
            pltpu.make_async_copy(field_hbm.at[parts[n]], field.at[parts[n]], sems.at[5 + n])
        )
    for copy in copies:
        copy.start()
    here = lax.axis_index("gz")
    leaving = []
    copies[0].wait()
    for n in range(chunks):
        copies[5 + n if n else 1].wait()
        for s in range(1, shares):
            start = pl.multiple_of((here ^ s) * y_share, y_share)
            rows = field[parts[n], pl.ds(start, y_share), :].reshape(step * y_share, m_cells)
            term = jnp.dot(rows, last_m[...], preferred_element_type=jnp.float32)
            terms[s - 1, parts[n]] = term.reshape(step, y_share, -1)
            part, at = divmod(n * step, x_cells // PARTS)
            leaving.append(
                pltpu.make_async_copy(
                    terms.at[s - 1, parts[n]],
                    terms_hbm[(s - 1) * PARTS + part].at[pl.ds(at, step)],
                    out_sems.at[s - 1, n],
                )
            )
            leaving[-1].start()

    for copy in copies[2:6]:
        copy.wait()
    for n in range(chunks):
        rows = field[parts[n]].reshape(step * y_cells, m_cells)
        left = last_x[parts[n]].astype(jnp.float32)[:, None, :]
        khatri = left * last_y[...].astype(jnp.float32)[None]
        khatri = khatri.astype(jnp.bfloat16).reshape(step * y_cells, -1)
        part = lax.dot_general(khatri, rows, COL_COL, preferred_element_type=jnp.float32)
        if n == 0:
            last_part[...] = part
        else:
            last_part[...] += part
        first = jnp.dot(rows, right_m[...], preferred_element_type=jnp.float32)
        first = first.reshape(step, y_cells, -1) * right_y[...].astype(jnp.float32)[None]
        first_part[parts[n], :] = jnp.sum(first, axis=1)
    for copy in leaving:
        copy.wait()


def local_products(shares, field, last_x, last_y, right_y, right_m, last_m):
    x_cells, y_cells, m_cells = field.shape
    rank, cols = last_x.shape[1], last_m.shape[1]
    chunks = max(x_cells // 8, 1)
    inputs = (field, last_x, last_y, right_y, right_m, last_m)
    dims = (x_cells, y_cells // shares, cols)
    part_dims = (x_cells // PARTS, *dims[1:])
    hbm = pl.BlockSpec(memory_space=pltpu.HBM)
    vmem = pl.BlockSpec(memory_space=pltpu.VMEM)
    return pl.pallas_call(
        functools.partial(local_kernel, chunks, shares),
        in_specs=[hbm] * len(inputs),
        out_specs=[vmem, vmem, *([hbm] * ((shares - 1) * PARTS))],
        out_shape=[
            jax.ShapeDtypeStruct((rank, m_cells), jnp.float32),
            jax.ShapeDtypeStruct((x_cells, cols), jnp.float32),
            *([jax.ShapeDtypeStruct(part_dims, jnp.float32)] * ((shares - 1) * PARTS)),
        ],
        scratch_shapes=[
            *(pltpu.VMEM(x.shape, x.dtype) for x in inputs),
            pltpu.VMEM((shares - 1, *dims), jnp.float32),
            pltpu.SemaphoreType.DMA((5 + chunks,)),
            pltpu.SemaphoreType.DMA((shares - 1, chunks)),
        ],
        compiler_params=pltpu.CompilerParams(vmem_limit_bytes=LOCAL_VMEM_BYTES),
        name="local_products",
    )(*inputs)


def two_terms(array):
    high = array.astype(jnp.bfloat16)
    return high, (array - high.astype(jnp.float32)).astype(jnp.bfloat16)


def inverse_kernel(system_shares, pinv):
    system = system_shares[:, 0]
    for k in range(1, system_shares.shape[1]):
        system = system + system_shares[:, k]
    system = system.reshape(-1, system.shape[-1])
    cols = system.shape[1]
    high, low = two_terms(spd_inverse(system))
    system_high, system_low = two_terms(system)
    both = jnp.dot(
        high,
        jnp.concatenate([system_high, system_low], axis=1),
        preferred_element_type=jnp.float32,
    )
    rest = jnp.dot(low, system_high, preferred_element_type=jnp.float32)
    pinv[...] = both[:, :cols] + (both[:, cols:] + rest)


def pseudo_inverse(system_shares):
    rank = system_shares.shape[0] * system_shares.shape[2]
    return pl.pallas_call(
        inverse_kernel,
        out_shape=jax.ShapeDtypeStruct((rank, system_shares.shape[3]), jnp.float32),
        cost_estimate=pl.CostEstimate(flops=5 * 10**9, bytes_accessed=0, transcendentals=0),
        compiler_params=pltpu.CompilerParams(vmem_limit_bytes=VMEM_BYTES),
        name="pseudo_inverse",
    )(system_shares)


def project_kernel(y_own, pinv, kept, *refs):
    *terms, projected, flat = refs
    rank = pinv.shape[0]
    pinv_high, pinv_low = two_terms(pinv[...])
    pinv_both = jnp.concatenate([pinv_high, pinv_low], axis=0)
    rows = flat.shape[0] // PARTS
    x_cells, y_cells, _ = kept.shape
    x_part = x_cells // PARTS
    for part in range(PARTS):
        total = kept[part * x_part : (part + 1) * x_part]
        for term in terms[part::PARTS]:
            total = total + term[...]
        high, low = two_terms(total.reshape(rows, -1))
        both = lax.dot_general(high, pinv_both, ROW_ROW, preferred_element_type=jnp.float32)
        rest = lax.dot_general(low, pinv_high, ROW_ROW, preferred_element_type=jnp.float32)
        flat[part * rows : (part + 1) * rows] = both[:, :rank] + (both[:, rank:] + rest)
    for b in range(projected.shape[0]):
        for j in range(y_own):
            projected[b, j * x_cells : (j + 1) * x_cells] = flat[
                pl.ds(b * y_own + j, x_cells, stride=y_cells), :
            ]


def project(blocks, pinv, kept, terms):
    rank = pinv.shape[0]
    x_cells, y_cells, _ = kept.shape
    y_own = y_cells // blocks
    rows = y_own * x_cells
    return pl.pallas_call(
        functools.partial(project_kernel, y_own),
        out_shape=jax.ShapeDtypeStruct((blocks, rows, rank), jnp.float32),
        scratch_shapes=[pltpu.VMEM((x_cells * y_cells, rank), jnp.float32)],
        cost_estimate=pl.CostEstimate(flops=2 * 10**9, bytes_accessed=0, transcendentals=0),
        compiler_params=pltpu.CompilerParams(vmem_limit_bytes=VMEM_BYTES),
        name="project",
    )(pinv, kept, *terms)


def sketch_kernel(order, pieces, left, out):
    me = lax.axis_index("gx")
    _, rows, cols = pieces.shape
    blocks, x_cells, _ = left.shape
    weights = jnp.concatenate([left[k] for k in range(blocks)], axis=0).astype(jnp.bfloat16)
    for j in range(rows // x_cells):
        column = jnp.concatenate(
            [pieces[me ^ o, j * x_cells : (j + 1) * x_cells] for o in order], axis=0
        )
        both = lax.dot_general(
            weights,
            jnp.concatenate(two_terms(column), axis=1),
            COL_COL,
            preferred_element_type=jnp.float32,
        )
        both = both[:, :cols] + both[:, cols:]
        out[:, j] = both.reshape(out.shape[0], out.shape[2], cols)


def sketch(order, own, pieces, left):
    _, rows, cols = pieces.shape
    _, x_cells, rank = left.shape
    return pl.pallas_call(
        functools.partial(sketch_kernel, order),
        out_shape=jax.ShapeDtypeStruct((rank // own, rows // x_cells, own, cols), jnp.float32),
        compiler_params=pltpu.CompilerParams(vmem_limit_bytes=VMEM_BYTES),
        name="sketch",
    )(pieces, left)


def first_sums_kernel(rows, left, mine, other, sums, extra):
    x_cells, cols = rows.shape
    blocks = left.shape[0]
    height = x_cells * cols // LANES
    left_all = jnp.concatenate([left[k] for k in range(blocks)], axis=0)
    sums[:x_cells] = rows[...]
    for c in range(cols // LANES):
        at = [k * height + c * x_cells for k in range(blocks // 2)]
        sums[x_cells:, c * LANES : (c + 1) * LANES] = lax.dot_general(
            left_all,
            jnp.concatenate([part[a : a + x_cells] for part in (mine, other) for a in at], axis=0),
            COL_COL,
            precision=HIGHEST,
            preferred_element_type=jnp.float32,
        )
    count = blocks // 4
    deep = extra.shape[1]
    for n, part in enumerate((mine, other)):
        for k in range(count):
            at = blocks // 2 * height + k * deep
            extra[n * count + k] = part[at : at + deep]


def first_sums(rows, left, mine, other):
    blocks, x_cells, rank = left.shape
    deep = (mine.shape[0] - blocks // 2 * x_cells * rows.shape[1] // LANES) // (blocks // 4)
    return pl.pallas_call(
        first_sums_kernel,
        out_shape=(
            jax.ShapeDtypeStruct((rows.shape[0] + rank, rows.shape[1]), jnp.float32),
            jax.ShapeDtypeStruct((blocks // 2, deep, rank), jnp.float32),
        ),
        compiler_params=pltpu.CompilerParams(vmem_limit_bytes=VMEM_BYTES),
        name="first_sums",
    )(rows, left, mine, other)


def first_kernel(*refs):
    *sums, core_first = refs
    x_cells = core_first.shape[0]
    total = sums[0][...]
    for other in sums[1:]:
        total = total + other[...]
    system = total[x_cells:]
    inverse = spd_inverse(system)
    scores = lax.dot_general(
        total[:x_cells], system, ROW_ROW, precision=HIGHEST, preferred_element_type=jnp.float32
    )
    core_first[...] = jnp.dot(
        scores, inverse, precision=HIGHEST, preferred_element_type=jnp.float32
    )


def solve_first(x_cells, *sums):
    return pl.pallas_call(
        first_kernel,
        out_shape=jax.ShapeDtypeStruct((x_cells, sums[0].shape[0] - x_cells), jnp.float32),
        compiler_params=pltpu.CompilerParams(vmem_limit_bytes=VMEM_BYTES),
        name="solve_first",
    )(*sums)


def place_kernel(own, outer_order, *refs):
    *parts, core_last = refs
    outer, inner = lax.axis_index("gx"), lax.axis_index("gy")
    for i, part in enumerate(parts):
        for k, o in enumerate(outer_order):
            at = ((outer ^ o) * len(parts) + (inner ^ i)) * own
            at = pl.multiple_of(at, own)
            for c in range(part.shape[1] // own):
                core_last[pl.ds(at, own), c * LANES : (c + 1) * LANES] = part[
                    k, c * own : (c + 1) * own
                ]


def place(own, outer_order, parts):
    outer, rows, lanes = parts[0].shape
    return pl.pallas_call(
        functools.partial(place_kernel, own, outer_order),
        out_shape=jax.ShapeDtypeStruct(
            (len(parts) * outer * own, rows // own * lanes), jnp.float32
        ),
        compiler_params=pltpu.CompilerParams(vmem_limit_bytes=VMEM_BYTES),
        name="place",
    )(*parts)


def per_device(flow_field, left_x, last_x, last_y, right_y, right_m, last_m):
    x_cells, y_cells, m_cells = flow_field.shape
    rank = left_x.shape[1]
    cols = right_m.shape[1]
    blocks, shares = lax.axis_size("gx"), lax.axis_size("gz")
    y_share = y_cells // shares
    y_own = y_share // blocks

    last_part, first_part, *terms = local_products(
        shares, flow_field, last_x, last_y, right_y, right_m, last_m
    )

    terms = [swap(term, "gz", 1 + at // PARTS) for at, term in enumerate(terms)]
    here = lax.axis_index("gz")
    kept = flow_field.reshape(x_cells, shares, y_share, m_cells)
    kept = lax.dynamic_index_in_dim(kept, here, 1, False).reshape(-1, m_cells)
    kept = jnp.dot(kept, last_m, preferred_element_type=jnp.float32)
    kept = kept.reshape(x_cells, y_share, cols)

    order = swap_order("gx")
    packed = jnp.concatenate(
        [
            first_part.reshape(x_cells, -1, LANES).transpose(1, 0, 2).reshape(-1, LANES),
            left_x.astype(jnp.float32),
        ],
        axis=0,
    )[None]
    left_at = x_cells * cols // LANES
    first_bit, *bits = gather_bits("gx")
    packed = swap_step(packed, "gx", first_bit)

    group = ("gx", "gy")
    own = rank // lax.axis_size(group)
    last_rows = lax.all_to_all(last_part.reshape(-1, own, m_cells), group, 0, 0, tiled=True)
    last_rows = jnp.sum(after(last_rows, *terms[::PARTS]), axis=0)
    both = jnp.dot(
        jnp.concatenate(split_terms(last_rows), axis=0), last_m, preferred_element_type=jnp.float32
    )
    both = after(both[:own] + both[own:], packed, kept)
    count = lax.axis_size(ALL)
    copies = jnp.broadcast_to(both[None], (count, own, cols))
    system = lax.all_to_all(copies, ALL, 0, 0, tiled=True).reshape(-1, shares, own, cols)
    if own % ROWS:
        system = jnp.sum(system, axis=1).reshape(-1, 1, ROWS, cols)

    *middle_bits, last_bit = bits
    for bit in middle_bits:
        packed = swap_step(packed, "gx", bit)
    left_all = swap_step(packed[:, left_at:], "gx", last_bit)

    if own % ROWS:
        extra = jnp.zeros((ROWS, LANES), jnp.float32)
    else:
        extra = last_rows.reshape(own, -1, LANES).transpose(1, 0, 2).reshape(-1, LANES)
    extra = extra[None]
    others = [0]
    for bit in middle_bits:
        extra = swap_step(extra, "gx", bit)
        others += [o ^ bit for o in others]
    others += [o ^ last_bit for o in others]
    mine = jnp.concatenate(
        [packed[:, :left_at].reshape(-1, LANES), extra.reshape(-1, LANES)], axis=0
    )
    system = after(system, left_all, *terms)
    other = swap(after(mine, system), "gx", last_bit)
    pinv = pseudo_inverse(system)
    projected = project(blocks, pinv, kept, terms)
    sums, extra = first_sums(first_part, left_all, mine, other)
    sums = swap_sum(sums, "gz")
    sums = [swap(sums, "gy", y) if y else sums for y in range(lax.axis_size("gy"))]

    pieces = lax.all_to_all(projected, "gx", 0, 0, tiled=True)
    group = ("gx", "gz")
    devices = lax.axis_size(group)
    rank_own = rank // devices
    if rank_own % ROWS:
        middle = sketch(order, rank, pieces, left_all)
        middle = middle.reshape(y_own, devices, rank_own, rank).transpose(1, 0, 2, 3)
    else:
        middle = sketch(order, rank_own, pieces, left_all)
    extra = jnp.concatenate([extra, swap(extra, "gx", 1)], axis=0)
    middle = after(middle, extra, *sums)
    received = lax.all_to_all(middle, group, 0, 0, tiled=True)
    received = received.reshape(blocks, shares, y_own, rank_own, rank)
    core_middle = received.transpose(3, 1, 0, 2, 4).reshape(rank_own, y_cells, rank)

    if own % ROWS:
        core_last = gather_rows(last_rows, "gx", "gy")
    else:
        outer = [o ^ n for n in range(2) for o in others]
        inner = range(lax.axis_size("gy"))
        core_last = place(own, outer, [swap(extra, "gy", i) if i else extra for i in inner])
    core_first = solve_first(x_cells, after(sums[0], middle), *sums[1:])
    return (core_first, core_middle, core_last)


def solution(mesh):
    return jax.shard_map(
        per_device,
        mesh=mesh,
        in_specs=(
            P("gx", "gy", "gz"),
            P("gx", None),
            P("gx", None),
            P("gy", None),
            P("gy", None),
            P("gz", None),
            P("gz", None),
        ),
        out_specs=(P("gx", None), P(("gx", "gz"), "gy", None), P(None, "gz")),
        check_vma=False,
    )
```

```python
import functools

import jax
import jax.numpy as jnp
from jax import lax
from jax.experimental import pallas as pl
from jax.experimental.pallas import tpu as pltpu
from jax.sharding import PartitionSpec as P

ALL = ("gx", "gy", "gz")
HIGHEST = lax.Precision.HIGHEST
VMEM_BYTES = 48 * 1024 * 1024
LOCAL_VMEM_BYTES = 63 * 1024 * 1024
ROWS = 8
LANES = 128
PARTS = 2
ROW_ROW = (((1,), (1,)), ((), ()))
COL_COL = (((0,), (0,)), ((), ()))


def gather_bits(axis):
    *bits, low, last = axis_bits(axis)
    return [low, *bits, last]


def axis_bits(axis):
    bit = lax.axis_size(axis) // 2
    while bit:
        yield bit
        bit //= 2


def swap(array, axis, bits):
    return lax.ppermute(array, axis, [(s, s ^ bits) for s in range(lax.axis_size(axis))])


def swap_sum(array, axis):
    for bit in axis_bits(axis):
        array = array + swap(array, axis, bit)
    return array


def after(value, *others):
    value, *_ = lax.optimization_barrier((value, *others))
    return value


def swap_order(axis):
    order = [0]
    for bit in gather_bits(axis):
        order += [o ^ bit for o in order]
    return order


def swap_step(held, axis, bit):
    return jnp.concatenate([held, swap(held, axis, bit)], axis=0)


def gather_rows(array, outer, inner):
    held = array[None, None]
    for dim, axis in ((0, outer), (1, inner)):
        shape = held.shape
        held = held.reshape(*shape[:dim], 1, 1, *shape[dim + 1 :])
        for bit in axis_bits(axis):
            other = swap(held, axis, bit)
            upper = (lax.axis_index(axis) & bit) != 0
            low = jnp.where(upper, other, held)
            high = jnp.where(upper, held, other)
            held = jnp.concatenate([low, high], axis=dim + 1)
            shape = held.shape
            held = held.reshape(*shape[:dim], shape[dim] * shape[dim + 1], 1, *shape[dim + 2 :])
        shape = held.shape
        held = held.reshape(*shape[: dim + 1], *shape[dim + 2 :])
    return held.reshape(-1, array.shape[-1])


def split_terms(array):
    high = lax.reduce_precision(array, 8, 7)
    return high.astype(jnp.bfloat16), (array - high).astype(jnp.bfloat16)


def invert(system):
    size = system.shape[0]
    lanes = lax.broadcasted_iota(jnp.int32, (ROWS, size), 1)
    subs = lax.broadcasted_iota(jnp.int32, (ROWS, size), 0)
    rows = [system[r : r + ROWS] for r in range(0, size, ROWS)]

    def column(block, at):
        return jnp.broadcast_to(block[:, at : at + 1], (ROWS, size))

    for panel in range(size // ROWS):
        first = panel * ROWS
        inside = (lanes >= first) & (lanes < first + ROWS)
        unit = (lanes - first == subs).astype(jnp.float32)
        work = [column(rows[panel], first + c) for c in range(ROWS)]
        work.append(jnp.where(inside, unit, rows[panel]))
        for k in range(0, ROWS, 2):
            p, q = work[k], work[k + 1]
            a, b, d = p[k : k + 1], q[k : k + 1], q[k + 1 : k + 2]
            scale = 1.0 / (a * d - b * b)
            a, b, d = a * scale, b * scale, d * scale
            for c in range(k + 2, ROWS + 1):
                upper, lower = work[c][k : k + 1], work[c][k + 1 : k + 2]
                top = d * upper - b * lower
                low = a * lower - b * upper
                rest = work[c] - p * top - q * low
                work[c] = jnp.where(subs == k, top, jnp.where(subs == k + 1, low, rest))
        solved = work[ROWS]
        for r in range(len(rows)):
            if r == panel:
                continue
            old = rows[r]
            new = jnp.where(inside, 0.0, old)
            for c in range(ROWS):
                new = new - column(old, first + c) * solved[c : c + 1]
            rows[r] = new
        rows[panel] = solved
    return jnp.concatenate(rows, axis=0)


def spd_inverse(system):
    square = lax.dot_general(
        system, system, ROW_ROW, precision=HIGHEST, preferred_element_type=jnp.float32
    )
    return invert(square)


def local_kernel(
    chunks,
    shares,
    field_hbm,
    last_x_hbm,
    last_y_hbm,
    right_y_hbm,
    right_m_hbm,
    last_m_hbm,
    last_part,
    first_part,
    *refs,
):
    count = (shares - 1) * PARTS
    terms_hbm = refs[:count]
    field, last_x, last_y, right_y, right_m, last_m, terms, sems, out_sems = refs[count:]
    x_cells, y_cells, m_cells = field.shape
    step = x_cells // chunks
    y_share = y_cells // shares
    parts = [pl.ds(n * step, step) for n in range(chunks)]
    copies = [
        pltpu.make_async_copy(last_m_hbm, last_m, sems.at[0]),
        pltpu.make_async_copy(field_hbm.at[parts[0]], field.at[parts[0]], sems.at[1]),
        pltpu.make_async_copy(last_x_hbm, last_x, sems.at[2]),
        pltpu.make_async_copy(last_y_hbm, last_y, sems.at[3]),
        pltpu.make_async_copy(right_m_hbm, right_m, sems.at[4]),
        pltpu.make_async_copy(right_y_hbm, right_y, sems.at[5]),
    ]
    for n in range(1, chunks):
        copies.append(
            pltpu.make_async_copy(field_hbm.at[parts[n]], field.at[parts[n]], sems.at[5 + n])
        )
    for copy in copies:
        copy.start()
    here = lax.axis_index("gz")
    leaving = []
    copies[0].wait()
    for n in range(chunks):
        copies[5 + n if n else 1].wait()
        for s in range(1, shares):
            start = pl.multiple_of((here ^ s) * y_share, y_share)
            rows = field[parts[n], pl.ds(start, y_share), :].reshape(step * y_share, m_cells)
            term = jnp.dot(rows, last_m[...], preferred_element_type=jnp.float32)
            terms[s - 1, parts[n]] = term.reshape(step, y_share, -1)
            part, at = divmod(n * step, x_cells // PARTS)
            leaving.append(
                pltpu.make_async_copy(
                    terms.at[s - 1, parts[n]],
                    terms_hbm[(s - 1) * PARTS + part].at[pl.ds(at, step)],
                    out_sems.at[s - 1, n],
                )
            )
            leaving[-1].start()

    for copy in copies[2:6]:
        copy.wait()
    for n in range(chunks):
        rows = field[parts[n]].reshape(step * y_cells, m_cells)
        left = last_x[parts[n]].astype(jnp.float32)[:, None, :]
        khatri = left * last_y[...].astype(jnp.float32)[None]
        khatri = khatri.astype(jnp.bfloat16).reshape(step * y_cells, -1)
        part = lax.dot_general(khatri, rows, COL_COL, preferred_element_type=jnp.float32)
        if n == 0:
            last_part[...] = part
        else:
            last_part[...] += part
        first = jnp.dot(rows, right_m[...], preferred_element_type=jnp.float32)
        first = first.reshape(step, y_cells, -1) * right_y[...].astype(jnp.float32)[None]
        first_part[parts[n], :] = jnp.sum(first, axis=1)
    for copy in leaving:
        copy.wait()


def local_products(shares, field, last_x, last_y, right_y, right_m, last_m):
    x_cells, y_cells, m_cells = field.shape
    rank, cols = last_x.shape[1], last_m.shape[1]
    chunks = max(x_cells // 8, 1)
    inputs = (field, last_x, last_y, right_y, right_m, last_m)
    dims = (x_cells, y_cells // shares, cols)
    part_dims = (x_cells // PARTS, *dims[1:])
    hbm = pl.BlockSpec(memory_space=pltpu.HBM)
    vmem = pl.BlockSpec(memory_space=pltpu.VMEM)
    return pl.pallas_call(
        functools.partial(local_kernel, chunks, shares),
        in_specs=[hbm] * len(inputs),
        out_specs=[vmem, vmem, *([hbm] * ((shares - 1) * PARTS))],
        out_shape=[
            jax.ShapeDtypeStruct((rank, m_cells), jnp.float32),
            jax.ShapeDtypeStruct((x_cells, cols), jnp.float32),
            *([jax.ShapeDtypeStruct(part_dims, jnp.float32)] * ((shares - 1) * PARTS)),
        ],
        scratch_shapes=[
            *(pltpu.VMEM(x.shape, x.dtype) for x in inputs),
            pltpu.VMEM((shares - 1, *dims), jnp.float32),
            pltpu.SemaphoreType.DMA((5 + chunks,)),
            pltpu.SemaphoreType.DMA((shares - 1, chunks)),
        ],
        compiler_params=pltpu.CompilerParams(vmem_limit_bytes=LOCAL_VMEM_BYTES),
        name="local_products",
    )(*inputs)


def two_terms(array):
    high = array.astype(jnp.bfloat16)
    return high, (array - high.astype(jnp.float32)).astype(jnp.bfloat16)


def last_kernel(y_own, system_shares, extra, kept, *refs):
    *terms, projected, flat = refs
    x_cells, y_cells, cols = kept.shape
    x_part = x_cells // PARTS
    totals = []
    for part in range(PARTS):
        total = kept[part * x_part : (part + 1) * x_part]
        for term in terms[part::PARTS]:
            total = total + term[...]
        totals.append(two_terms(total.reshape(x_part * y_cells, cols)))

    system = system_shares[:, 0]
    for k in range(1, system_shares.shape[1]):
        system = system + system_shares[:, k]
    system = system.reshape(-1, cols)
    rank = system.shape[0]
    system_high, system_low = two_terms(system)
    high, low = two_terms(spd_inverse(system))
    both = jnp.dot(
        high,
        jnp.concatenate([system_high, system_low], axis=1),
        preferred_element_type=jnp.float32,
    )
    rest = jnp.dot(low, system_high, preferred_element_type=jnp.float32)
    pinv_high, pinv_low = two_terms(both[:, :cols] + (both[:, cols:] + rest))
    pinv_both = jnp.concatenate([pinv_high, pinv_low], axis=0)

    rows = flat.shape[0] // PARTS
    for part, (high, low) in enumerate(totals):
        both = lax.dot_general(high, pinv_both, ROW_ROW, preferred_element_type=jnp.float32)
        rest = lax.dot_general(low, pinv_high, ROW_ROW, preferred_element_type=jnp.float32)
        flat[part * rows : (part + 1) * rows] = both[:, :rank] + (both[:, rank:] + rest)
    for b in range(projected.shape[0]):
        for j in range(y_own):
            projected[b, j * x_cells : (j + 1) * x_cells] = flat[
                pl.ds(b * y_own + j, x_cells, stride=y_cells), :
            ]
        projected[b, y_own * x_cells :] = extra[...]


def solve_last(blocks, system_shares, extra, kept, terms):
    rank = system_shares.shape[0] * system_shares.shape[2]
    x_cells, y_cells, _ = kept.shape
    y_own = y_cells // blocks
    rows = y_own * x_cells + extra.shape[0]
    return pl.pallas_call(
        functools.partial(last_kernel, y_own),
        out_shape=jax.ShapeDtypeStruct((blocks, rows, rank), jnp.float32),
        scratch_shapes=[pltpu.VMEM((x_cells * y_cells, rank), jnp.float32)],
        cost_estimate=pl.CostEstimate(flops=6 * 10**9, bytes_accessed=0, transcendentals=0),
        compiler_params=pltpu.CompilerParams(vmem_limit_bytes=VMEM_BYTES),
        name="solve_last",
    )(system_shares, extra, kept, *terms)


def sketch_kernel(order, left_at, y_own, pieces, packed, out, extra):
    me = lax.axis_index("gx")
    blocks, _, cols = pieces.shape
    x_cells = packed.shape[1] - left_at
    weights = jnp.concatenate([packed[k, left_at:] for k in range(blocks)], axis=0)
    weights = weights.astype(jnp.bfloat16)
    for j in range(y_own):
        column = jnp.concatenate(
            [pieces[me ^ o, j * x_cells : (j + 1) * x_cells] for o in order], axis=0
        )
        high = column.astype(jnp.bfloat16)
        low = (column - high.astype(jnp.float32)).astype(jnp.bfloat16)
        both = lax.dot_general(
            weights,
            jnp.concatenate([high, low], axis=1),
            COL_COL,
            preferred_element_type=jnp.float32,
        )
        both = both[:, :cols] + both[:, cols:]
        out[:, j] = both.reshape(out.shape[0], out.shape[2], cols)
    extra[...] = pieces[:, y_own * x_cells :]


def sketch(order, left_at, y_own, own, pieces, packed):
    blocks, rows, cols = pieces.shape
    rank = packed.shape[2]
    extra = rows - y_own * (packed.shape[1] - left_at)
    return pl.pallas_call(
        functools.partial(sketch_kernel, order, left_at, y_own),
        out_shape=(
            jax.ShapeDtypeStruct((rank // own, y_own, own, cols), jnp.float32),
            jax.ShapeDtypeStruct((blocks, extra, cols), jnp.float32),
        ),
        compiler_params=pltpu.CompilerParams(vmem_limit_bytes=VMEM_BYTES),
        name="sketch",
    )(pieces, packed)


def first_sums_kernel(left_at, rows, packed, sums):
    x_cells, cols = rows.shape
    blocks = range(packed.shape[0])
    left = jnp.concatenate([packed[k, left_at : left_at + x_cells] for k in blocks], axis=0)
    sums[:x_cells] = rows[...]
    for c in range(cols // LANES):
        at = c * x_cells
        sums[x_cells:, c * LANES : (c + 1) * LANES] = lax.dot_general(
            left,
            jnp.concatenate([packed[k, at : at + x_cells] for k in blocks], axis=0),
            COL_COL,
            precision=HIGHEST,
            preferred_element_type=jnp.float32,
        )


def first_sums(left_at, rows, packed):
    return pl.pallas_call(
        functools.partial(first_sums_kernel, left_at),
        out_shape=jax.ShapeDtypeStruct(
            (rows.shape[0] + packed.shape[2], rows.shape[1]), jnp.float32
        ),
        compiler_params=pltpu.CompilerParams(vmem_limit_bytes=VMEM_BYTES),
        name="first_sums",
    )(rows, packed)


def first_kernel(*refs):
    *sums, core_first = refs
    x_cells = core_first.shape[0]
    total = sums[0][...]
    for other in sums[1:]:
        total = total + other[...]
    system = total[x_cells:]
    inverse = spd_inverse(system)
    scores = lax.dot_general(
        total[:x_cells], system, ROW_ROW, precision=HIGHEST, preferred_element_type=jnp.float32
    )
    core_first[...] = jnp.dot(
        scores, inverse, precision=HIGHEST, preferred_element_type=jnp.float32
    )


def solve_first(x_cells, *sums):
    return pl.pallas_call(
        first_kernel,
        out_shape=jax.ShapeDtypeStruct((x_cells, sums[0].shape[0] - x_cells), jnp.float32),
        compiler_params=pltpu.CompilerParams(vmem_limit_bytes=VMEM_BYTES),
        name="solve_first",
    )(*sums)


def place_kernel(own, inner_order, *refs):
    *parts, core_last = refs
    inner = lax.axis_index("gy")
    for part, i in zip(parts, inner_order):
        for o in range(part.shape[0]):
            at = pl.multiple_of((o * len(parts) + (inner ^ i)) * own, own)
            for c in range(part.shape[1] // own):
                core_last[pl.ds(at, own), c * LANES : (c + 1) * LANES] = part[
                    o, c * own : (c + 1) * own
                ]


def place(own, inner_order, parts):
    outer, rows, lanes = parts[0].shape
    return pl.pallas_call(
        functools.partial(place_kernel, own, inner_order),
        out_shape=jax.ShapeDtypeStruct(
            (len(parts) * outer * own, rows // own * lanes), jnp.float32
        ),
        compiler_params=pltpu.CompilerParams(vmem_limit_bytes=VMEM_BYTES),
        name="place",
    )(*parts)


def per_device(flow_field, left_x, last_x, last_y, right_y, right_m, last_m):
    x_cells, y_cells, m_cells = flow_field.shape
    rank = left_x.shape[1]
    cols = right_m.shape[1]
    blocks, shares = lax.axis_size("gx"), lax.axis_size("gz")
    y_share = y_cells // shares
    y_own = y_share // blocks

    last_part, first_part, *terms = local_products(
        shares, flow_field, last_x, last_y, right_y, right_m, last_m
    )

    terms = [swap(term, "gz", 1 + at // PARTS) for at, term in enumerate(terms)]
    here = lax.axis_index("gz")
    kept = flow_field.reshape(x_cells, shares, y_share, m_cells)
    kept = lax.dynamic_index_in_dim(kept, here, 1, False).reshape(-1, m_cells)
    kept = jnp.dot(kept, last_m, preferred_element_type=jnp.float32)
    kept = kept.reshape(x_cells, y_share, cols)

    order = swap_order("gx")
    packed = jnp.concatenate(
        [
            first_part.reshape(x_cells, -1, LANES).transpose(1, 0, 2).reshape(-1, LANES),
            left_x.astype(jnp.float32),
        ],
        axis=0,
    )[None]
    left_at = x_cells * cols // LANES
    first_bit, *bits = gather_bits("gx")
    packed = swap_step(packed, "gx", first_bit)

    group = ("gx", "gy")
    own = rank // lax.axis_size(group)
    last_rows = lax.all_to_all(last_part.reshape(-1, own, m_cells), group, 0, 0, tiled=True)
    last_rows = jnp.sum(after(last_rows, *terms[::PARTS]), axis=0)
    both = jnp.dot(
        jnp.concatenate(split_terms(last_rows), axis=0), last_m, preferred_element_type=jnp.float32
    )
    both = after(both[:own] + both[own:], packed, kept)
    count = lax.axis_size(ALL)
    copies = jnp.broadcast_to(both[None], (count, own, cols))
    system = lax.all_to_all(copies, ALL, 0, 0, tiled=True).reshape(-1, shares, own, cols)
    if own % ROWS:
        system = jnp.sum(system, axis=1).reshape(-1, 1, ROWS, cols)

    for bit in bits:
        packed = swap_step(packed, "gx", bit)
    sums = first_sums(left_at, first_part, packed)
    if own % ROWS:
        extra = jnp.zeros((ROWS, LANES), jnp.float32)
    else:
        extra = last_rows.reshape(own, -1, LANES).transpose(1, 0, 2).reshape(-1, LANES)
    projected = solve_last(blocks, after(system, packed), extra, kept, terms)
    sums = swap_sum(sums, "gz")
    sums = [swap(sums, "gy", y) if y else sums for y in range(lax.axis_size("gy"))]

    pieces = lax.all_to_all(projected, "gx", 0, 0, tiled=True)
    core_first = solve_first(x_cells, after(sums[0], projected), *sums[1:])
    group = ("gx", "gz")
    devices = lax.axis_size(group)
    rank_own = rank // devices
    if rank_own % ROWS:
        middle, extra = sketch(order, left_at, y_own, rank, pieces, packed)
        middle = middle.reshape(y_own, devices, rank_own, rank).transpose(1, 0, 2, 3)
    else:
        middle, extra = sketch(order, left_at, y_own, rank_own, pieces, packed)
    middle, core_first = lax.optimization_barrier((middle, core_first))
    received = lax.all_to_all(middle, group, 0, 0, tiled=True)
    received = received.reshape(blocks, shares, y_own, rank_own, rank)
    core_middle = received.transpose(3, 1, 0, 2, 4).reshape(rank_own, y_cells, rank)

    if own % ROWS:
        core_last = gather_rows(last_rows, "gx", "gy")
    else:
        inner = range(lax.axis_size("gy"))
        core_last = place(own, inner, [swap(extra, "gy", i) if i else extra for i in inner])
    return (core_first, core_middle, core_last)


def solution(mesh):
    return jax.shard_map(
        per_device,
        mesh=mesh,
        in_specs=(
            P("gx", "gy", "gz"),
            P("gx", None),
            P("gx", None),
            P("gy", None),
            P("gy", None),
            P("gz", None),
            P("gz", None),
        ),
        out_specs=(P("gx", None), P(("gx", "gz"), "gy", None), P(None, "gz")),
        check_vma=False,
    )
```

```python
import functools

import jax
import jax.numpy as jnp
from jax import lax
from jax.experimental import pallas as pl
from jax.experimental.pallas import tpu as pltpu
from jax.sharding import PartitionSpec as P

ALL = ("gx", "gy", "gz")
HIGHEST = lax.Precision.HIGHEST
VMEM_BYTES = 48 * 1024 * 1024
LOCAL_VMEM_BYTES = 63 * 1024 * 1024
ROWS = 8
LANES = 128
PARTS = 2
ROW_ROW = (((1,), (1,)), ((), ()))
COL_COL = (((0,), (0,)), ((), ()))


def gather_bits(axis):
    *bits, low, last = axis_bits(axis)
    return [low, *bits, last]


def axis_bits(axis):
    bit = lax.axis_size(axis) // 2
    while bit:
        yield bit
        bit //= 2


def swap(array, axis, bits):
    return lax.ppermute(array, axis, [(s, s ^ bits) for s in range(lax.axis_size(axis))])


def swap_sum(array, axis):
    for bit in axis_bits(axis):
        array = array + swap(array, axis, bit)
    return array


def after(value, *others):
    value, *_ = lax.optimization_barrier((value, *others))
    return value


def swap_order(axis):
    order = [0]
    for bit in gather_bits(axis):
        order += [o ^ bit for o in order]
    return order


def swap_step(held, axis, bit):
    return jnp.concatenate([held, swap(held, axis, bit)], axis=0)


def gather_rows(array, outer, inner):
    held = array[None, None]
    for dim, axis in ((0, outer), (1, inner)):
        shape = held.shape
        held = held.reshape(*shape[:dim], 1, 1, *shape[dim + 1 :])
        for bit in axis_bits(axis):
            other = swap(held, axis, bit)
            upper = (lax.axis_index(axis) & bit) != 0
            low = jnp.where(upper, other, held)
            high = jnp.where(upper, held, other)
            held = jnp.concatenate([low, high], axis=dim + 1)
            shape = held.shape
            held = held.reshape(*shape[:dim], shape[dim] * shape[dim + 1], 1, *shape[dim + 2 :])
        shape = held.shape
        held = held.reshape(*shape[: dim + 1], *shape[dim + 2 :])
    return held.reshape(-1, array.shape[-1])


def split_terms(array):
    high = lax.reduce_precision(array, 8, 7)
    return high.astype(jnp.bfloat16), (array - high).astype(jnp.bfloat16)


def invert(system):
    size = system.shape[0]
    lanes = lax.broadcasted_iota(jnp.int32, (ROWS, size), 1)
    subs = lax.broadcasted_iota(jnp.int32, (ROWS, size), 0)
    rows = [system[r : r + ROWS] for r in range(0, size, ROWS)]

    def column(block, at):
        return jnp.broadcast_to(block[:, at : at + 1], (ROWS, size))

    for panel in range(size // ROWS):
        first = panel * ROWS
        inside = (lanes >= first) & (lanes < first + ROWS)
        unit = (lanes - first == subs).astype(jnp.float32)
        work = [column(rows[panel], first + c) for c in range(ROWS)]
        work.append(jnp.where(inside, unit, rows[panel]))
        for k in range(0, ROWS, 2):
            p, q = work[k], work[k + 1]
            a, b, d = p[k : k + 1], q[k : k + 1], q[k + 1 : k + 2]
            scale = 1.0 / (a * d - b * b)
            a, b, d = a * scale, b * scale, d * scale
            for c in range(k + 2, ROWS + 1):
                upper, lower = work[c][k : k + 1], work[c][k + 1 : k + 2]
                top = d * upper - b * lower
                low = a * lower - b * upper
                rest = work[c] - p * top - q * low
                work[c] = jnp.where(subs == k, top, jnp.where(subs == k + 1, low, rest))
        solved = work[ROWS]
        for r in range(len(rows)):
            if r == panel:
                continue
            old = rows[r]
            new = jnp.where(inside, 0.0, old)
            for c in range(ROWS):
                new = new - column(old, first + c) * solved[c : c + 1]
            rows[r] = new
        rows[panel] = solved
    return jnp.concatenate(rows, axis=0)


def spd_inverse(system):
    square = lax.dot_general(
        system, system, ROW_ROW, precision=HIGHEST, preferred_element_type=jnp.float32
    )
    return invert(square)


def local_kernel(
    chunks,
    shares,
    field_hbm,
    last_x_hbm,
    last_y_hbm,
    right_y_hbm,
    right_m_hbm,
    last_m_hbm,
    last_part,
    first_part,
    *refs,
):
    count = (shares - 1) * PARTS
    terms_hbm = refs[:count]
    field, last_x, last_y, right_y, right_m, last_m, terms, sems, out_sems = refs[count:]
    x_cells, y_cells, m_cells = field.shape
    step = x_cells // chunks
    y_share = y_cells // shares
    parts = [pl.ds(n * step, step) for n in range(chunks)]
    copies = [
        pltpu.make_async_copy(last_m_hbm, last_m, sems.at[0]),
        pltpu.make_async_copy(field_hbm.at[parts[0]], field.at[parts[0]], sems.at[1]),
        pltpu.make_async_copy(last_x_hbm, last_x, sems.at[2]),
        pltpu.make_async_copy(last_y_hbm, last_y, sems.at[3]),
        pltpu.make_async_copy(right_m_hbm, right_m, sems.at[4]),
        pltpu.make_async_copy(right_y_hbm, right_y, sems.at[5]),
    ]
    for n in range(1, chunks):
        copies.append(
            pltpu.make_async_copy(field_hbm.at[parts[n]], field.at[parts[n]], sems.at[5 + n])
        )
    for copy in copies:
        copy.start()
    here = lax.axis_index("gz")
    leaving = []
    copies[0].wait()
    for n in range(chunks):
        copies[5 + n if n else 1].wait()
        for s in range(1, shares):
            start = pl.multiple_of((here ^ s) * y_share, y_share)
            rows = field[parts[n], pl.ds(start, y_share), :].reshape(step * y_share, m_cells)
            term = jnp.dot(rows, last_m[...], preferred_element_type=jnp.float32)
            terms[s - 1, parts[n]] = term.reshape(step, y_share, -1)
            part, at = divmod(n * step, x_cells // PARTS)
            leaving.append(
                pltpu.make_async_copy(
                    terms.at[s - 1, parts[n]],
                    terms_hbm[(s - 1) * PARTS + part].at[pl.ds(at, step)],
                    out_sems.at[s - 1, n],
                )
            )
            leaving[-1].start()

    for copy in copies[2:6]:
        copy.wait()
    for n in range(chunks):
        rows = field[parts[n]].reshape(step * y_cells, m_cells)
        left = last_x[parts[n]].astype(jnp.float32)[:, None, :]
        khatri = left * last_y[...].astype(jnp.float32)[None]
        khatri = khatri.astype(jnp.bfloat16).reshape(step * y_cells, -1)
        part = lax.dot_general(khatri, rows, COL_COL, preferred_element_type=jnp.float32)
        if n == 0:
            last_part[...] = part
        else:
            last_part[...] += part
        first = jnp.dot(rows, right_m[...], preferred_element_type=jnp.float32)
        first = first.reshape(step, y_cells, -1) * right_y[...].astype(jnp.float32)[None]
        first_part[parts[n], :] = jnp.sum(first, axis=1)
    for copy in leaving:
        copy.wait()


def local_products(shares, field, last_x, last_y, right_y, right_m, last_m):
    x_cells, y_cells, m_cells = field.shape
    rank, cols = last_x.shape[1], last_m.shape[1]
    chunks = max(x_cells // 8, 1)
    inputs = (field, last_x, last_y, right_y, right_m, last_m)
    dims = (x_cells, y_cells // shares, cols)
    part_dims = (x_cells // PARTS, *dims[1:])
    hbm = pl.BlockSpec(memory_space=pltpu.HBM)
    vmem = pl.BlockSpec(memory_space=pltpu.VMEM)
    return pl.pallas_call(
        functools.partial(local_kernel, chunks, shares),
        in_specs=[hbm] * len(inputs),
        out_specs=[vmem, vmem, *([hbm] * ((shares - 1) * PARTS))],
        out_shape=[
            jax.ShapeDtypeStruct((rank, m_cells), jnp.float32),
            jax.ShapeDtypeStruct((x_cells, cols), jnp.float32),
            *([jax.ShapeDtypeStruct(part_dims, jnp.float32)] * ((shares - 1) * PARTS)),
        ],
        scratch_shapes=[
            *(pltpu.VMEM(x.shape, x.dtype) for x in inputs),
            pltpu.VMEM((shares - 1, *dims), jnp.float32),
            pltpu.SemaphoreType.DMA((5 + chunks,)),
            pltpu.SemaphoreType.DMA((shares - 1, chunks)),
        ],
        compiler_params=pltpu.CompilerParams(vmem_limit_bytes=LOCAL_VMEM_BYTES),
        name="local_products",
    )(*inputs)


def two_terms(array):
    high = array.astype(jnp.bfloat16)
    return high, (array - high.astype(jnp.float32)).astype(jnp.bfloat16)


def last_kernel(y_own, system_shares, kept, *refs):
    *terms, projected, flat = refs
    x_cells, y_cells, cols = kept.shape
    x_part = x_cells // PARTS
    totals = []
    for part in range(PARTS):
        total = kept[part * x_part : (part + 1) * x_part]
        for term in terms[part::PARTS]:
            total = total + term[...]
        totals.append(two_terms(total.reshape(x_part * y_cells, cols)))

    system = system_shares[:, 0]
    for k in range(1, system_shares.shape[1]):
        system = system + system_shares[:, k]
    system = system.reshape(-1, cols)
    rank = system.shape[0]
    system_high, system_low = two_terms(system)
    high, low = two_terms(spd_inverse(system))
    both = jnp.dot(
        high,
        jnp.concatenate([system_high, system_low], axis=1),
        preferred_element_type=jnp.float32,
    )
    rest = jnp.dot(low, system_high, preferred_element_type=jnp.float32)
    pinv_high, pinv_low = two_terms(both[:, :cols] + (both[:, cols:] + rest))
    pinv_both = jnp.concatenate([pinv_high, pinv_low], axis=0)

    rows = flat.shape[0] // PARTS
    for part, (high, low) in enumerate(totals):
        both = lax.dot_general(high, pinv_both, ROW_ROW, preferred_element_type=jnp.float32)
        rest = lax.dot_general(low, pinv_high, ROW_ROW, preferred_element_type=jnp.float32)
        flat[part * rows : (part + 1) * rows] = both[:, :rank] + (both[:, rank:] + rest)
    for b in range(projected.shape[0]):
        for j in range(y_own):
            projected[b, j * x_cells : (j + 1) * x_cells] = flat[
                pl.ds(b * y_own + j, x_cells, stride=y_cells), :
            ]


def solve_last(blocks, system_shares, kept, terms):
    rank = system_shares.shape[0] * system_shares.shape[2]
    x_cells, y_cells, _ = kept.shape
    y_own = y_cells // blocks
    rows = y_own * x_cells
    return pl.pallas_call(
        functools.partial(last_kernel, y_own),
        out_shape=jax.ShapeDtypeStruct((blocks, rows, rank), jnp.float32),
        scratch_shapes=[pltpu.VMEM((x_cells * y_cells, rank), jnp.float32)],
        cost_estimate=pl.CostEstimate(flops=6 * 10**9, bytes_accessed=0, transcendentals=0),
        compiler_params=pltpu.CompilerParams(vmem_limit_bytes=VMEM_BYTES),
        name="solve_last",
    )(system_shares, kept, *terms)


def packed_units(parts, unit):
    return [(part, n * unit) for part in parts for n in range(part.shape[0] // unit)]


def sketch_kernel(order, left_at, unit, pieces, mine, other, out):
    me = lax.axis_index("gx")
    _, rows, cols = pieces.shape
    x_cells = unit - left_at
    weights = jnp.concatenate(
        [part[at + left_at : at + unit] for part, at in packed_units((mine, other), unit)], axis=0
    )
    weights = weights.astype(jnp.bfloat16)
    columns = []
    for j in range(rows // x_cells):
        columns += two_terms(
            jnp.concatenate(
                [pieces[me ^ o, j * x_cells : (j + 1) * x_cells] for o in order], axis=0
            )
        )
    sums = lax.dot_general(
        weights,
        jnp.concatenate(columns, axis=1),
        COL_COL,
        preferred_element_type=jnp.float32,
    )
    for j in range(rows // x_cells):
        at = 2 * j * cols
        core = sums[:, at : at + cols] + sums[:, at + cols : at + 2 * cols]
        out[:, j] = core.reshape(out.shape[0], out.shape[2], cols)


def sketch(order, left_at, unit, own, pieces, mine, other):
    _, rows, cols = pieces.shape
    rank = mine.shape[1]
    y_own = rows // (unit - left_at)
    return pl.pallas_call(
        functools.partial(sketch_kernel, order, left_at, unit),
        out_shape=jax.ShapeDtypeStruct((rank // own, y_own, own, cols), jnp.float32),
        compiler_params=pltpu.CompilerParams(vmem_limit_bytes=VMEM_BYTES),
        name="sketch",
    )(pieces, mine, other)


def first_sums_kernel(left_at, unit, rows, mine, other, sums, extra):
    x_cells, cols = rows.shape
    units = packed_units((mine, other), unit)
    left = jnp.concatenate([part[at + left_at : at + unit] for part, at in units], axis=0)
    sums[:x_cells] = rows[...]
    for c in range(cols // LANES):
        first = c * x_cells
        sums[x_cells:, c * LANES : (c + 1) * LANES] = lax.dot_general(
            left,
            jnp.concatenate(
                [part[at + first : at + first + x_cells] for part, at in units], axis=0
            ),
            COL_COL,
            precision=HIGHEST,
            preferred_element_type=jnp.float32,
        )
    extra[0] = mine[len(units) // 2 * unit :]
    extra[1] = other[len(units) // 2 * unit :]


def first_sums(left_at, unit, rows, mine, other):
    height, rank = mine.shape
    return pl.pallas_call(
        functools.partial(first_sums_kernel, left_at, unit),
        out_shape=(
            jax.ShapeDtypeStruct((rows.shape[0] + rank, rows.shape[1]), jnp.float32),
            jax.ShapeDtypeStruct((2, height % unit, rank), jnp.float32),
        ),
        compiler_params=pltpu.CompilerParams(vmem_limit_bytes=VMEM_BYTES),
        name="first_sums",
    )(rows, mine, other)


def first_kernel(*refs):
    *sums, core_first = refs
    x_cells = core_first.shape[0]
    total = sums[0][...]
    for other in sums[1:]:
        total = total + other[...]
    system = total[x_cells:]
    inverse = spd_inverse(system)
    scores = lax.dot_general(
        total[:x_cells], system, ROW_ROW, precision=HIGHEST, preferred_element_type=jnp.float32
    )
    core_first[...] = jnp.dot(
        scores, inverse, precision=HIGHEST, preferred_element_type=jnp.float32
    )


def solve_first(x_cells, *sums):
    return pl.pallas_call(
        first_kernel,
        out_shape=jax.ShapeDtypeStruct((x_cells, sums[0].shape[0] - x_cells), jnp.float32),
        compiler_params=pltpu.CompilerParams(vmem_limit_bytes=VMEM_BYTES),
        name="solve_first",
    )(*sums)


def place_kernel(own, outer_order, *refs):
    *parts, core_last = refs
    outer, inner = lax.axis_index("gx"), lax.axis_index("gy")
    for i, part in enumerate(parts):
        for k, o in enumerate(outer_order):
            at = ((outer ^ o) * len(parts) + (inner ^ i)) * own
            at = pl.multiple_of(at, own)
            for c in range(part.shape[1] // own):
                core_last[pl.ds(at, own), c * LANES : (c + 1) * LANES] = part[
                    k, c * own : (c + 1) * own
                ]


def place(own, outer_order, parts):
    outer, rows, lanes = parts[0].shape
    return pl.pallas_call(
        functools.partial(place_kernel, own, outer_order),
        out_shape=jax.ShapeDtypeStruct(
            (len(parts) * outer * own, rows // own * lanes), jnp.float32
        ),
        compiler_params=pltpu.CompilerParams(vmem_limit_bytes=VMEM_BYTES),
        name="place",
    )(*parts)


def per_device(flow_field, left_x, last_x, last_y, right_y, right_m, last_m):
    x_cells, y_cells, m_cells = flow_field.shape
    rank = left_x.shape[1]
    cols = right_m.shape[1]
    blocks, shares = lax.axis_size("gx"), lax.axis_size("gz")
    y_share = y_cells // shares
    y_own = y_share // blocks

    last_part, first_part, *terms = local_products(
        shares, flow_field, last_x, last_y, right_y, right_m, last_m
    )

    terms = [swap(term, "gz", 1 + at // PARTS) for at, term in enumerate(terms)]
    here = lax.axis_index("gz")
    kept = flow_field.reshape(x_cells, shares, y_share, m_cells)
    kept = lax.dynamic_index_in_dim(kept, here, 1, False).reshape(-1, m_cells)
    kept = jnp.dot(kept, last_m, preferred_element_type=jnp.float32)
    kept = kept.reshape(x_cells, y_share, cols)

    order = swap_order("gx")
    packed = jnp.concatenate(
        [
            first_part.reshape(x_cells, -1, LANES).transpose(1, 0, 2).reshape(-1, LANES),
            left_x.astype(jnp.float32),
        ],
        axis=0,
    )[None]
    left_at = x_cells * cols // LANES
    unit = left_at + x_cells
    first_bit, *bits = gather_bits("gx")
    packed = after(swap_step(packed, "gx", first_bit), *terms[::PARTS])

    group = ("gx", "gy")
    own = rank // lax.axis_size(group)
    last_rows = lax.all_to_all(last_part.reshape(-1, own, m_cells), group, 0, 0, tiled=True)
    last_rows = jnp.sum(after(last_rows, *terms[::PARTS]), axis=0)
    both = jnp.dot(
        jnp.concatenate(split_terms(last_rows), axis=0), last_m, preferred_element_type=jnp.float32
    )
    both = after(both[:own] + both[own:], packed, kept)
    count = lax.axis_size(ALL)
    copies = jnp.broadcast_to(both[None], (count, own, cols))
    system = lax.all_to_all(copies, ALL, 0, 0, tiled=True).reshape(-1, shares, own, cols)
    if own % ROWS:
        system = jnp.sum(system, axis=1).reshape(-1, 1, ROWS, cols)

    if own % ROWS:
        extra = jnp.zeros((ROWS, LANES), jnp.float32)
    else:
        extra = last_rows.reshape(own, -1, LANES).transpose(1, 0, 2).reshape(-1, LANES)
    *bits, last_bit = bits
    for bit in bits:
        packed = swap_step(packed, "gx", bit)
    mine = jnp.concatenate([packed.reshape(-1, LANES), extra], axis=0)
    other = swap(mine, "gx", last_bit)
    projected = solve_last(blocks, after(system, other), kept, terms)
    sums, extra = first_sums(left_at, unit, first_part, mine, other)
    sums = swap_sum(sums, "gz")
    sums = [swap(sums, "gy", y) if y else sums for y in range(lax.axis_size("gy"))]

    pieces = lax.all_to_all(projected, "gx", 0, 0, tiled=True)
    group = ("gx", "gz")
    devices = lax.axis_size(group)
    rank_own = rank // devices
    if rank_own % ROWS:
        middle = sketch(order, left_at, unit, rank, pieces, mine, other)
        middle = middle.reshape(y_own, devices, rank_own, rank).transpose(1, 0, 2, 3)
    else:
        middle = sketch(order, left_at, unit, rank_own, pieces, mine, other)
    outer = [0, last_bit]
    for bit in (*bits, first_bit):
        extra = swap_step(extra, "gx", bit)
        outer += [o ^ bit for o in outer]
    middle = after(middle, extra, *sums)
    received = lax.all_to_all(middle, group, 0, 0, tiled=True)
    received = received.reshape(blocks, shares, y_own, rank_own, rank)
    core_middle = received.transpose(3, 1, 0, 2, 4).reshape(rank_own, y_cells, rank)

    if own % ROWS:
        core_last = gather_rows(last_rows, "gx", "gy")
    else:
        inner = range(lax.axis_size("gy"))
        core_last = place(own, outer, [swap(extra, "gy", i) if i else extra for i in inner])
    core_first = solve_first(x_cells, after(sums[0], middle), *sums[1:])
    return (core_first, core_middle, core_last)


def solution(mesh):
    return jax.shard_map(
        per_device,
        mesh=mesh,
        in_specs=(
            P("gx", "gy", "gz"),
            P("gx", None),
            P("gx", None),
            P("gy", None),
            P("gy", None),
            P("gz", None),
            P("gz", None),
        ),
        out_specs=(P("gx", None), P(("gx", "gz"), "gy", None), P(None, "gz")),
        check_vma=False,
    )
```

```python
import functools

import jax
import jax.numpy as jnp
from jax import lax
from jax.experimental import pallas as pl
from jax.experimental.pallas import tpu as pltpu
from jax.sharding import PartitionSpec as P

ALL = ("gx", "gy", "gz")
HIGHEST = lax.Precision.HIGHEST
VMEM_BYTES = 48 * 1024 * 1024
LOCAL_VMEM_BYTES = 63 * 1024 * 1024
ROWS = 8
LANES = 128
PARTS = 2
ROW_ROW = (((1,), (1,)), ((), ()))
COL_COL = (((0,), (0,)), ((), ()))


def gather_bits(axis):
    *bits, low, last = axis_bits(axis)
    return [low, *bits, last]


def axis_bits(axis):
    bit = lax.axis_size(axis) // 2
    while bit:
        yield bit
        bit //= 2


def swap(array, axis, bits):
    return lax.ppermute(array, axis, [(s, s ^ bits) for s in range(lax.axis_size(axis))])


def swap_sum(array, axis):
    for bit in axis_bits(axis):
        array = array + swap(array, axis, bit)
    return array


def after(value, *others):
    value, *_ = lax.optimization_barrier((value, *others))
    return value


def swap_order(axis):
    order = [0]
    for bit in gather_bits(axis):
        order += [o ^ bit for o in order]
    return order


def swap_step(held, axis, bit):
    return jnp.concatenate([held, swap(held, axis, bit)], axis=0)


def gather_rows(array, outer, inner):
    held = array[None, None]
    for dim, axis in ((0, outer), (1, inner)):
        shape = held.shape
        held = held.reshape(*shape[:dim], 1, 1, *shape[dim + 1 :])
        for bit in axis_bits(axis):
            other = swap(held, axis, bit)
            upper = (lax.axis_index(axis) & bit) != 0
            low = jnp.where(upper, other, held)
            high = jnp.where(upper, held, other)
            held = jnp.concatenate([low, high], axis=dim + 1)
            shape = held.shape
            held = held.reshape(*shape[:dim], shape[dim] * shape[dim + 1], 1, *shape[dim + 2 :])
        shape = held.shape
        held = held.reshape(*shape[: dim + 1], *shape[dim + 2 :])
    return held.reshape(-1, array.shape[-1])


def split_terms(array):
    high = lax.reduce_precision(array, 8, 7)
    return high.astype(jnp.bfloat16), (array - high).astype(jnp.bfloat16)


def invert(system):
    size = system.shape[0]
    lanes = lax.broadcasted_iota(jnp.int32, (ROWS, size), 1)
    subs = lax.broadcasted_iota(jnp.int32, (ROWS, size), 0)
    rows = [system[r : r + ROWS] for r in range(0, size, ROWS)]

    def column(block, at):
        return jnp.broadcast_to(block[:, at : at + 1], (ROWS, size))

    for panel in range(size // ROWS):
        first = panel * ROWS
        inside = (lanes >= first) & (lanes < first + ROWS)
        unit = (lanes - first == subs).astype(jnp.float32)
        work = [column(rows[panel], first + c) for c in range(ROWS)]
        work.append(jnp.where(inside, unit, rows[panel]))
        for k in range(0, ROWS, 2):
            p, q = work[k], work[k + 1]
            a, b, d = p[k : k + 1], q[k : k + 1], q[k + 1 : k + 2]
            scale = 1.0 / (a * d - b * b)
            a, b, d = a * scale, b * scale, d * scale
            for c in range(k + 2, ROWS + 1):
                upper, lower = work[c][k : k + 1], work[c][k + 1 : k + 2]
                top = d * upper - b * lower
                low = a * lower - b * upper
                rest = work[c] - p * top - q * low
                work[c] = jnp.where(subs == k, top, jnp.where(subs == k + 1, low, rest))
        solved = work[ROWS]
        for r in range(len(rows)):
            if r == panel:
                continue
            old = rows[r]
            new = jnp.where(inside, 0.0, old)
            for c in range(ROWS):
                new = new - column(old, first + c) * solved[c : c + 1]
            rows[r] = new
        rows[panel] = solved
    return jnp.concatenate(rows, axis=0)


def spd_inverse(system):
    square = lax.dot_general(
        system, system, ROW_ROW, precision=HIGHEST, preferred_element_type=jnp.float32
    )
    return invert(square)


def local_kernel(
    chunks,
    shares,
    field_hbm,
    last_x_hbm,
    last_y_hbm,
    right_y_hbm,
    right_m_hbm,
    last_m_hbm,
    last_part,
    first_part,
    *refs,
):
    count = (shares - 1) * PARTS
    terms_hbm = refs[:count]
    field, last_x, last_y, right_y, right_m, last_m, terms, sems, out_sems = refs[count:]
    x_cells, y_cells, m_cells = field.shape
    step = x_cells // chunks
    y_share = y_cells // shares
    parts = [pl.ds(n * step, step) for n in range(chunks)]
    copies = [
        pltpu.make_async_copy(last_m_hbm, last_m, sems.at[0]),
        pltpu.make_async_copy(field_hbm.at[parts[0]], field.at[parts[0]], sems.at[1]),
        pltpu.make_async_copy(last_x_hbm, last_x, sems.at[2]),
        pltpu.make_async_copy(last_y_hbm, last_y, sems.at[3]),
        pltpu.make_async_copy(right_m_hbm, right_m, sems.at[4]),
        pltpu.make_async_copy(right_y_hbm, right_y, sems.at[5]),
    ]
    for n in range(1, chunks):
        copies.append(
            pltpu.make_async_copy(field_hbm.at[parts[n]], field.at[parts[n]], sems.at[5 + n])
        )
    for copy in copies:
        copy.start()
    here = lax.axis_index("gz")
    leaving = []
    copies[0].wait()
    for n in range(chunks):
        copies[5 + n if n else 1].wait()
        for s in range(1, shares):
            start = pl.multiple_of((here ^ s) * y_share, y_share)
            rows = field[parts[n], pl.ds(start, y_share), :].reshape(step * y_share, m_cells)
            term = jnp.dot(rows, last_m[...], preferred_element_type=jnp.float32)
            terms[s - 1, parts[n]] = term.reshape(step, y_share, -1)
            part, at = divmod(n * step, x_cells // PARTS)
            leaving.append(
                pltpu.make_async_copy(
                    terms.at[s - 1, parts[n]],
                    terms_hbm[(s - 1) * PARTS + part].at[pl.ds(at, step)],
                    out_sems.at[s - 1, n],
                )
            )
            leaving[-1].start()

    for copy in copies[2:6]:
        copy.wait()
    for n in range(chunks):
        rows = field[parts[n]].reshape(step * y_cells, m_cells)
        left = last_x[parts[n]].astype(jnp.float32)[:, None, :]
        khatri = left * last_y[...].astype(jnp.float32)[None]
        khatri = khatri.astype(jnp.bfloat16).reshape(step * y_cells, -1)
        part = lax.dot_general(khatri, rows, COL_COL, preferred_element_type=jnp.float32)
        if n == 0:
            last_part[...] = part
        else:
            last_part[...] += part
        first = jnp.dot(rows, right_m[...], preferred_element_type=jnp.float32)
        first = first.reshape(step, y_cells, -1) * right_y[...].astype(jnp.float32)[None]
        first_part[parts[n], :] = jnp.sum(first, axis=1)
    for copy in leaving:
        copy.wait()


def local_products(shares, field, last_x, last_y, right_y, right_m, last_m):
    x_cells, y_cells, m_cells = field.shape
    rank, cols = last_x.shape[1], last_m.shape[1]
    chunks = max(x_cells // 8, 1)
    inputs = (field, last_x, last_y, right_y, right_m, last_m)
    dims = (x_cells, y_cells // shares, cols)
    part_dims = (x_cells // PARTS, *dims[1:])
    hbm = pl.BlockSpec(memory_space=pltpu.HBM)
    vmem = pl.BlockSpec(memory_space=pltpu.VMEM)
    return pl.pallas_call(
        functools.partial(local_kernel, chunks, shares),
        in_specs=[hbm] * len(inputs),
        out_specs=[vmem, vmem, *([hbm] * ((shares - 1) * PARTS))],
        out_shape=[
            jax.ShapeDtypeStruct((rank, m_cells), jnp.float32),
            jax.ShapeDtypeStruct((x_cells, cols), jnp.float32),
            *([jax.ShapeDtypeStruct(part_dims, jnp.float32)] * ((shares - 1) * PARTS)),
        ],
        scratch_shapes=[
            *(pltpu.VMEM(x.shape, x.dtype) for x in inputs),
            pltpu.VMEM((shares - 1, *dims), jnp.float32),
            pltpu.SemaphoreType.DMA((5 + chunks,)),
            pltpu.SemaphoreType.DMA((shares - 1, chunks)),
        ],
        compiler_params=pltpu.CompilerParams(vmem_limit_bytes=LOCAL_VMEM_BYTES),
        name="local_products",
    )(*inputs)


def two_terms(array):
    high = array.astype(jnp.bfloat16)
    return high, (array - high.astype(jnp.float32)).astype(jnp.bfloat16)


def last_kernel(y_own, system_shares, extra, kept, *refs):
    *terms, projected, flat = refs
    x_cells, y_cells, cols = kept.shape
    x_part = x_cells // PARTS
    totals = []
    for part in range(PARTS):
        total = kept[part * x_part : (part + 1) * x_part]
        for term in terms[part::PARTS]:
            total = total + term[...]
        totals.append(two_terms(total.reshape(x_part * y_cells, cols)))

    system = system_shares[:, 0]
    for k in range(1, system_shares.shape[1]):
        system = system + system_shares[:, k]
    system = system.reshape(-1, cols)
    rank = system.shape[0]
    system_high, system_low = two_terms(system)
    high, low = two_terms(spd_inverse(system))
    both = jnp.dot(
        high,
        jnp.concatenate([system_high, system_low], axis=1),
        preferred_element_type=jnp.float32,
    )
    rest = jnp.dot(low, system_high, preferred_element_type=jnp.float32)
    pinv_high, pinv_low = two_terms(both[:, :cols] + (both[:, cols:] + rest))
    pinv_both = jnp.concatenate([pinv_high, pinv_low], axis=0)

    rows = flat.shape[0] // PARTS
    for part, (high, low) in enumerate(totals):
        both = lax.dot_general(high, pinv_both, ROW_ROW, preferred_element_type=jnp.float32)
        rest = lax.dot_general(low, pinv_high, ROW_ROW, preferred_element_type=jnp.float32)
        flat[part * rows : (part + 1) * rows] = both[:, :rank] + (both[:, rank:] + rest)
    for b in range(projected.shape[0]):
        for j in range(y_own):
            projected[b, j * x_cells : (j + 1) * x_cells] = flat[
                pl.ds(b * y_own + j, x_cells, stride=y_cells), :
            ]
        projected[b, y_own * x_cells :] = extra[...]


def solve_last(blocks, system_shares, extra, kept, terms):
    rank = system_shares.shape[0] * system_shares.shape[2]
    x_cells, y_cells, _ = kept.shape
    y_own = y_cells // blocks
    rows = y_own * x_cells + extra.shape[0]
    return pl.pallas_call(
        functools.partial(last_kernel, y_own),
        out_shape=jax.ShapeDtypeStruct((blocks, rows, rank), jnp.float32),
        scratch_shapes=[pltpu.VMEM((x_cells * y_cells, rank), jnp.float32)],
        cost_estimate=pl.CostEstimate(flops=6 * 10**9, bytes_accessed=0, transcendentals=0),
        compiler_params=pltpu.CompilerParams(vmem_limit_bytes=VMEM_BYTES),
        name="solve_last",
    )(system_shares, extra, kept, *terms)


def sketch_kernel(order, left_at, y_own, pieces, packed, out, extra):
    me = lax.axis_index("gx")
    blocks, _, cols = pieces.shape
    x_cells = packed.shape[1] - left_at
    weights = jnp.concatenate([packed[k, left_at:] for k in range(blocks)], axis=0)
    weights = weights.astype(jnp.bfloat16)
    columns = []
    for j in range(y_own):
        columns += two_terms(
            jnp.concatenate(
                [pieces[me ^ o, j * x_cells : (j + 1) * x_cells] for o in order], axis=0
            )
        )
    sums = lax.dot_general(
        weights,
        jnp.concatenate(columns, axis=1),
        COL_COL,
        preferred_element_type=jnp.float32,
    )
    for j in range(y_own):
        at = 2 * j * cols
        core = sums[:, at : at + cols] + sums[:, at + cols : at + 2 * cols]
        out[:, j] = core.reshape(out.shape[0], out.shape[2], cols)
    extra[...] = pieces[:, y_own * x_cells :]


def sketch(order, left_at, y_own, own, pieces, packed):
    blocks, rows, cols = pieces.shape
    rank = packed.shape[2]
    extra = rows - y_own * (packed.shape[1] - left_at)
    return pl.pallas_call(
        functools.partial(sketch_kernel, order, left_at, y_own),
        out_shape=(
            jax.ShapeDtypeStruct((rank // own, y_own, own, cols), jnp.float32),
            jax.ShapeDtypeStruct((blocks, extra, cols), jnp.float32),
        ),
        compiler_params=pltpu.CompilerParams(vmem_limit_bytes=VMEM_BYTES),
        name="sketch",
    )(pieces, packed)


def first_sums_kernel(left_at, rows, packed, sums):
    x_cells, cols = rows.shape
    blocks = range(packed.shape[0])
    left = jnp.concatenate([packed[k, left_at : left_at + x_cells] for k in blocks], axis=0)
    sums[:x_cells] = rows[...]
    for c in range(cols // LANES):
        at = c * x_cells
        sums[x_cells:, c * LANES : (c + 1) * LANES] = lax.dot_general(
            left,
            jnp.concatenate([packed[k, at : at + x_cells] for k in blocks], axis=0),
            COL_COL,
            precision=HIGHEST,
            preferred_element_type=jnp.float32,
        )


def first_sums(left_at, rows, packed):
    return pl.pallas_call(
        functools.partial(first_sums_kernel, left_at),
        out_shape=jax.ShapeDtypeStruct(
            (rows.shape[0] + packed.shape[2], rows.shape[1]), jnp.float32
        ),
        compiler_params=pltpu.CompilerParams(vmem_limit_bytes=VMEM_BYTES),
        name="first_sums",
    )(rows, packed)


def first_kernel(*refs):
    *sums, core_first = refs
    x_cells = core_first.shape[0]
    total = sums[0][...]
    for other in sums[1:]:
        total = total + other[...]
    system = total[x_cells:]
    inverse = spd_inverse(system)
    scores = lax.dot_general(
        total[:x_cells], system, ROW_ROW, precision=HIGHEST, preferred_element_type=jnp.float32
    )
    core_first[...] = jnp.dot(
        scores, inverse, precision=HIGHEST, preferred_element_type=jnp.float32
    )


def solve_first(x_cells, *sums):
    return pl.pallas_call(
        first_kernel,
        out_shape=jax.ShapeDtypeStruct((x_cells, sums[0].shape[0] - x_cells), jnp.float32),
        compiler_params=pltpu.CompilerParams(vmem_limit_bytes=VMEM_BYTES),
        name="solve_first",
    )(*sums)


def place_kernel(own, inner_order, *refs):
    *parts, core_last = refs
    inner = lax.axis_index("gy")
    for part, i in zip(parts, inner_order):
        for o in range(part.shape[0]):
            at = pl.multiple_of((o * len(parts) + (inner ^ i)) * own, own)
            for c in range(part.shape[1] // own):
                core_last[pl.ds(at, own), c * LANES : (c + 1) * LANES] = part[
                    o, c * own : (c + 1) * own
                ]


def place(own, inner_order, parts):
    outer, rows, lanes = parts[0].shape
    return pl.pallas_call(
        functools.partial(place_kernel, own, inner_order),
        out_shape=jax.ShapeDtypeStruct(
            (len(parts) * outer * own, rows // own * lanes), jnp.float32
        ),
        compiler_params=pltpu.CompilerParams(vmem_limit_bytes=VMEM_BYTES),
        name="place",
    )(*parts)


def per_device(flow_field, left_x, last_x, last_y, right_y, right_m, last_m):
    x_cells, y_cells, m_cells = flow_field.shape
    rank = left_x.shape[1]
    cols = right_m.shape[1]
    blocks, shares = lax.axis_size("gx"), lax.axis_size("gz")
    y_share = y_cells // shares
    y_own = y_share // blocks

    last_part, first_part, *terms = local_products(
        shares, flow_field, last_x, last_y, right_y, right_m, last_m
    )

    terms = [swap(term, "gz", 1 + at // PARTS) for at, term in enumerate(terms)]
    here = lax.axis_index("gz")
    kept = flow_field.reshape(x_cells, shares, y_share, m_cells)
    kept = lax.dynamic_index_in_dim(kept, here, 1, False).reshape(-1, m_cells)
    kept = jnp.dot(kept, last_m, preferred_element_type=jnp.float32)
    kept = kept.reshape(x_cells, y_share, cols)

    order = swap_order("gx")
    packed = jnp.concatenate(
        [
            first_part.reshape(x_cells, -1, LANES).transpose(1, 0, 2).reshape(-1, LANES),
            left_x.astype(jnp.float32),
        ],
        axis=0,
    )[None]
    left_at = x_cells * cols // LANES
    first_bit, *bits = gather_bits("gx")
    packed = swap_step(packed, "gx", first_bit)

    group = ("gx", "gy")
    own = rank // lax.axis_size(group)
    last_rows = lax.all_to_all(last_part.reshape(-1, own, m_cells), group, 0, 0, tiled=True)
    last_rows = jnp.sum(after(last_rows, *terms[::PARTS]), axis=0)
    both = jnp.dot(
        jnp.concatenate(split_terms(last_rows), axis=0), last_m, preferred_element_type=jnp.float32
    )
    both = after(both[:own] + both[own:], packed, kept)
    count = lax.axis_size(ALL)
    copies = jnp.broadcast_to(both[None], (count, own, cols))
    system = lax.all_to_all(copies, ALL, 0, 0, tiled=True).reshape(-1, shares, own, cols)
    if own % ROWS:
        system = jnp.sum(system, axis=1).reshape(-1, 1, ROWS, cols)

    for bit in bits:
        packed = swap_step(packed, "gx", bit)
    sums = first_sums(left_at, first_part, packed)
    if own % ROWS:
        extra = jnp.zeros((ROWS, LANES), jnp.float32)
    else:
        extra = last_rows.reshape(own, -1, LANES).transpose(1, 0, 2).reshape(-1, LANES)
    projected = solve_last(blocks, after(system, packed), extra, kept, terms)
    sums = swap_sum(sums, "gz")
    sums = [swap(sums, "gy", y) if y else sums for y in range(lax.axis_size("gy"))]

    pieces = lax.all_to_all(projected, "gx", 0, 0, tiled=True)
    core_first = solve_first(x_cells, after(sums[0], projected), *sums[1:])
    group = ("gx", "gz")
    devices = lax.axis_size(group)
    rank_own = rank // devices
    if rank_own % ROWS:
        middle, extra = sketch(order, left_at, y_own, rank, pieces, packed)
        middle = middle.reshape(y_own, devices, rank_own, rank).transpose(1, 0, 2, 3)
    else:
        middle, extra = sketch(order, left_at, y_own, rank_own, pieces, packed)
    middle, core_first = lax.optimization_barrier((middle, core_first))
    received = lax.all_to_all(middle, group, 0, 0, tiled=True)
    received = received.reshape(blocks, shares, y_own, rank_own, rank)
    core_middle = received.transpose(3, 1, 0, 2, 4).reshape(rank_own, y_cells, rank)

    if own % ROWS:
        core_last = gather_rows(last_rows, "gx", "gy")
    else:
        inner = range(lax.axis_size("gy"))
        core_last = place(own, inner, [swap(extra, "gy", i) if i else extra for i in inner])
    return (core_first, core_middle, core_last)


def solution(mesh):
    return jax.shard_map(
        per_device,
        mesh=mesh,
        in_specs=(
            P("gx", "gy", "gz"),
            P("gx", None),
            P("gx", None),
            P("gy", None),
            P("gy", None),
            P("gz", None),
            P("gz", None),
        ),
        out_specs=(P("gx", None), P(("gx", "gz"), "gy", None), P(None, "gz")),
        check_vma=False,
    )
```
